256 devices in a mesh: wide: 32 (over z, y), narrow: 8 (over x, core).
Axes of the slice: x: 4, y: 4, z: 8, core: 2. Of those that a mesh axis runs over, the one named last changes fastest.
Arguments:
- point_feats: bfloat16 [64, 524288], P(None, ('wide', 'narrow')), may hold values from -6 to 6
- point_pos: float32 [3, 524288], P(None, ('wide', 'narrow')), may hold values from 0 to 1
- point_weight: float32 [524288], P(('wide', 'narrow')), may hold values from 0.1 to 1
- nbr_point: int32 [32, 8, 32, 2, 128], P('wide', 'narrow'), may hold values from 0 to 2047
- nbr_cell: int32 [32, 8, 32, 2, 128], P('wide', 'narrow'), may hold values from 0 to 1023
- block_count: int32 [32, 8, 32], P('wide', 'narrow'), may hold values from 1 to 2, as said below
- latent: bfloat16 [64, 64, 4096], P('wide', None, 'narrow'), may hold values from -6 to 6
- preact: bfloat16 [64, 64, 4096], P('wide', None, 'narrow'), may hold values from -8 to 8
- cotangent: bfloat16 [64, 64, 4096], P('wide', None, 'narrow'), may hold values from -6 to 6
- spectral_weight: float32 [32, 32, 32, 64, 128], P('wide', None, 'narrow'), may hold values from -0.75 to 0.75
- kernel_mat: bfloat16 [64, 64], replicated, may hold values from -0.75 to 0.75
- first_weight: float32 [3, 64], replicated, may hold values from -12 to 12
- first_bias: float32 [64], replicated, may hold values from -6 to 6
- second_weight: bfloat16 [64, 64], replicated, may hold values from -0.75 to 0.75
- mix_weight: bfloat16 [64, 64], replicated, may hold values from -0.75 to 0.75
Outputs:
- d_points: float32 [64, 524288], P(None, ('wide', 'narrow'))
- d_kernel: float32 [64, 64], replicated
- d_first: float32 [3, 64], replicated
- d_first_bias: float32 [64], replicated
- d_second: float32 [64, 64], replicated
- d_mix: float32 [64, 64], replicated
- d_spectral: float32 [32, 32, 32, 64, 128], P('wide', None, 'narrow')
The draws below stay inside these ranges and needn't reach their ends.
Inputs may be any that keep to these rules, and one draw needn't show every extreme that they name: Of the 2 block slots that a sending device has for one index of wide, the first block_count of them are live and every row of a live block is an edge; later slots are padding. For every index of narrow, one index of wide receives 2 live blocks from every sending device of that index of narrow; every other count is at least 1.
All inputs are finite; a program needn't handle non-finite values.
Results may differ from the reference program's by a relative error of at most 0.0068.
Values may be sent and summed in bfloat16 or wider, within the bound.
No kernel may reach another device: no remote copies, remote signals or barrier semaphores. Data moves between devices by JAX's collectives and lax.ppermute only.
A program may use at most 128 MiB of HBM per device.

```python
import math
import jax
import jax.numpy as jnp
from jax import lax

C = 64
GZ = 64
MZ = 32
XPL = 2
YR = 8
BLK = 128
CAP = 2
P_DEV = 2048
GX = 64
GY = 64
MX = 32
MY = 32
P_SIZE = 524288
N_WIDE = 32
N_NARROW = 8
DEVICES = 256


def draw_block_count(key, part):
    key = jax.random.fold_in(key, 11)
    base_key, hot_key = jax.random.split(key)
    base_counts = jax.random.randint(base_key, (N_WIDE, N_NARROW, N_WIDE), 1, max(CAP // 2, 1) + 1)
    hot_target = jax.random.randint(hot_key, (N_NARROW,), 0, N_WIDE)
    full_mask = jnp.arange(N_WIDE)[None, None, :] == hot_target[None, :, None]
    return jnp.where(full_mask, CAP, base_counts).astype(jnp.int32)


def with_ends(drawn, stream_key, smallest, largest):
    place = [jax.random.randint(jax.random.fold_in(stream_key, axis), (), 0, length) for axis, length in enumerate(drawn.shape)]
    longest = drawn.shape.index(max(drawn.shape))
    beside = place[:longest] + [(place[longest] + 1) % drawn.shape[longest]] + place[longest + 1:]
    return drawn.at[tuple(place)].set(smallest).at[tuple(beside)].set(largest)


def shard_levels(own_key, shape, cuts, smallest, largest):
    loudness, own = 1.0, jax.random.fold_in(own_key, 6)
    for position, shards_of in cuts:
        draws = jnp.exp(jax.random.uniform(jax.random.fold_in(own, position), (shards_of,), jnp.float32, smallest / len(cuts), largest / len(cuts)))
        loudness = loudness * jnp.repeat(draws, shape[position] // shards_of).reshape([-1 if axis == position else 1 for axis in range(len(shape))])
    return loudness


def bell_draw(key, shape, deviation, limit, cuts=(), kind=jnp.bfloat16):
    gain = shard_levels(key, shape, cuts, -0.22, 0.18) if cuts else 1.0
    values = jax.random.normal(key, shape, jnp.float32) * deviation * gain
    return jnp.minimum(jnp.maximum(values, -limit), limit).astype(kind)


def setup_inputs(seed: int = 0) -> dict:
    streams_of = jax.random.split(jax.random.key(seed), 16)
    return {
        "point_feats": bell_draw(streams_of[0], (C, P_SIZE), 1.0, 6.0, ((1, 256),)),
        "point_pos": jnp.clip(1.0 * jax.random.uniform(streams_of[1], (3, P_SIZE), jnp.float32) ** shard_levels(streams_of[1], (3, P_SIZE), ((1, 256),), -0.2, 0.2), 0.0, 1.0),
        "point_weight": jnp.clip(jnp.exp(math.log(1.0) - 2.3025851 * jax.random.uniform(streams_of[2], (P_SIZE,), jnp.float32) ** shard_levels(streams_of[2], (P_SIZE,), ((0, 256),), -0.2, 0.2)), 0.1, 1.0),
        "nbr_point": with_ends(jax.random.randint(streams_of[3], (N_WIDE, N_NARROW, N_WIDE, CAP, BLK), 0, P_DEV), jax.random.fold_in(streams_of[3], 1), 0, P_DEV - 1).astype(jnp.int32),
        "nbr_cell": with_ends(jax.random.randint(streams_of[4], (N_WIDE, N_NARROW, N_WIDE, CAP, BLK), 0, XPL * YR * GZ), jax.random.fold_in(streams_of[4], 1), 0, (XPL * YR * GZ) - 1).astype(jnp.int32),
        "block_count": draw_block_count(jax.random.fold_in(streams_of[15], 71), 0),
        "latent": bell_draw(streams_of[6], (GX, C, GY * GZ), 1.0, 6.0, ((0, 32), (2, 8))),
        "preact": bell_draw(streams_of[7], (GX, C, GY * GZ), 1.5, 8.0, ((0, 32), (2, 8))),
        "cotangent": bell_draw(streams_of[8], (GX, C, GY * GZ), 1.0, 6.0, ((0, 32), (2, 8))),
        "spectral_weight": bell_draw(streams_of[9], (MY, MX, MZ, C, 2 * C), C ** -0.5, 0.75, ((0, 32), (2, 8)), jnp.float32),
        "kernel_mat": bell_draw(streams_of[10], (C, C), C ** -0.5, 0.75),
        "first_weight": bell_draw(streams_of[11], (3, C), 2.0, 12.0, (), jnp.float32),
        "first_bias": bell_draw(streams_of[12], (C,), 1.0, 6.0, (), jnp.float32),
        "second_weight": bell_draw(streams_of[13], (C, C), C ** -0.5, 0.75),
        "mix_weight": bell_draw(streams_of[14], (C, C), C ** -0.5, 0.75),
    }


root_half = 0.7071067811865476
inv_root_tau = 0.3989422804014327


def gelu_value(values):
    return 0.5 * values * (1.0 + jax.scipy.special.erf(values * root_half))


def gelu_slope(values):
    return 0.5 * (1.0 + jax.scipy.special.erf(values * root_half)) + values * jnp.exp(-0.5 * values * values) * inv_root_tau


def wave_table(freq_list, positions, length):
    phase_idx = jnp.mod(freq_list[:, None] * positions[None, :], length).astype(jnp.float32)
    angles = phase_idx * (2.0 * math.pi / length)
    return jnp.cos(angles), jnp.sin(angles)


def signed_modes(mode_count):
    indices = jnp.arange(mode_count, dtype=jnp.int32)
    return jnp.where(indices < mode_count // 2, indices, indices - mode_count)


def forward_modes(field_in):
    highest = lax.Precision.HIGHEST
    depth_cos, depth_sin = wave_table(jnp.arange(MZ, dtype=jnp.int32), jnp.arange(GZ, dtype=jnp.int32), GZ)
    row_cos, row_sin = wave_table(signed_modes(MY), jnp.arange(GY, dtype=jnp.int32), GY)
    plane_cos, plane_sin = wave_table(signed_modes(MX), jnp.arange(GX, dtype=jnp.int32), GX)
    cube_view = field_in.reshape(GX, C, GY, GZ)
    depth_real = jnp.einsum('xcyz,kz->xykc', cube_view, depth_cos, precision=highest)
    depth_imag = -jnp.einsum('xcyz,kz->xykc', cube_view, depth_sin, precision=highest)
    row_real = jnp.einsum('xykc,jy->xjkc', depth_real, row_cos, precision=highest) + jnp.einsum('xykc,jy->xjkc', depth_imag, row_sin, precision=highest)
    row_imag = jnp.einsum('xykc,jy->xjkc', depth_imag, row_cos, precision=highest) - jnp.einsum('xykc,jy->xjkc', depth_real, row_sin, precision=highest)
    plane_real = jnp.einsum('xjkc,ix->jikc', row_real, plane_cos, precision=highest) + jnp.einsum('xjkc,ix->jikc', row_imag, plane_sin, precision=highest)
    plane_imag = jnp.einsum('xjkc,ix->jikc', row_imag, plane_cos, precision=highest) - jnp.einsum('xjkc,ix->jikc', row_real, plane_sin, precision=highest)
    return plane_real, plane_imag


def edge_math(weighted, offsets, grads, first_weight, first_bias, second_weight, kernel_mat):
    highest = lax.Precision.HIGHEST
    offset_vals = offsets.astype(jnp.float32)
    before = jnp.einsum('ih,isbr->hsbr', first_weight, offset_vals, precision=highest) + first_bias[:, None, None, None]
    active = gelu_value(before).astype(jnp.bfloat16)
    second_f = second_weight.astype(jnp.float32)
    kernel_f = kernel_mat.astype(jnp.float32)
    kernel_val = jnp.einsum('ho,hsbr->osbr', second_f, active.astype(jnp.float32))
    lifted = jnp.einsum('co,csbr->osbr', kernel_f, weighted.astype(jnp.float32))
    grad_vals = grads.astype(jnp.float32)
    gated = (grad_vals * kernel_val).astype(jnp.bfloat16)
    d_kval = (grad_vals * lifted).astype(jnp.bfloat16)
    row_grads = jnp.einsum('co,osbr->csbr', kernel_f, gated.astype(jnp.float32))
    part_kernel = jnp.einsum('csbr,osbr->cob', weighted.astype(jnp.float32), gated.astype(jnp.float32))
    part_second = jnp.einsum('hsbr,osbr->hob', active.astype(jnp.float32), d_kval.astype(jnp.float32))
    d_active = jnp.einsum('ho,osbr->hsbr', second_f, d_kval.astype(jnp.float32))
    d_before = d_active * gelu_slope(before)
    part_first = jnp.einsum('isbr,hsbr->ihb', offset_vals, d_before, precision=highest)
    part_bias = jnp.sum(d_before, axis=(1, 3))[:, None, :]
    return row_grads, part_kernel, part_second, part_first, part_bias


def reference(point_feats, point_pos, point_weight, nbr_point, nbr_cell, block_count, latent, preact, cotangent, spectral_weight, kernel_mat, first_weight, first_bias, second_weight, mix_weight):
    highest = lax.Precision.HIGHEST
    slab_size = YR * GZ
    volume = GX * GY * GZ
    source_field = latent.astype(jnp.float32)
    grad_field = cotangent.astype(jnp.float32) * gelu_slope(preact.astype(jnp.float32))
    d_mix = jnp.einsum('xcp,xop->co', source_field, grad_field, precision=highest)
    u_real, u_imag = forward_modes(source_field)
    d_real, d_imag = forward_modes(grad_field)

    def per_mode(pieces):
        real_u, imag_u, real_d, imag_d, weight_slice = pieces
        grad_real = (real_u[..., :, None] * real_d[..., None, :] + imag_u[..., :, None] * imag_d[..., None, :]) / volume
        grad_imag = (real_u[..., :, None] * imag_d[..., None, :] - imag_u[..., :, None] * real_d[..., None, :]) / volume
        weight_real = weight_slice[..., :C]
        weight_imag = weight_slice[..., C:]
        back_real = jnp.einsum('ikco,iko->ikc', weight_real, real_d, precision=highest) + jnp.einsum('ikco,iko->ikc', weight_imag, imag_d, precision=highest)
        back_imag = jnp.einsum('ikco,iko->ikc', weight_real, imag_d, precision=highest) - jnp.einsum('ikco,iko->ikc', weight_imag, real_d, precision=highest)
        return jnp.concatenate([grad_real, grad_imag], axis=-1), back_real, back_imag

    d_spectral, back_real, back_imag = lax.map(per_mode, (u_real, u_imag, d_real, d_imag, spectral_weight))
    depth_cos, depth_sin = wave_table(jnp.arange(MZ, dtype=jnp.int32), jnp.arange(GZ, dtype=jnp.int32), GZ)
    row_cos, row_sin = wave_table(signed_modes(MY), jnp.arange(GY, dtype=jnp.int32), GY)
    plane_cos, plane_sin = wave_table(signed_modes(MX), jnp.arange(GX, dtype=jnp.int32), GX)
    plane_real = jnp.einsum('jikc,ix->xjkc', back_real, plane_cos, precision=highest) - jnp.einsum('jikc,ix->xjkc', back_imag, plane_sin, precision=highest)
    plane_imag = jnp.einsum('jikc,ix->xjkc', back_imag, plane_cos, precision=highest) + jnp.einsum('jikc,ix->xjkc', back_real, plane_sin, precision=highest)
    row_real = jnp.einsum('xjkc,jy->xykc', plane_real, row_cos, precision=highest) - jnp.einsum('xjkc,jy->xykc', plane_imag, row_sin, precision=highest)
    row_imag = jnp.einsum('xjkc,jy->xykc', plane_imag, row_cos, precision=highest) + jnp.einsum('xjkc,jy->xykc', plane_real, row_sin, precision=highest)
    spectral_part = (jnp.einsum('xykc,kz->xcyz', row_real, depth_cos, precision=highest) - jnp.einsum('xykc,kz->xcyz', row_imag, depth_sin, precision=highest)) / volume
    d_latent = jnp.einsum('co,xop->xcp', mix_weight.astype(jnp.float32), grad_field, precision=highest) + spectral_part.reshape(GX, C, GY * GZ)
    grad_latent = d_latent.astype(jnp.bfloat16)
    latent_rows = grad_latent.reshape(GX, C, N_NARROW, slab_size)

    feats_dev = point_feats.reshape(C, DEVICES, P_DEV).transpose(1, 0, 2)
    pos_dev = point_pos.reshape(3, DEVICES, P_DEV).transpose(1, 0, 2)
    weight_dev = point_weight.reshape(DEVICES, P_DEV)
    points_dev = nbr_point.reshape(DEVICES, N_WIDE, CAP, BLK)
    cells_dev = nbr_cell.reshape(DEVICES, N_WIDE, CAP, BLK)
    counts_dev = block_count.reshape(DEVICES, N_WIDE)
    narrow_ids = jnp.arange(DEVICES, dtype=jnp.int32) % N_NARROW

    def one_device(pieces):
        gathered_src, positions, weights, point_idx, cell_idx, counts, narrow_id = pieces
        grad_table = lax.dynamic_index_in_dim(latent_rows, narrow_id, axis=2, keepdims=False)
        grad_table = jnp.transpose(grad_table, (1, 0, 2)).reshape(C, GX * slab_size)
        live_mask = (jnp.arange(CAP, dtype=jnp.int32)[None, :] < counts[:, None]).astype(jnp.float32)
        quad_weight = jnp.take(weights, point_idx) * live_mask[:, :, None]
        gathered = jnp.take(gathered_src, point_idx, axis=1)
        weighted = (quad_weight[None] * gathered.astype(jnp.float32)).astype(jnp.bfloat16)
        plane_local = cell_idx // slab_size
        within = cell_idx % slab_size
        row_local = within // GZ
        depth_idx = within % GZ
        target = jnp.arange(N_WIDE, dtype=jnp.int32)[:, None, None]
        cell_first = ((target * XPL + plane_local).astype(jnp.float32) + 0.5) / GX
        cell_second = ((narrow_id * YR + row_local).astype(jnp.float32) + 0.5) / GY
        cell_third = (depth_idx.astype(jnp.float32) + 0.5) / GZ
        spots = jnp.take(positions, point_idx, axis=1)
        offsets = (jnp.stack([cell_first, cell_second, cell_third]) - spots).astype(jnp.bfloat16)
        grads = jnp.take(grad_table, target * (XPL * slab_size) + cell_idx, axis=1)
        row_grads, part_kernel, part_second, part_first, part_bias = edge_math(weighted, offsets, grads, first_weight, first_bias, second_weight, kernel_mat)
        terms = (row_grads * quad_weight[None]).reshape(C, -1)
        d_local = jnp.zeros((C, P_DEV), jnp.float32).at[:, point_idx.reshape(-1)].add(terms)
        return d_local, jnp.sum(part_kernel, axis=2), jnp.sum(part_second, axis=2), jnp.sum(part_first, axis=2), jnp.sum(part_bias, axis=(1, 2))

    d_local_all, kernel_all, second_all, first_all, bias_all = lax.map(one_device, (feats_dev, pos_dev, weight_dev, points_dev, cells_dev, counts_dev, narrow_ids))
    d_points = jnp.transpose(d_local_all, (1, 0, 2)).reshape(C, P_SIZE)
    d_kernel = jnp.sum(kernel_all, axis=0)
    d_second = jnp.sum(second_all, axis=0)
    d_first = jnp.sum(first_all, axis=0)
    d_first_bias = jnp.sum(bias_all, axis=0)
    return (d_points, d_kernel, d_first, d_first_bias, d_second, d_mix, d_spectral)
```

```python
import math

import numpy as np
import ml_dtypes
import jax
import jax.numpy as jnp
from jax import lax
from jax.experimental import pallas as pl
from jax.experimental.pallas import tpu as pltpu
from jax.sharding import PartitionSpec as P

C = 64
GZ = 64
MZ = 32
CAP = 2
BLK = 128
XPL = 2
YR = 8
NW = 32
NN = 8
PDEV = 2048
CELLS = XPL * YR * GZ
KZL = MZ // NN
MODES = 32 * KZL

bf16 = jnp.bfloat16
f32 = jnp.float32
root_half = 0.7071067811865476
inv_root_tau = 0.3989422804014327


def hi_lo(table):
    table = np.asarray(table, np.float64)
    high = table.astype(ml_dtypes.bfloat16)
    low = (table - high.astype(np.float64)).astype(ml_dtypes.bfloat16)
    return high, low


def phases(freqs, positions):
    angle = (2.0 * math.pi / 64) * np.mod(np.outer(freqs, positions), 64)
    return np.cos(angle), np.sin(angle)


def make_tables():
    depth_f = np.arange(MZ)
    signed = np.where(np.arange(32) < 16, np.arange(32), np.arange(32) - 32)
    spots = np.arange(64)
    dc, ds = phases(depth_f, spots)
    rc, rs = phases(signed, spots)
    eye_2 = np.eye(2)
    eye_4 = np.eye(4)
    eye_k = np.eye(KZL)
    eye_x = np.eye(XPL)
    dri = np.stack([dc, -ds], 1).reshape(NN, KZL, 2, GZ)
    depth = np.einsum("nkrz,yw->nykrwz", dri, eye_2).reshape(128, 128)
    rot = np.zeros((2, 2, 32, 64))
    rot[0, 0] = rc
    rot[0, 1] = rs
    rot[1, 0] = -rs
    rot[1, 1] = rc
    row = np.einsum("abfy,kl->fkaylb", rot, eye_k).reshape(32 * KZL * 2, 64 * KZL * 2)
    plane = np.einsum("abfx,kl->afkxlb", rot, eye_k).reshape(2 * MODES, 64 * KZL * 2)
    volume = 64.0 * 64.0 * 64.0
    rinv = np.zeros((2, 2, 32, 64))
    rinv[0, 0] = rc
    rinv[0, 1] = -rs
    rinv[1, 0] = rs
    rinv[1, 1] = rc
    plane_inv = np.einsum("abfx,kl->axkbfl", rinv, eye_k).reshape(2 * 256, 2 * MODES) / volume
    both = np.stack([rc, rs], 0).reshape(2, 32, NN, YR)
    row_inv = np.einsum("pfny,xw,kl->nxykpfwl", both, eye_x, eye_k).reshape(512, 512)
    dinv = np.stack([dc, -ds], 0).reshape(2, NN, KZL, GZ)
    depth_inv = np.einsum("rnkz,yw->yzrnwk", dinv, eye_4).reshape(256, 256)
    return [hi_lo(t) for t in (depth, row, plane, plane_inv, row_inv, depth_inv)]


def stack_hi_lo(pair):
    return np.stack(pair, 0)


def dot(a, b, contract=((1,), (0,))):
    return lax.dot_general(a, b, (contract, ((), ())), preferred_element_type=f32)


def split2(values):
    high = values.astype(bf16)
    return high, (values - high.astype(f32)).astype(bf16)


def iota(shape, axis):
    return lax.broadcasted_iota(jnp.int32, shape, axis)


def fiota(shape, axis):
    return iota(shape, axis).astype(f32)


def call(kernel, out_shape, *, vmem=56, flops=10**8, bytes_accessed=4 * 10**6, name=None, **kw):
    return pl.pallas_call(
        kernel,
        out_shape=out_shape,
        name=name,
        compiler_params=pltpu.CompilerParams(vmem_limit_bytes=vmem * 1024 * 1024),
        cost_estimate=pl.CostEstimate(
            flops=flops, bytes_accessed=bytes_accessed, transcendentals=0
        ),
        **kw,
    )


def sds(shape, dtype):
    return jax.ShapeDtypeStruct(shape, dtype)


def depth_kernel(lat_ref, pre_ref, cot_ref, mix_ref, tab_ref, send_ref, dmix_ref, mixg_ref):
    dmix = jnp.zeros((C, C), f32)
    mix = mix_ref[...]
    nt = ((1,), (1,))
    for x in range(XPL):
        u = lat_ref[x]
        pre = pre_ref[x].astype(f32)
        slope = 0.5 * (1.0 + lax.erf(pre * root_half)) + pre * jnp.exp(
            -0.5 * pre * pre
        ) * inv_root_tau
        grad = cot_ref[x].astype(f32) * slope
        high, low = split2(grad)
        main = jnp.concatenate([u, high], axis=0)
        rest = jnp.concatenate([jnp.zeros_like(low), low], axis=0)
        for pair in range(YR // 2):
            cols = slice(pair * 128, (pair + 1) * 128)
            out = dot(tab_ref[0], main[:, cols], nt) + dot(tab_ref[1], main[:, cols], nt)
            out = out + dot(tab_ref[0], rest[:, cols], nt)
            send_ref[:, x, pair * 16 : (pair + 1) * 16, :] = out.reshape(NN, 16, 2 * C).astype(
                bf16
            )
        dmix = dmix + dot(u, high, nt) + dot(u, low, nt)
        mixg_ref[x] = dot(high, mix, ((0,), (1,))) + dot(low, mix, ((0,), (1,)))
    dmix_ref[...] = dmix


def row_kernel(recv_ref, tab_ref, send_ref):
    parts = []
    for x in range(XPL):
        block = recv_ref[:, x].reshape(512, 2 * C)
        out = dot(tab_ref[0], block) + dot(tab_ref[1], block)
        parts.append(out.reshape(32, 8, 2 * C))
    send_ref[...] = jnp.concatenate(parts, axis=1).astype(bf16)


def mode_kernel(recv_ref, tab_ref, inv_ref, w_ref, cell_ref, spec_ref, send_ref, x_ref):
    block = recv_ref[...].reshape(512, 2 * C)
    spec = dot(tab_ref[0], block) + dot(tab_ref[1], block)
    spec_ref[...] = spec
    dr = spec[:MODES, C:]
    di = spec[MODES:, C:]
    x_ref[:MODES, :] = jnp.concatenate([dr, di], axis=1).astype(bf16)
    x_ref[MODES:, :] = jnp.concatenate([di, -dr], axis=1).astype(bf16)
    lane = jnp.bitwise_and(iota((C, 2 * MODES), 1), MODES - 1)
    per = 16
    nt = ((1,), (1,))

    def body(step, acc):
        weights = w_ref[pl.ds(pl.multiple_of(step * per * C, per * C), per * C), :]
        res = dot(weights, x_ref[...], nt)
        for j in range(per):
            acc = acc + jnp.where(lane == step * per + j, res[j * C : (j + 1) * C], 0.0)
        return acc

    acc = lax.fori_loop(0, MODES // per, body, jnp.zeros((C, 2 * MODES), f32))
    high, low = split2(acc)
    out = dot(inv_ref[0], high, nt) + dot(inv_ref[1], high, nt) + dot(inv_ref[0], low, nt)
    rows = jnp.concatenate([out[:256], out[256:]], axis=1).reshape(NW, 8, 2 * C)
    cells = cell_ref[...]
    part = iota((NW, 8, BLK), 1)
    cell = jnp.where(part < 2, cells[:, 0:1, :], cells[:, 1:2, :])
    high = jnp.right_shift(cell, 8)
    low = jnp.bitwise_and(cell, 255)
    tail = jnp.where(jnp.bitwise_and(part, 1) == 0, high, low).astype(f32)
    tail = jnp.where(part < 4, tail, 0.0)
    send_ref[...] = jnp.concatenate([rows, tail], axis=1).astype(bf16)


def outer_kernel(spec_ref, out_ref, l_ref, x_ref):
    step = pl.program_id(0)
    per = out_ref.shape[0]

    @pl.when(step == 0)
    def _():
        spec = spec_ref[...]
        l_ref[...] = jnp.transpose(spec)[:C] * (1.0 / 262144.0)
        dr = spec[:MODES, C:]
        di = spec[MODES:, C:]
        first = jnp.concatenate([dr, di], axis=1)
        second = jnp.concatenate([di, -dr], axis=1)
        high, low = split2(jnp.concatenate([first, second], axis=0))
        x_ref[0] = high
        x_ref[1] = low

    ut = l_ref[...]
    lane = jnp.bitwise_and(iota((C, 2 * MODES), 1), MODES - 1)
    rows = [jnp.where(lane == step * per + j, ut, 0.0) for j in range(per)]
    high, low = split2(jnp.concatenate(rows, axis=0))
    out = dot(high, x_ref[0]) + dot(high, x_ref[1]) + dot(low, x_ref[0])
    out_ref[...] = out.reshape(per, C, 2 * C)


def row_inv_kernel(recv_ref, tab_ref, send_ref):
    block = recv_ref[...].astype(f32)[:, :8, :].reshape(256, 2 * C)
    swapped = jnp.concatenate([-block[:, C:], block[:, :C]], axis=1)
    both = jnp.concatenate([block, swapped], axis=0).astype(bf16)
    out = dot(tab_ref[0], both) + dot(tab_ref[1], both)
    send_ref[...] = out.reshape(NN, 64, 2 * C).astype(bf16)


def gather_kernel(recv_ref, mixg_ref, dinv_ref, cell_ref, out_ref):
    quarters = []
    for x in range(XPL):
        for half in range(2):
            start = x * 32 + half * 16
            block = recv_ref[:, start : start + 16, :].reshape(128, 2 * C)
            both = jnp.concatenate([block[:, :C], block[:, C:]], axis=0)
            grad = dot(dinv_ref[0], both) + dot(dinv_ref[1], both)
            quarters.append(grad + mixg_ref[x, half * 256 : (half + 1) * 256, :])
    table = jnp.concatenate(quarters, axis=1).astype(bf16)

    per = 8
    rows = per * BLK
    row16 = iota((16, 4 * BLK), 0)
    part16 = jnp.right_shift(iota((16, 4 * BLK), 1), 7)
    sel = jnp.where(row16 == part16 + 8, 1.0, 0.0).astype(bf16)
    low_lane = fiota((rows, 256), 1)
    quarter = jnp.right_shift(iota((rows, 256), 1), 6).astype(f32)
    left = iota((rows, 2 * C), 1) < C
    for g in range(NW // per):
        cells = jnp.concatenate([cell_ref[g * per + j] for j in range(per)], axis=1)
        spread = dot(cells, sel, ((0,), (0,)))
        hots = []
        for s in range(CAP):
            low = spread[:, (2 * s + 1) * BLK : (2 * s + 2) * BLK]
            hots.append(
                jnp.where(jnp.concatenate([low, low], axis=1) == low_lane, 1.0, 0.0).astype(bf16)
            )
        got = dot(jnp.concatenate(hots, axis=0), table)
        found = []
        for s in range(CAP):
            high = spread[:, 2 * s * BLK : (2 * s + 1) * BLK]
            keep = jnp.concatenate([high, high], axis=1) == quarter
            one = jnp.where(keep, got[s * rows : (s + 1) * rows], 0.0)
            one = one[:, : 2 * C] + one[:, 2 * C :]
            found.append(one + pltpu.roll(one, C, 1))
        out = jnp.where(left, found[0], found[1]).astype(bf16)
        out_ref[g * per : (g + 1) * per] = out.reshape(per, BLK, 2 * C)


def prep_kernel(
    count_ref,
    me_ref,
    feat_ref,
    pos_ref,
    wgt_ref,
    idx_ref,
    cell_ref,
    first_ref,
    wt_ref,
    act_ref,
    slope_ref,
    off_ref,
    tab_ref,
):
    weighted = feat_ref[...].astype(f32) * wgt_ref[...]
    pos = pos_ref[...]
    p0 = pos.astype(bf16).astype(f32)
    p1 = (pos - p0).astype(bf16).astype(f32)
    p2 = pos - p0 - p1
    rest = jnp.concatenate([p0, p1, p2, jnp.zeros((40, PDEV), f32)], axis=0)
    tab_ref[0] = jnp.transpose(jnp.concatenate([weighted, rest], axis=0)).astype(bf16)
    tab_ref[1] = jnp.transpose(jnp.concatenate([rest, weighted], axis=0)).astype(bf16)

    point_lane = fiota((BLK, PDEV), 1)
    row8 = iota((8, BLK), 0)
    left = iota((BLK, 2 * C), 1) < C
    sel = jnp.where(row8 == 0, 64.0, jnp.where(row8 == 1, 1.0, 0.0)).astype(bf16)
    half = NW // 2

    def one_hot(idx_row):
        high = jnp.right_shift(idx_row, 6).astype(f32)
        low = jnp.bitwise_and(idx_row, 63).astype(f32)
        packed = jnp.where(row8 == 0, high, jnp.where(row8 == 1, low, 0.0)).astype(bf16)
        spread = dot(packed, sel, ((0,), (0,)))
        spread = jnp.concatenate([spread] * (PDEV // BLK), axis=1)
        return jnp.where(spread == point_lane, 1.0, 0.0).astype(bf16)

    def edge_rows(found_t, cell, target):
        spot = found_t[0:8] + found_t[8:16] + found_t[16:24]
        plane = jnp.right_shift(cell, 9)
        rowy = jnp.bitwise_and(jnp.right_shift(cell, 6), 7)
        depth = jnp.bitwise_and(cell, 63)
        first = ((target * XPL + plane).astype(f32) + 0.5) * (1.0 / 64)
        second = ((me_ref[0] * YR + rowy).astype(f32) + 0.5) * (1.0 / 64)
        third = (depth.astype(f32) + 0.5) * (1.0 / 64)
        centre = jnp.where(row8 == 0, first, jnp.where(row8 == 1, second, third))
        return jnp.where(row8 < 3, centre - spot, jnp.where(row8 == 5, 1.0, 0.0))

    def finish(slot, pair, one, two):
        wt_ref[slot, pair] = jnp.where(left, one, two).astype(bf16)
        rows = [
            edge_rows(
                jnp.transpose(one)[C : C + 24], cell_ref[pair, pl.ds(slot, 1), :], pair
            ),
            edge_rows(
                jnp.transpose(two)[:24], cell_ref[pair + half, pl.ds(slot, 1), :], pair + half
            ),
        ]
        edge = jnp.concatenate(rows, axis=0).astype(bf16)
        off_ref[slot, pair] = edge
        before = dot(jnp.concatenate([edge, edge, edge], axis=0), first_ref[...], ((0,), (0,)))
        phi = 0.5 * (1.0 + lax.erf(before * root_half))
        act_ref[slot, pair] = (before * phi).astype(bf16)
        slope_ref[slot, pair] = phi + before * jnp.exp(-0.5 * before * before) * inv_root_tau

    group = 4

    def body(g, carry):
        base = g * group
        found = []
        for side in range(2):
            hot = jnp.concatenate(
                [
                    one_hot(idx_ref[base + j + side * half, pl.ds(0, 1), :])
                    for j in range(group)
                ],
                axis=0,
            )
            found.append(dot(hot, tab_ref[side]))
        for j in range(group):
            rows = slice(j * BLK, (j + 1) * BLK)
            finish(0, base + j, found[0][rows], found[1][rows])
        return carry

    lax.fori_loop(0, half // group, body, 0)

    def second(pair, carry):
        live_one = count_ref[pair] > 1
        live_two = count_ref[pair + half] > 1

        @pl.when(jnp.logical_or(live_one, live_two))
        def _():
            one = dot(one_hot(idx_ref[pair, pl.ds(1, 1), :]), tab_ref[0])
            two = dot(one_hot(idx_ref[pair + half, pl.ds(1, 1), :]), tab_ref[1])
            keep_one = jnp.where(live_one, 1.0, 0.0)
            keep_two = jnp.where(live_two, 1.0, 0.0)
            finish(1, pair, one * keep_one, two * keep_two)

        return carry

    lax.fori_loop(0, half, second, 0)


def edge_kernel(
    count_ref,
    grad_ref,
    wt_ref,
    act_ref,
    slope_ref,
    off_ref,
    wa_ref,
    wb_ref,
    dmix_ref,
    out_ref,
    red_ref,
    pk_ref,
    pf_ref,
):
    half = NW // 2
    pk_ref[...] = jnp.zeros_like(pk_ref)
    pf_ref[...] = jnp.zeros_like(pf_ref)

    def work(first, count, slot):
        rows = count * BLK
        take = lambda ref: ref[slot, pl.ds(first, count)].reshape(rows, 2 * C)
        left = iota((rows, 2 * C), 1) < C
        one = grad_ref[0, pl.ds(first, count)].reshape(rows, 2 * C).astype(f32)
        two = grad_ref[1, pl.ds(first, count)].reshape(rows, 2 * C).astype(f32)
        if slot == 0:
            grads = jnp.where(left, one, pltpu.roll(two, C, 1))
        else:
            grads = jnp.where(left, pltpu.roll(one, C, 1), two)
        actwgt = jnp.concatenate([take(act_ref), take(wt_ref)], axis=1)
        kl = dot(actwgt, wa_ref[...])
        gated = (grads * kl[:, : 2 * C]).astype(bf16)
        dkval = (grads * kl[:, 2 * C :]).astype(bf16)
        gk = jnp.concatenate([gated, dkval], axis=1)
        back = dot(gk, wb_ref[...])
        out_ref[slot, pl.ds(first, count)] = (
            back[:, : 2 * C].reshape(count, BLK, 2 * C).astype(bf16)
        )
        dbefore = back[:, 2 * C :] * take(slope_ref)
        pk_ref[...] += dot(actwgt, gk, ((0,), (0,)))
        high, low = split2(dbefore)
        edges = jnp.concatenate([off_ref[slot, first + j] for j in range(count)], axis=1)
        pf_ref[...] += dot(edges, high) + dot(edges, low)

    per = 4
    for g in range(half // per):
        work(g * per, per, 0)

    def second(pair, carry):
        @pl.when(jnp.logical_or(count_ref[pair] > 1, count_ref[pair + half] > 1))
        def _():
            work(pair, 1, 1)

        return carry

    lax.fori_loop(0, half, second, 0)

    pk = pk_ref[...]
    pf = pf_ref[...]
    second_sum = pk[:C, 2 * C : 3 * C] + pk[C : 2 * C, 3 * C :]
    kernel_sum = pk[2 * C : 3 * C, :C] + pk[3 * C :, C : 2 * C]
    first_sum = pf[:8, :C] + pf[8:, C:]
    low_rows = jnp.concatenate([first_sum, jnp.zeros((C - 8, C), f32)], axis=0)
    red_ref[:C, :] = jnp.concatenate([kernel_sum, second_sum], axis=1)
    red_ref[C:, :] = jnp.concatenate([dmix_ref[...], low_rows], axis=1)


def scatter_kernel(count_ref, rows_ref, idx_ref, wgt_ref, out_ref, acc_ref):
    step = pl.program_id(0)
    per = rows_ref.shape[1]
    half = NW // 2

    @pl.when(step == 0)
    def _():
        acc_ref[...] = jnp.zeros_like(acc_ref)

    point_row = iota((PDEV, BLK), 0)

    def one_hot(target, slot):
        return jnp.where(point_row == idx_ref[target, pl.ds(slot, 1), :], 1.0, 0.0).astype(bf16)

    rows = rows_ref[0].reshape(per * BLK, 2 * C)
    for side in range(2):
        hots = [one_hot(step * per + j + side * half, 0) for j in range(per)]
        acc_ref[side] += dot(jnp.concatenate(hots, axis=1), rows)
    for j in range(per):
        for side in range(2):
            target = step * per + j + side * half

            @pl.when(count_ref[target] > 1)
            def _():
                acc_ref[side] += dot(one_hot(target, 1), rows_ref[1, j])

    @pl.when(step == pl.num_programs(0) - 1)
    def _():
        total = jnp.transpose(acc_ref[0])[:C] + jnp.transpose(acc_ref[1])[C:]
        out_ref[...] = total * wgt_ref[...]


def sum_kernel(in_ref, out_ref):
    total = in_ref[0]
    for j in range(1, in_ref.shape[0]):
        total = total + in_ref[j]
    out_ref[...] = jnp.broadcast_to(total[None], out_ref.shape)


def split_kernel(in_ref, kernel_ref, second_ref, mix_ref, first_ref, bias_ref):
    total = in_ref[...].reshape(2 * C, 2 * C)
    kernel_ref[...] = total[:C, :C]
    second_ref[...] = total[:C, C:]
    mix_ref[...] = total[C:, :C]
    first_ref[...] = total[C : C + 3, C:]
    bias_ref[...] = total[C + 5 : C + 6, C:]


def exchange(block, axis):
    return lax.all_to_all(block, axis, split_axis=0, concat_axis=0, tiled=True)


def vspec():
    return pl.BlockSpec(memory_space=pltpu.VMEM)


def sspec():
    return pl.BlockSpec(memory_space=pltpu.SMEM)


def whole(shape):
    return pl.BlockSpec(shape, lambda g: (0,) * len(shape))


def lead(shape):
    return pl.BlockSpec(shape, lambda g: (g,) + (0,) * (len(shape) - 1))


def split3(values):
    a = lax.reduce_precision(values, 8, 7)
    b = lax.reduce_precision(values - a, 8, 7)
    c = values - a - b
    return [part.astype(bf16) for part in (a, b, c)]


def local(
    point_feats,
    point_pos,
    point_weight,
    nbr_point,
    nbr_cell,
    block_count,
    latent,
    preact,
    cotangent,
    spectral_weight,
    kernel_mat,
    first_weight,
    first_bias,
    second_weight,
    mix_weight,
):
    depth_t, row_t, plane_t, plane_inv_t, row_inv_t, depth_inv_t = [
        jnp.asarray(stack_hi_lo(pair)) for pair in make_tables()
    ]
    me = lax.axis_index("narrow").astype(jnp.int32).reshape(1)
    counts = block_count.reshape(NW)
    idx = nbr_point.reshape(NW, CAP, BLK)
    cell = nbr_cell.reshape(NW, CAP, BLK)
    wgt = point_weight.reshape(1, PDEV)
    pos8 = jnp.concatenate([point_pos, jnp.zeros((5, PDEV), f32)], axis=0)

    zero = jnp.zeros((C, C), bf16)
    sec = second_weight
    ker = kernel_mat
    wa = jnp.block(
        [
            [sec, zero, zero, zero],
            [zero, sec, zero, zero],
            [zero, zero, ker, zero],
            [zero, zero, zero, ker],
        ]
    )
    kt = ker.T
    st = sec.T
    wb = jnp.block(
        [
            [kt, zero, zero, zero],
            [zero, kt, zero, zero],
            [zero, zero, st, zero],
            [zero, zero, zero, st],
        ]
    )
    z2 = jnp.zeros((2, C), f32)
    half = jnp.concatenate([first_weight, z2, first_bias[None], z2], axis=0)
    zh = jnp.zeros((8, C), f32)
    first_full = jnp.concatenate(
        [jnp.concatenate([half, zh], axis=1), jnp.concatenate([zh, half], axis=1)], axis=0
    )
    first48 = jnp.concatenate(split3(first_full), axis=0)

    send1, dmix_part, mixg = call(
        depth_kernel,
        (sds((NN, XPL, 64, 2 * C), bf16), sds((C, C), f32), sds((XPL, 512, C), f32)),
        in_specs=[vspec()] * 5,
        out_specs=(vspec(),) * 3,
        name="depth_forward",
    )(latent, preact, cotangent, mix_weight, depth_t)
    recv1 = exchange(send1, "narrow")

    send2 = call(
        row_kernel,
        sds((NW, 16, 2 * C), bf16),
        in_specs=[vspec()] * 2,
        out_specs=vspec(),
        vmem=4,
        name="row_forward",
    )(recv1, row_t)
    send2, weights = lax.optimization_barrier(
        (send2, spectral_weight.reshape(MODES * C, 2 * C))
    )
    recv2 = exchange(send2, "wide")
    weights = weights.astype(bf16)


    spec, send3 = call(
        mode_kernel,
        (sds((2 * MODES, 2 * C), f32), sds((NW, 16, 2 * C), bf16)),
        in_specs=[vspec()] * 5,
        out_specs=(vspec(),) * 2,
        scratch_shapes=[pltpu.VMEM((2 * MODES, 2 * C), bf16)],
        vmem=12,
        name="mode_mix",
    )(recv2, plane_t, plane_inv_t, weights, cell)
    recv3 = exchange(send3, "wide")

    send4 = call(
        row_inv_kernel,
        sds((NN, 64, 2 * C), bf16),
        in_specs=[vspec()] * 2,
        out_specs=vspec(),
        vmem=8,
        name="row_inverse",
    )(recv3, row_inv_t)
    recv4 = exchange(send4, "narrow")

    found = call(
        gather_kernel,
        sds((NW, BLK, 2 * C), bf16),
        in_specs=[vspec()] * 4,
        out_specs=vspec(),
        vmem=20,
        name="cell_gather",
    )(recv4, mixg, depth_inv_t, recv3)

    found, idx, spec = lax.optimization_barrier((found, idx, spec))
    grads = exchange(found, "wide")

    half = NW // 2
    wt, act, slope, off = call(
        prep_kernel,
        (
            sds((CAP, half, BLK, 2 * C), bf16),
            sds((CAP, half, BLK, 2 * C), bf16),
            sds((CAP, half, BLK, 2 * C), f32),
            sds((CAP, half, 16, 2 * C), bf16),
        ),
        in_specs=[sspec(), sspec()] + [vspec()] * 6,
        out_specs=(vspec(),) * 4,
        scratch_shapes=[pltpu.VMEM((2, PDEV, 2 * C), bf16)],
        flops=2 * 10**9,
        bytes_accessed=2 * 10**7,
        vmem=32,
        name="edge_prepare",
    )(counts, me, point_feats, pos8, wgt, idx, cell, first48)

    d_spectral = call(
        outer_kernel,
        sds((MODES, C, 2 * C), f32),
        grid=(8,),
        in_specs=[whole((2 * MODES, 2 * C))],
        out_specs=lead((MODES // 8, C, 2 * C)),
        scratch_shapes=[pltpu.VMEM((C, 2 * MODES), f32), pltpu.VMEM((2, 2 * MODES, 2 * C), bf16)],
        flops=2 * 10**9,
        vmem=16,
        name="spectral_grad",
    )(spec).reshape(spectral_weight.shape)

    wt, d_spectral = lax.optimization_barrier((wt, d_spectral))
    rows, red = call(
        edge_kernel,
        (sds((CAP, half, BLK, 2 * C), bf16), sds((2 * C, 2 * C), f32)),
        in_specs=[sspec()] + [vspec()] * 8,
        out_specs=(vspec(),) * 2,
        scratch_shapes=[
            pltpu.VMEM((4 * C, 4 * C), f32),
            pltpu.VMEM((16, 2 * C), f32),
        ],
        vmem=24,
        name="edge_grads",
    )(counts, grads.reshape(2, half, BLK, 2 * C), wt, act, slope, off, wa, wb, dmix_part)

    part = exchange(red.reshape(NN, 16, 2 * C), "narrow")
    part = call(
        sum_kernel,
        sds((NW, 16, 2 * C), f32),
        in_specs=[vspec()],
        out_specs=vspec(),
        vmem=4,
        name="sum_narrow",
    )(part)
    part = exchange(part, "wide")

    d_points = call(
        scatter_kernel,
        sds((C, PDEV), f32),
        grid=(4,),
        in_specs=[
            sspec(),
            pl.BlockSpec((CAP, half // 4, BLK, 2 * C), lambda g: (0, g, 0, 0)),
            whole((NW, CAP, BLK)),
            whole((1, PDEV)),
        ],
        out_specs=whole((C, PDEV)),
        scratch_shapes=[pltpu.VMEM((2, PDEV, 2 * C), f32)],
        flops=2 * 10**9,
        vmem=32,
        name="point_grads",
    )(counts, rows, idx, wgt)

    part, d_points = lax.optimization_barrier((part, d_points))
    part = call(
        sum_kernel,
        sds((NN, 16, 2 * C), f32),
        in_specs=[vspec()],
        out_specs=vspec(),
        vmem=4,
        name="sum_wide",
    )(part)
    part = exchange(part, "narrow")

    d_kernel, d_second, d_mix, d_first, d_bias = call(
        split_kernel,
        (sds((C, C), f32),) * 3 + (sds((3, C), f32), sds((1, C), f32)),
        in_specs=[vspec()],
        out_specs=(vspec(),) * 5,
        vmem=4,
        name="split_sums",
    )(part)
    return (d_points, d_kernel, d_first, d_bias.reshape(C), d_second, d_mix, d_spectral)


def solution(mesh):
    return jax.shard_map(
        local,
        mesh=mesh,
        in_specs=(
            P(None, ("wide", "narrow")),
            P(None, ("wide", "narrow")),
            P(("wide", "narrow")),
            P("wide", "narrow", None, None, None),
            P("wide", "narrow", None, None, None),
            P("wide", "narrow", None),
            P("wide", None, "narrow"),
            P("wide", None, "narrow"),
            P("wide", None, "narrow"),
            P("wide", None, "narrow", None, None),
            P(),
            P(),
            P(),
            P(),
            P(),
        ),
        out_specs=(
            P(None, ("wide", "narrow")),
            P(),
            P(),
            P(),
            P(),
            P(),
            P("wide", None, "narrow", None, None),
        ),
        check_vma=False,
    )
```

```python
import math

import numpy as np
import ml_dtypes
import jax
import jax.numpy as jnp
from jax import lax
from jax.experimental import pallas as pl
from jax.experimental.pallas import tpu as pltpu
from jax.sharding import PartitionSpec as P

C = 64
GZ = 64
MZ = 32
CAP = 2
BLK = 128
XPL = 2
YR = 8
NW = 32
NN = 8
PDEV = 2048
CELLS = XPL * YR * GZ
KZL = MZ // NN
MODES = 32 * KZL

bf16 = jnp.bfloat16
f32 = jnp.float32
root_half = 0.7071067811865476
inv_root_tau = 0.3989422804014327


def hi_lo(table):
    table = np.asarray(table, np.float64)
    high = table.astype(ml_dtypes.bfloat16)
    low = (table - high.astype(np.float64)).astype(ml_dtypes.bfloat16)
    return high, low


def phases(freqs, positions):
    angle = (2.0 * math.pi / 64) * np.mod(np.outer(freqs, positions), 64)
    return np.cos(angle), np.sin(angle)


def make_tables():
    depth_f = np.arange(MZ)
    signed = np.where(np.arange(32) < 16, np.arange(32), np.arange(32) - 32)
    spots = np.arange(64)
    dc, ds = phases(depth_f, spots)
    rc, rs = phases(signed, spots)
    eye_2 = np.eye(2)
    eye_4 = np.eye(4)
    eye_k = np.eye(KZL)
    eye_x = np.eye(XPL)
    dri = np.stack([dc, -ds], 1).reshape(NN, KZL, 2, GZ)
    depth = np.einsum("nkrz,yw->nykrwz", dri, eye_2).reshape(128, 128)
    rot = np.zeros((2, 2, 32, 64))
    rot[0, 0] = rc
    rot[0, 1] = rs
    rot[1, 0] = -rs
    rot[1, 1] = rc
    row = np.einsum("abfy,kl->fkaylb", rot, eye_k).reshape(32 * KZL * 2, 64 * KZL * 2)
    plane = np.einsum("abfx,kl->afkxlb", rot, eye_k).reshape(2 * MODES, 64 * KZL * 2)
    volume = 64.0 * 64.0 * 64.0
    rinv = np.zeros((2, 2, 32, 64))
    rinv[0, 0] = rc
    rinv[0, 1] = -rs
    rinv[1, 0] = rs
    rinv[1, 1] = rc
    plane_inv = np.einsum("abfx,kl->axkbfl", rinv, eye_k).reshape(2 * 256, 2 * MODES) / volume
    both = np.stack([rc, rs], 0).reshape(2, 32, NN, YR)
    row_inv = np.einsum("pfny,xw,kl->nxykpfwl", both, eye_x, eye_k).reshape(512, 512)
    dinv = np.stack([dc, -ds], 0).reshape(2, NN, KZL, GZ)
    depth_inv = np.einsum("rnkz,yw->yzrnwk", dinv, eye_4).reshape(256, 256)
    return [hi_lo(t) for t in (depth, row, plane, plane_inv, row_inv, depth_inv)]


def stack_hi_lo(pair):
    return np.stack(pair, 0)


def dot(a, b, contract=((1,), (0,))):
    return lax.dot_general(a, b, (contract, ((), ())), preferred_element_type=f32)


def split2(values):
    high = values.astype(bf16)
    return high, (values - high.astype(f32)).astype(bf16)


def iota(shape, axis):
    return lax.broadcasted_iota(jnp.int32, shape, axis)


def fiota(shape, axis):
    return iota(shape, axis).astype(f32)


def call(kernel, out_shape, *, vmem=56, flops=10**8, bytes_accessed=4 * 10**6, name=None, **kw):
    return pl.pallas_call(
        kernel,
        out_shape=out_shape,
        name=name,
        compiler_params=pltpu.CompilerParams(vmem_limit_bytes=vmem * 1024 * 1024),
        cost_estimate=pl.CostEstimate(
            flops=flops, bytes_accessed=bytes_accessed, transcendentals=0
        ),
        **kw,
    )


def sds(shape, dtype):
    return jax.ShapeDtypeStruct(shape, dtype)


def depth_kernel(lat_ref, pre_ref, cot_ref, tab_ref, send_ref, grad_ref):
    nt = ((1,), (1,))
    for x in range(XPL):
        u = lat_ref[x]
        pre = pre_ref[x].astype(f32)
        slope = 0.5 * (1.0 + lax.erf(pre * root_half)) + pre * jnp.exp(
            -0.5 * pre * pre
        ) * inv_root_tau
        grad = cot_ref[x].astype(f32) * slope
        high, low = split2(grad)
        grad_ref[x] = jnp.concatenate([high, low], axis=0)
        main = jnp.concatenate([u, high], axis=0)
        rest = jnp.concatenate([jnp.zeros_like(low), low], axis=0)
        for pair in range(YR // 2):
            cols = slice(pair * 128, (pair + 1) * 128)
            out = dot(tab_ref[0], main[:, cols], nt) + dot(tab_ref[1], main[:, cols], nt)
            out = out + dot(tab_ref[0], rest[:, cols], nt)
            send_ref[:, x, pair * 16 : (pair + 1) * 16, :] = out.reshape(NN, 16, 2 * C).astype(
                bf16
            )


def mix_kernel(lat_ref, grad_ref, mix_ref, tab_ref, dmix_ref, mixg_ref, tab_out_ref):
    dmix = jnp.zeros((C, C), f32)
    mix = mix_ref[...]
    nt = ((1,), (1,))
    for x in range(XPL):
        u = lat_ref[x]
        high = grad_ref[x, :C]
        low = grad_ref[x, C:]
        dmix = dmix + dot(u, high, nt) + dot(u, low, nt)
        mixg_ref[x] = dot(high, mix, ((0,), (1,))) + dot(low, mix, ((0,), (1,)))
    dmix_ref[...] = dmix
    tab_out_ref[...] = tab_ref[...]


def stage_kernel(after_ref, tab_ref, inv_ref, cell_ref, tab_out_ref, inv_out_ref, cell_out_ref):
    tab_out_ref[...] = tab_ref[...]
    inv_out_ref[...] = inv_ref[...]
    cell_out_ref[...] = cell_ref[...]


def row_kernel(recv_ref, tab_ref, send_ref):
    parts = []
    for x in range(XPL):
        block = recv_ref[:, x].reshape(512, 2 * C)
        out = dot(tab_ref[0], block) + dot(tab_ref[1], block)
        parts.append(out.reshape(32, 8, 2 * C))
    send_ref[...] = jnp.concatenate(parts, axis=1).astype(bf16)


def mode_kernel(
    recv_ref, tab_ref, inv_ref, w_hbm, cell_ref, spec_ref, send_ref, x_ref, w_ref, sems
):
    per = 16
    steps = MODES // per
    copies = [
        pltpu.make_async_copy(
            w_hbm.at[pl.ds(g * per * C, per * C)], w_ref.at[pl.ds(g * per * C, per * C)], sems.at[g]
        )
        for g in range(steps)
    ]
    for copy in copies:
        copy.start()
    block = recv_ref[...].reshape(512, 2 * C)
    spec = dot(tab_ref[0], block) + dot(tab_ref[1], block)
    spec_ref[...] = spec
    dr = spec[:MODES, C:]
    di = spec[MODES:, C:]
    x_ref[:MODES, :] = jnp.concatenate([dr, di], axis=1).astype(bf16)
    x_ref[MODES:, :] = jnp.concatenate([di, -dr], axis=1).astype(bf16)
    lane = jnp.bitwise_and(iota((C, 2 * MODES), 1), MODES - 1)
    nt = ((1,), (1,))
    acc = jnp.zeros((C, 2 * MODES), f32)
    for g in range(steps):
        copies[g].wait()
        weights = w_ref[g * per * C : (g + 1) * per * C, :].astype(bf16)
        res = dot(weights, x_ref[...], nt)
        for j in range(per):
            acc = acc + jnp.where(lane == g * per + j, res[j * C : (j + 1) * C], 0.0)
    high, low = split2(acc)
    out = dot(inv_ref[0], high, nt) + dot(inv_ref[1], high, nt) + dot(inv_ref[0], low, nt)
    rows = jnp.concatenate([out[:256], out[256:]], axis=1).reshape(NW, 8, 2 * C)
    cells = cell_ref[...]
    part = iota((NW, 8, BLK), 1)
    cell = jnp.where(part < 2, cells[:, 0:1, :], cells[:, 1:2, :])
    high = jnp.right_shift(cell, 8)
    low = jnp.bitwise_and(cell, 255)
    tail = jnp.where(jnp.bitwise_and(part, 1) == 0, high, low).astype(f32)
    tail = jnp.where(part < 4, tail, 0.0)
    send_ref[...] = jnp.concatenate([rows, tail], axis=1).astype(bf16)


def outer_kernel(spec_ref, out_ref, l_ref, x_ref):
    step = pl.program_id(0)
    per = out_ref.shape[0]

    @pl.when(step == 0)
    def _():
        spec = spec_ref[...]
        l_ref[...] = jnp.transpose(spec)[:C] * (1.0 / 262144.0)
        dr = spec[:MODES, C:]
        di = spec[MODES:, C:]
        first = jnp.concatenate([dr, di], axis=1)
        second = jnp.concatenate([di, -dr], axis=1)
        high, low = split2(jnp.concatenate([first, second], axis=0))
        x_ref[0] = high
        x_ref[1] = low

    ut = l_ref[...]
    lane = jnp.bitwise_and(iota((C, 2 * MODES), 1), MODES - 1)
    rows = [jnp.where(lane == step * per + j, ut, 0.0) for j in range(per)]
    high, low = split2(jnp.concatenate(rows, axis=0))
    out = dot(high, x_ref[0]) + dot(high, x_ref[1]) + dot(low, x_ref[0])
    out_ref[...] = out.reshape(per, C, 2 * C)


def row_inv_kernel(recv_ref, tab_ref, send_ref):
    block = recv_ref[...].astype(f32)[:, :8, :].reshape(256, 2 * C)
    swapped = jnp.concatenate([-block[:, C:], block[:, :C]], axis=1)
    both = jnp.concatenate([block, swapped], axis=0).astype(bf16)
    out = dot(tab_ref[0], both) + dot(tab_ref[1], both)
    send_ref[...] = out.reshape(NN, 64, 2 * C).astype(bf16)


def gather_kernel(recv_ref, mixg_ref, dinv_ref, cell_ref, out_ref):
    quarters = []
    for x in range(XPL):
        for half in range(2):
            start = x * 32 + half * 16
            block = recv_ref[:, start : start + 16, :].reshape(128, 2 * C)
            both = jnp.concatenate([block[:, :C], block[:, C:]], axis=0)
            grad = dot(dinv_ref[0], both) + dot(dinv_ref[1], both)
            quarters.append(grad + mixg_ref[x, half * 256 : (half + 1) * 256, :])
    table = jnp.concatenate(quarters, axis=1).astype(bf16)

    per = 8
    rows = per * BLK
    row16 = iota((16, 4 * BLK), 0)
    part16 = jnp.right_shift(iota((16, 4 * BLK), 1), 7)
    sel = jnp.where(row16 == part16 + 8, 1.0, 0.0).astype(bf16)
    low_lane = fiota((rows, 256), 1)
    quarter = jnp.right_shift(iota((rows, 256), 1), 6).astype(f32)
    left = iota((rows, 2 * C), 1) < C
    for g in range(NW // per):
        cells = jnp.concatenate([cell_ref[g * per + j] for j in range(per)], axis=1)
        spread = dot(cells, sel, ((0,), (0,)))
        hots = []
        for s in range(CAP):
            low = spread[:, (2 * s + 1) * BLK : (2 * s + 2) * BLK]
            hots.append(
                jnp.where(jnp.concatenate([low, low], axis=1) == low_lane, 1.0, 0.0).astype(bf16)
            )
        got = dot(jnp.concatenate(hots, axis=0), table)
        found = []
        for s in range(CAP):
            high = spread[:, 2 * s * BLK : (2 * s + 1) * BLK]
            keep = jnp.concatenate([high, high], axis=1) == quarter
            one = jnp.where(keep, got[s * rows : (s + 1) * rows], 0.0)
            one = one[:, : 2 * C] + one[:, 2 * C :]
            found.append(one + pltpu.roll(one, C, 1))
        out = jnp.where(left, found[0], found[1]).astype(bf16)
        out_ref[g * per : (g + 1) * per] = out.reshape(per, BLK, 2 * C)


def prep_kernel(
    count_ref,
    me_ref,
    feat_ref,
    pos_ref,
    wgt_ref,
    idx_ref,
    cell_ref,
    first_ref,
    aw_ref,
    slope_ref,
    off_ref,
    tab_ref,
):
    weighted = feat_ref[...].astype(f32) * wgt_ref[...]
    pos = pos_ref[...]
    p0 = pos.astype(bf16).astype(f32)
    p1 = (pos - p0).astype(bf16).astype(f32)
    p2 = pos - p0 - p1
    rest = jnp.concatenate([p0, p1, p2, jnp.zeros((40, PDEV), f32)], axis=0)
    tab_ref[0] = jnp.transpose(jnp.concatenate([weighted, rest], axis=0)).astype(bf16)
    tab_ref[1] = jnp.transpose(jnp.concatenate([rest, weighted], axis=0)).astype(bf16)

    point_lane = fiota((BLK, PDEV), 1)
    row8 = iota((8, BLK), 0)
    left = iota((BLK, 2 * C), 1) < C
    sel = jnp.where(row8 == 0, 64.0, jnp.where(row8 == 1, 1.0, 0.0)).astype(bf16)
    half = NW // 2

    def one_hot(idx_row):
        high = jnp.right_shift(idx_row, 6).astype(f32)
        low = jnp.bitwise_and(idx_row, 63).astype(f32)
        packed = jnp.where(row8 == 0, high, jnp.where(row8 == 1, low, 0.0)).astype(bf16)
        spread = dot(packed, sel, ((0,), (0,)))
        spread = jnp.concatenate([spread] * (PDEV // BLK), axis=1)
        return jnp.where(spread == point_lane, 1.0, 0.0).astype(bf16)

    def edge_rows(found_t, cell, target):
        spot = found_t[0:8] + found_t[8:16] + found_t[16:24]
        plane = jnp.right_shift(cell, 9)
        rowy = jnp.bitwise_and(jnp.right_shift(cell, 6), 7)
        depth = jnp.bitwise_and(cell, 63)
        first = ((target * XPL + plane).astype(f32) + 0.5) * (1.0 / 64)
        second = ((me_ref[0] * YR + rowy).astype(f32) + 0.5) * (1.0 / 64)
        third = (depth.astype(f32) + 0.5) * (1.0 / 64)
        centre = jnp.where(row8 == 0, first, jnp.where(row8 == 1, second, third))
        return jnp.where(row8 < 3, centre - spot, jnp.where(row8 == 5, 1.0, 0.0))

    def finish(slot, pair, one, two):
        weighted_pair = jnp.where(left, one, two)
        rows = [
            edge_rows(
                jnp.transpose(one)[C : C + 24], cell_ref[pair, pl.ds(slot, 1), :], pair
            ),
            edge_rows(
                jnp.transpose(two)[:24], cell_ref[pair + half, pl.ds(slot, 1), :], pair + half
            ),
        ]
        edge = jnp.concatenate(rows, axis=0).astype(bf16)
        off_ref[slot, pair] = edge
        before = dot(jnp.concatenate([edge, edge, edge], axis=0), first_ref[...], ((0,), (0,)))
        phi = 0.5 * (1.0 + lax.erf(before * root_half))
        aw_ref[slot, pair] = jnp.concatenate([before * phi, weighted_pair], axis=1).astype(bf16)
        slope_ref[slot, pair] = phi + before * jnp.exp(-0.5 * before * before) * inv_root_tau

    group = 4

    def body(g, carry):
        base = g * group
        found = []
        for side in range(2):
            hot = jnp.concatenate(
                [
                    one_hot(idx_ref[base + j + side * half, pl.ds(0, 1), :])
                    for j in range(group)
                ],
                axis=0,
            )
            found.append(dot(hot, tab_ref[side]))
        for j in range(group):
            rows = slice(j * BLK, (j + 1) * BLK)
            finish(0, base + j, found[0][rows], found[1][rows])
        return carry

    lax.fori_loop(0, half // group, body, 0)

    def second(pair, carry):
        live_one = count_ref[pair] > 1
        live_two = count_ref[pair + half] > 1

        @pl.when(jnp.logical_or(live_one, live_two))
        def _():
            one = dot(one_hot(idx_ref[pair, pl.ds(1, 1), :]), tab_ref[0])
            two = dot(one_hot(idx_ref[pair + half, pl.ds(1, 1), :]), tab_ref[1])
            keep_one = jnp.where(live_one, 1.0, 0.0)
            keep_two = jnp.where(live_two, 1.0, 0.0)
            finish(1, pair, one * keep_one, two * keep_two)

        return carry

    lax.fori_loop(0, half, second, 0)


def edge_kernel(
    count_ref,
    grad_ref,
    aw_hbm,
    slope_hbm,
    off_hbm,
    dmix_hbm,
    wa_ref,
    wb_ref,
    out_hbm,
    red_ref,
    pk_ref,
    pf_ref,
    aw_ref,
    slope_ref,
    off_ref,
    dmix_ref,
    rows_ref,
    in_sems,
    out_sems,
):
    half = NW // 2
    per = 4
    groups = half // per

    def group_copies(g):
        span = pl.ds(g * per, per)
        return [
            pltpu.make_async_copy(aw_hbm.at[0, span], aw_ref.at[0, span], in_sems.at[2 * g]),
            pltpu.make_async_copy(
                slope_hbm.at[0, span], slope_ref.at[0, span], in_sems.at[2 * g + 1]
            ),
        ]

    base = 2 * groups
    off_copy = pltpu.make_async_copy(off_hbm, off_ref, in_sems.at[base])
    late = [
        pltpu.make_async_copy(aw_hbm.at[1], aw_ref.at[1], in_sems.at[base + 1]),
        pltpu.make_async_copy(slope_hbm.at[1], slope_ref.at[1], in_sems.at[base + 2]),
        pltpu.make_async_copy(dmix_hbm, dmix_ref, in_sems.at[base + 3]),
    ]
    out_copies = [
        pltpu.make_async_copy(
            rows_ref.at[0, pl.ds(g * per, per)],
            out_hbm.at[0, pl.ds(g * per, per)],
            out_sems.at[g],
        )
        for g in range(groups)
    ]
    out_late = pltpu.make_async_copy(rows_ref.at[1], out_hbm.at[1], out_sems.at[groups])

    for copy in group_copies(0):
        copy.start()
    off_copy.start()
    for g in range(1, groups):
        for copy in group_copies(g):
            copy.start()
    for copy in late:
        copy.start()

    pk_ref[...] = jnp.zeros_like(pk_ref)
    pf_ref[...] = jnp.zeros_like(pf_ref)

    def work(first, count, slot):
        rows = count * BLK
        left = iota((rows, 2 * C), 1) < C
        one = grad_ref[0, pl.ds(first, count)].reshape(rows, 2 * C).astype(f32)
        two = grad_ref[1, pl.ds(first, count)].reshape(rows, 2 * C).astype(f32)
        if slot == 0:
            grads = jnp.where(left, one, pltpu.roll(two, C, 1))
        else:
            grads = jnp.where(left, pltpu.roll(one, C, 1), two)
        actwgt = aw_ref[slot, pl.ds(first, count)].reshape(rows, 4 * C)
        kl = dot(actwgt, wa_ref[...])
        gated = (grads * kl[:, : 2 * C]).astype(bf16)
        dkval = (grads * kl[:, 2 * C :]).astype(bf16)
        gk = jnp.concatenate([gated, dkval], axis=1)
        back = dot(gk, wb_ref[...])
        rows_ref[slot, pl.ds(first, count)] = (
            back[:, : 2 * C].reshape(count, BLK, 2 * C).astype(bf16)
        )
        slope = slope_ref[slot, pl.ds(first, count)].reshape(rows, 2 * C)
        dbefore = back[:, 2 * C :] * slope
        pk_ref[...] += dot(actwgt, gk, ((0,), (0,)))
        high, low = split2(dbefore)
        edges = jnp.concatenate([off_ref[slot, first + j] for j in range(count)], axis=1)
        pf_ref[...] += dot(edges, high) + dot(edges, low)

    for g in range(groups):
        for copy in group_copies(g):
            copy.wait()
        if g == 0:
            off_copy.wait()
        work(g * per, per, 0)
        out_copies[g].start()
    for copy in late:
        copy.wait()

    def second(pair, carry):
        @pl.when(jnp.logical_or(count_ref[pair] > 1, count_ref[pair + half] > 1))
        def _():
            work(pair, 1, 1)

        return carry

    lax.fori_loop(0, half, second, 0)
    out_late.start()

    pk = pk_ref[...]
    pf = pf_ref[...]
    second_sum = pk[:C, 2 * C : 3 * C] + pk[C : 2 * C, 3 * C :]
    kernel_sum = pk[2 * C : 3 * C, :C] + pk[3 * C :, C : 2 * C]
    first_sum = pf[:8, :C] + pf[8:, C:]
    low_rows = jnp.concatenate([first_sum, jnp.zeros((C - 8, C), f32)], axis=0)
    red_ref[:C, :] = jnp.concatenate([kernel_sum, second_sum], axis=1)
    red_ref[C:, :] = jnp.concatenate([dmix_ref[...], low_rows], axis=1)
    for copy in out_copies:
        copy.wait()
    out_late.wait()


def scatter_kernel(count_ref, rows_ref, idx_ref, wgt_ref, out_ref, acc_ref):
    step = pl.program_id(0)
    per = rows_ref.shape[1]
    half = NW // 2

    @pl.when(step == 0)
    def _():
        acc_ref[...] = jnp.zeros_like(acc_ref)

    low_row = iota((512, BLK), 0)
    row8 = iota((8, BLK), 0)
    ones = jnp.where(row8 == 0, 1.0, 0.0).astype(bf16)

    def add(targets, slot, values, count):
        hots = []
        tops = []
        for target in targets:
            idx = idx_ref[target, pl.ds(slot, 1), :]
            low = jnp.bitwise_and(idx, 511)
            hots.append(jnp.where(low_row == low, 1.0, 0.0).astype(bf16))
            top = jnp.right_shift(idx, 9).astype(f32)
            tops.append(jnp.where(row8 == 0, top, 0.0).astype(bf16))
        spread = dot(jnp.concatenate(tops, axis=1), ones, ((0,), (0,)))
        right = iota((count * BLK, 2 * C), 1) >= C
        quarter = jnp.where(right, 1.0, 0.0)
        first = jnp.where(spread == quarter, values, 0.0)
        second = jnp.where(spread == quarter + 2.0, values, 0.0)
        both = jnp.concatenate([first, second], axis=1).astype(bf16)
        acc_ref[...] += dot(jnp.concatenate(hots, axis=1), both)

    def doubled(values, side):
        left = iota(values.shape, 1) < C
        turned = pltpu.roll(values, C, 1)
        if side == 0:
            return jnp.where(left, values, turned)
        return jnp.where(left, turned, values)

    rows = rows_ref[0].reshape(per * BLK, 2 * C).astype(f32)
    for side in range(2):
        targets = [step * per + j + side * half for j in range(per)]
        add(targets, 0, doubled(rows, side), per)
    for j in range(per):
        for side in range(2):
            target = step * per + j + side * half

            @pl.when(count_ref[target] > 1)
            def _():
                add([target], 1, doubled(rows_ref[1, j].astype(f32), side), 1)

    @pl.when(step == pl.num_programs(0) - 1)
    def _():
        for pair in range(2):
            part = jnp.transpose(acc_ref[:, pair * 2 * C : (pair + 1) * 2 * C])
            for one in range(2):
                start = (2 * pair + one) * 512
                out_ref[:, start : start + 512] = (
                    part[one * C : (one + 1) * C] * wgt_ref[:, start : start + 512]
                )


def sum_kernel(in_ref, out_ref):
    total = in_ref[0]
    for j in range(1, in_ref.shape[0]):
        total = total + in_ref[j]
    out_ref[...] = jnp.broadcast_to(total[None], out_ref.shape)


def split_kernel(in_ref, kernel_ref, second_ref, mix_ref, first_ref, bias_ref):
    total = in_ref[...].reshape(2 * C, 2 * C)
    kernel_ref[...] = total[:C, :C]
    second_ref[...] = total[:C, C:]
    mix_ref[...] = total[C:, :C]
    first_ref[...] = total[C : C + 3, C:]
    bias_ref[...] = total[C + 5 : C + 6, C:]


def exchange(block, axis):
    return lax.all_to_all(block, axis, split_axis=0, concat_axis=0, tiled=True)


def vspec():
    return pl.BlockSpec(memory_space=pltpu.VMEM)


def hspec():
    return pl.BlockSpec(memory_space=pltpu.HBM)


def far(array):
    return pltpu.with_memory_space_constraint(array, pltpu.HBM)


def sspec():
    return pl.BlockSpec(memory_space=pltpu.SMEM)


def whole(shape):
    return pl.BlockSpec(shape, lambda g: (0,) * len(shape))


def lead(shape):
    return pl.BlockSpec(shape, lambda g: (g,) + (0,) * (len(shape) - 1))


def split3(values):
    a = lax.reduce_precision(values, 8, 7)
    b = lax.reduce_precision(values - a, 8, 7)
    c = values - a - b
    return [part.astype(bf16) for part in (a, b, c)]


def local(
    point_feats,
    point_pos,
    point_weight,
    nbr_point,
    nbr_cell,
    block_count,
    latent,
    preact,
    cotangent,
    spectral_weight,
    kernel_mat,
    first_weight,
    first_bias,
    second_weight,
    mix_weight,
):
    depth_t, row_t, plane_t, plane_inv_t, row_inv_t, depth_inv_t = [
        jnp.asarray(stack_hi_lo(pair)) for pair in make_tables()
    ]
    me = lax.axis_index("narrow").astype(jnp.int32).reshape(1)
    counts = block_count.reshape(NW)
    idx = nbr_point.reshape(NW, CAP, BLK)
    cell = nbr_cell.reshape(NW, CAP, BLK)
    wgt = point_weight.reshape(1, PDEV)
    pos8 = jnp.concatenate([point_pos, jnp.zeros((5, PDEV), f32)], axis=0)

    zero = jnp.zeros((C, C), bf16)
    sec = second_weight
    ker = kernel_mat
    wa = jnp.block(
        [
            [sec, zero, zero, zero],
            [zero, sec, zero, zero],
            [zero, zero, ker, zero],
            [zero, zero, zero, ker],
        ]
    )
    kt = ker.T
    st = sec.T
    wb = jnp.block(
        [
            [kt, zero, zero, zero],
            [zero, kt, zero, zero],
            [zero, zero, st, zero],
            [zero, zero, zero, st],
        ]
    )
    z2 = jnp.zeros((2, C), f32)
    half = jnp.concatenate([first_weight, z2, first_bias[None], z2], axis=0)
    zh = jnp.zeros((8, C), f32)
    first_full = jnp.concatenate(
        [jnp.concatenate([half, zh], axis=1), jnp.concatenate([zh, half], axis=1)], axis=0
    )
    first48 = jnp.concatenate(split3(first_full), axis=0)

    send1, grad_parts = call(
        depth_kernel,
        (sds((NN, XPL, 64, 2 * C), bf16), sds((XPL, 2 * C, 512), bf16)),
        in_specs=[vspec()] * 4,
        out_specs=(vspec(),) * 2,
        name="depth_forward",
    )(latent, preact, cotangent, depth_t)
    recv1 = exchange(send1, "narrow")
    dmix_part, mixg, row_t = call(
        mix_kernel,
        (sds((C, C), f32), sds((XPL, 512, C), f32), sds(row_t.shape, bf16)),
        in_specs=[vspec()] * 4,
        out_specs=(vspec(),) * 3,
        vmem=8,
        name="pointwise_mix",
    )(latent, grad_parts, mix_weight, row_t)
    recv1, mixg = lax.optimization_barrier((recv1, mixg))

    send2 = call(
        row_kernel,
        sds((NW, 16, 2 * C), bf16),
        in_specs=[vspec()] * 2,
        out_specs=vspec(),
        vmem=4,
        name="row_forward",
    )(recv1, row_t)
    recv2 = exchange(send2, "wide")
    plane_t, plane_inv_t, cell_near = call(
        stage_kernel,
        (sds(plane_t.shape, bf16), sds(plane_inv_t.shape, bf16), sds(cell.shape, jnp.int32)),
        in_specs=[hspec()] + [vspec()] * 3,
        out_specs=(vspec(),) * 3,
        vmem=8,
        name="stage_tables",
    )(send2, plane_t, plane_inv_t, cell)
    recv2, plane_t = lax.optimization_barrier((recv2, plane_t))
    weights = far(spectral_weight.reshape(MODES * C, 2 * C))
    spec, send3 = call(
        mode_kernel,
        (sds((2 * MODES, 2 * C), f32), sds((NW, 16, 2 * C), bf16)),
        in_specs=[vspec()] * 3 + [hspec(), vspec()],
        out_specs=(vspec(),) * 2,
        scratch_shapes=[
            pltpu.VMEM((2 * MODES, 2 * C), bf16),
            pltpu.VMEM((MODES * C, 2 * C), f32),
            pltpu.SemaphoreType.DMA((8,)),
        ],
        vmem=20,
        name="mode_mix",
    )(recv2, plane_t, plane_inv_t, weights, cell_near)
    recv3 = exchange(send3, "wide")

    send4 = call(
        row_inv_kernel,
        sds((NN, 64, 2 * C), bf16),
        in_specs=[vspec()] * 2,
        out_specs=vspec(),
        vmem=8,
        name="row_inverse",
    )(recv3, row_inv_t)
    recv4 = exchange(send4, "narrow")

    found = call(
        gather_kernel,
        sds((NW, BLK, 2 * C), bf16),
        in_specs=[vspec()] * 4,
        out_specs=vspec(),
        vmem=20,
        name="cell_gather",
    )(recv4, mixg, depth_inv_t, recv3)

    found, idx, spec = lax.optimization_barrier((found, idx, spec))
    grads = exchange(found, "wide")

    half = NW // 2
    aw, slope, off = call(
        prep_kernel,
        (
            pltpu.HBM((CAP, half, BLK, 4 * C), bf16),
            pltpu.HBM((CAP, half, BLK, 2 * C), f32),
            pltpu.HBM((CAP, half, 16, 2 * C), bf16),
        ),
        in_specs=[sspec(), sspec()] + [vspec()] * 6,
        out_specs=(vspec(),) * 3,
        scratch_shapes=[pltpu.VMEM((2, PDEV, 2 * C), bf16)],
        flops=2 * 10**9,
        bytes_accessed=2 * 10**7,
        vmem=32,
        name="edge_prepare",
    )(counts, me, point_feats, pos8, wgt, idx, cell, first48)

    d_spectral = call(
        outer_kernel,
        sds((MODES, C, 2 * C), f32),
        grid=(8,),
        in_specs=[whole((2 * MODES, 2 * C))],
        out_specs=lead((MODES // 8, C, 2 * C)),
        scratch_shapes=[pltpu.VMEM((C, 2 * MODES), f32), pltpu.VMEM((2, 2 * MODES, 2 * C), bf16)],
        flops=2 * 10**9,
        vmem=16,
        name="spectral_grad",
    )(spec).reshape(spectral_weight.shape)

    aw, d_spectral = lax.optimization_barrier((aw, d_spectral))
    rows, red = call(
        edge_kernel,
        (pltpu.HBM((CAP, half, BLK, 2 * C), bf16), sds((2 * C, 2 * C), f32)),
        in_specs=[sspec(), vspec()] + [hspec()] * 4 + [vspec()] * 2,
        out_specs=(hspec(), vspec()),
        scratch_shapes=[
            pltpu.VMEM((4 * C, 4 * C), f32),
            pltpu.VMEM((16, 2 * C), f32),
            pltpu.VMEM((CAP, half, BLK, 4 * C), bf16),
            pltpu.VMEM((CAP, half, BLK, 2 * C), f32),
            pltpu.VMEM((CAP, half, 16, 2 * C), bf16),
            pltpu.VMEM((C, C), f32),
            pltpu.VMEM((CAP, half, BLK, 2 * C), bf16),
            pltpu.SemaphoreType.DMA((12,)),
            pltpu.SemaphoreType.DMA((5,)),
        ],
        vmem=24,
        name="edge_grads",
    )(
        counts,
        grads.reshape(2, half, BLK, 2 * C),
        far(aw),
        far(slope),
        far(off),
        far(dmix_part),
        wa,
        wb,
    )

    part = exchange(red.reshape(NN, 16, 2 * C), "narrow")
    part = call(
        sum_kernel,
        sds((NW, 16, 2 * C), f32),
        in_specs=[vspec()],
        out_specs=vspec(),
        vmem=4,
        name="sum_narrow",
    )(part)
    part = exchange(part, "wide")

    d_points = call(
        scatter_kernel,
        sds((C, PDEV), f32),
        grid=(4,),
        in_specs=[
            sspec(),
            pl.BlockSpec((CAP, half // 4, BLK, 2 * C), lambda g: (0, g, 0, 0)),
            whole((NW, CAP, BLK)),
            whole((1, PDEV)),
        ],
        out_specs=whole((C, PDEV)),
        scratch_shapes=[pltpu.VMEM((512, 4 * C), f32)],
        flops=2 * 10**9,
        vmem=32,
        name="point_grads",
    )(counts, far(rows), idx, wgt)

    part, d_points = lax.optimization_barrier((part, d_points))
    part = call(
        sum_kernel,
        sds((NN, 16, 2 * C), f32),
        in_specs=[vspec()],
        out_specs=vspec(),
        vmem=4,
        name="sum_wide",
    )(part)
    part = exchange(part, "narrow")

    d_kernel, d_second, d_mix, d_first, d_bias = call(
        split_kernel,
        (sds((C, C), f32),) * 3 + (sds((3, C), f32), sds((1, C), f32)),
        in_specs=[vspec()],
        out_specs=(vspec(),) * 5,
        vmem=4,
        name="split_sums",
    )(part)
    return (d_points, d_kernel, d_first, d_bias.reshape(C), d_second, d_mix, d_spectral)


def solution(mesh):
    return jax.shard_map(
        local,
        mesh=mesh,
        in_specs=(
            P(None, ("wide", "narrow")),
            P(None, ("wide", "narrow")),
            P(("wide", "narrow")),
            P("wide", "narrow", None, None, None),
            P("wide", "narrow", None, None, None),
            P("wide", "narrow", None),
            P("wide", None, "narrow"),
            P("wide", None, "narrow"),
            P("wide", None, "narrow"),
            P("wide", None, "narrow", None, None),
            P(),
            P(),
            P(),
            P(),
            P(),
        ),
        out_specs=(
            P(None, ("wide", "narrow")),
            P(),
            P(),
            P(),
            P(),
            P(),
            P("wide", None, "narrow", None, None),
        ),
        check_vma=False,
    )
```

```python
import math

import numpy as np
import ml_dtypes
import jax
import jax.numpy as jnp
from jax import lax
from jax.experimental import pallas as pl
from jax.experimental.pallas import tpu as pltpu
from jax.sharding import PartitionSpec as P

C = 64
GZ = 64
MZ = 32
CAP = 2
BLK = 128
XPL = 2
YR = 8
NW = 32
NN = 8
PDEV = 2048
CELLS = XPL * YR * GZ
KZL = MZ // NN
MODES = 32 * KZL

bf16 = jnp.bfloat16
f32 = jnp.float32
root_half = 0.7071067811865476
inv_root_tau = 0.3989422804014327


def hi_lo(table):
    table = np.asarray(table, np.float64)
    high = table.astype(ml_dtypes.bfloat16)
    low = (table - high.astype(np.float64)).astype(ml_dtypes.bfloat16)
    return high, low


def phases(freqs, positions):
    angle = (2.0 * math.pi / 64) * np.mod(np.outer(freqs, positions), 64)
    return np.cos(angle), np.sin(angle)


def make_tables():
    depth_f = np.arange(MZ)
    signed = np.where(np.arange(32) < 16, np.arange(32), np.arange(32) - 32)
    spots = np.arange(64)
    dc, ds = phases(depth_f, spots)
    rc, rs = phases(signed, spots)
    eye_2 = np.eye(2)
    eye_4 = np.eye(4)
    eye_k = np.eye(KZL)
    eye_x = np.eye(XPL)
    dri = np.stack([dc, -ds], 1).reshape(NN, KZL, 2, GZ)
    depth = np.einsum("nkrz,yw->nykrwz", dri, eye_2).reshape(128, 128)
    rot = np.zeros((2, 2, 32, 64))
    rot[0, 0] = rc
    rot[0, 1] = rs
    rot[1, 0] = -rs
    rot[1, 1] = rc
    row = np.einsum("abfy,kl->fkaylb", rot, eye_k).reshape(32 * KZL * 2, 64 * KZL * 2)
    plane = np.einsum("abfx,kl->afkxlb", rot, eye_k).reshape(2 * MODES, 64 * KZL * 2)
    volume = 64.0 * 64.0 * 64.0
    rinv = np.zeros((2, 2, 32, 64))
    rinv[0, 0] = rc
    rinv[0, 1] = -rs
    rinv[1, 0] = rs
    rinv[1, 1] = rc
    plane_inv = np.einsum("abfx,kl->axkbfl", rinv, eye_k).reshape(2 * 256, 2 * MODES) / volume
    both = np.stack([rc, rs], 0).reshape(2, 32, NN, YR)
    row_inv = np.einsum("pfny,xw,kl->nxykpfwl", both, eye_x, eye_k).reshape(512, 512)
    dinv = np.stack([dc, -ds], 0).reshape(2, NN, KZL, GZ)
    depth_inv = np.einsum("rnkz,yw->yzrnwk", dinv, eye_4).reshape(256, 256)
    return [hi_lo(t) for t in (depth, row, plane, plane_inv, row_inv, depth_inv)]


def stack_hi_lo(pair):
    return np.stack(pair, 0)


def dot(a, b, contract=((1,), (0,))):
    return lax.dot_general(a, b, (contract, ((), ())), preferred_element_type=f32)


def split2(values):
    high = values.astype(bf16)
    return high, (values - high.astype(f32)).astype(bf16)


def iota(shape, axis):
    return lax.broadcasted_iota(jnp.int32, shape, axis)


def fiota(shape, axis):
    return iota(shape, axis).astype(f32)


def call(kernel, out_shape, *, vmem=56, flops=10**8, bytes_accessed=4 * 10**6, name=None, **kw):
    return pl.pallas_call(
        kernel,
        out_shape=out_shape,
        name=name,
        compiler_params=pltpu.CompilerParams(vmem_limit_bytes=vmem * 1024 * 1024),
        cost_estimate=pl.CostEstimate(
            flops=flops, bytes_accessed=bytes_accessed, transcendentals=0
        ),
        **kw,
    )


def sds(shape, dtype):
    return jax.ShapeDtypeStruct(shape, dtype)


def depth_kernel(lat_ref, pre_ref, cot_ref, tab_ref, send_ref, grad_ref):
    nt = ((1,), (1,))
    for x in range(XPL):
        u = lat_ref[x]
        pre = pre_ref[x].astype(f32)
        slope = 0.5 * (1.0 + lax.erf(pre * root_half)) + pre * jnp.exp(
            -0.5 * pre * pre
        ) * inv_root_tau
        grad = cot_ref[x].astype(f32) * slope
        high, low = split2(grad)
        grad_ref[x] = jnp.concatenate([high, low], axis=0)
        main = jnp.concatenate([u, high], axis=0)
        rest = jnp.concatenate([jnp.zeros_like(low), low], axis=0)
        for pair in range(YR // 2):
            cols = slice(pair * 128, (pair + 1) * 128)
            out = dot(tab_ref[0], main[:, cols], nt) + dot(tab_ref[1], main[:, cols], nt)
            out = out + dot(tab_ref[0], rest[:, cols], nt)
            send_ref[:, x, pair * 16 : (pair + 1) * 16, :] = out.reshape(NN, 16, 2 * C).astype(
                bf16
            )


def mix_kernel(lat_ref, grad_ref, mix_ref, dmix_ref, mixg_ref):
    dmix = jnp.zeros((C, C), f32)
    mix = mix_ref[...]
    nt = ((1,), (1,))
    for x in range(XPL):
        u = lat_ref[x]
        high = grad_ref[x, :C]
        low = grad_ref[x, C:]
        dmix = dmix + dot(u, high, nt) + dot(u, low, nt)
        mixg_ref[x] = dot(high, mix, ((0,), (1,))) + dot(low, mix, ((0,), (1,)))
    dmix_ref[...] = dmix


def row_kernel(recv_ref, tab_hbm, send_ref, tab_ref, sem):
    copy = pltpu.make_async_copy(tab_hbm, tab_ref, sem)
    copy.start()
    copy.wait()
    parts = []
    for x in range(XPL):
        block = recv_ref[:, x].reshape(512, 2 * C)
        out = dot(tab_ref[0], block) + dot(tab_ref[1], block)
        parts.append(out.reshape(32, 8, 2 * C))
    send_ref[...] = jnp.concatenate(parts, axis=1).astype(bf16)


def mode_kernel(
    recv_ref,
    w_ref,
    tab_hbm,
    inv_hbm,
    cell_hbm,
    spec_ref,
    send_ref,
    x_ref,
    tab_ref,
    inv_ref,
    cell_ref,
    sems,
):
    per = 16
    steps = MODES // per
    copies = [
        pltpu.make_async_copy(source, target, sems.at[k])
        for k, (source, target) in enumerate(
            ((tab_hbm, tab_ref), (inv_hbm, inv_ref), (cell_hbm, cell_ref))
        )
    ]
    for copy in copies:
        copy.start()
    copies[0].wait()
    block = recv_ref[...].reshape(512, 2 * C)
    spec = dot(tab_ref[0], block) + dot(tab_ref[1], block)
    spec_ref[...] = spec
    dr = spec[:MODES, C:]
    di = spec[MODES:, C:]
    x_ref[:MODES, :] = jnp.concatenate([dr, di], axis=1).astype(bf16)
    x_ref[MODES:, :] = jnp.concatenate([di, -dr], axis=1).astype(bf16)
    lane = jnp.bitwise_and(iota((C, 2 * MODES), 1), MODES - 1)
    nt = ((1,), (1,))
    acc = jnp.zeros((C, 2 * MODES), f32)
    for g in range(steps):
        weights = w_ref[g * per * C : (g + 1) * per * C, :]
        res = dot(weights, x_ref[...], nt)
        for j in range(per):
            acc = acc + jnp.where(lane == g * per + j, res[j * C : (j + 1) * C], 0.0)
    high, low = split2(acc)
    copies[1].wait()
    copies[2].wait()
    out = dot(inv_ref[0], high, nt) + dot(inv_ref[1], high, nt) + dot(inv_ref[0], low, nt)
    rows = jnp.concatenate([out[:256], out[256:]], axis=1).reshape(NW, 8, 2 * C)
    cells = cell_ref[...]
    part = iota((NW, 8, BLK), 1)
    cell = jnp.where(part < 2, cells[:, 0:1, :], cells[:, 1:2, :])
    high = jnp.right_shift(cell, 8)
    low = jnp.bitwise_and(cell, 255)
    tail = jnp.where(jnp.bitwise_and(part, 1) == 0, high, low).astype(f32)
    tail = jnp.where(part < 4, tail, 0.0)
    send_ref[...] = jnp.concatenate([rows, tail], axis=1).astype(bf16)


def outer_kernel(spec_ref, out_ref, l_ref, x_ref):
    step = pl.program_id(0)
    per = out_ref.shape[0]

    @pl.when(step == 0)
    def _():
        spec = spec_ref[...]
        l_ref[...] = jnp.transpose(spec)[:C] * (1.0 / 262144.0)
        dr = spec[:MODES, C:]
        di = spec[MODES:, C:]
        first = jnp.concatenate([dr, di], axis=1)
        second = jnp.concatenate([di, -dr], axis=1)
        high, low = split2(jnp.concatenate([first, second], axis=0))
        x_ref[0] = high
        x_ref[1] = low

    ut = l_ref[...]
    lane = jnp.bitwise_and(iota((C, 2 * MODES), 1), MODES - 1)
    rows = [jnp.where(lane == step * per + j, ut, 0.0) for j in range(per)]
    high, low = split2(jnp.concatenate(rows, axis=0))
    out = dot(high, x_ref[0]) + dot(high, x_ref[1]) + dot(low, x_ref[0])
    out_ref[...] = out.reshape(per, C, 2 * C)


def row_inv_kernel(recv_ref, tab_ref, send_ref):
    block = recv_ref[...].astype(f32)[:, :8, :].reshape(256, 2 * C)
    swapped = jnp.concatenate([-block[:, C:], block[:, :C]], axis=1)
    both = jnp.concatenate([block, swapped], axis=0).astype(bf16)
    out = dot(tab_ref[0], both) + dot(tab_ref[1], both)
    send_ref[...] = out.reshape(NN, 64, 2 * C).astype(bf16)


def gather_kernel(recv_ref, mixg_ref, dinv_ref, cell_ref, out_hbm, out_ref, sems):
    quarters = []
    for x in range(XPL):
        for half in range(2):
            start = x * 32 + half * 16
            block = recv_ref[:, start : start + 16, :].reshape(128, 2 * C)
            both = jnp.concatenate([block[:, :C], block[:, C:]], axis=0)
            grad = dot(dinv_ref[0], both) + dot(dinv_ref[1], both)
            quarters.append(grad + mixg_ref[x, half * 256 : (half + 1) * 256, :])
    table = jnp.concatenate(quarters, axis=1).astype(bf16)

    per = 8
    copies = [
        pltpu.make_async_copy(
            out_ref.at[pl.ds(g * per, per)], out_hbm.at[pl.ds(g * per, per)], sems.at[g]
        )
        for g in range(NW // per)
    ]
    rows = per * BLK
    row16 = iota((16, 4 * BLK), 0)
    part16 = jnp.right_shift(iota((16, 4 * BLK), 1), 7)
    sel = jnp.where(row16 == part16 + 8, 1.0, 0.0).astype(bf16)
    low_lane = fiota((rows, 256), 1)
    quarter = jnp.right_shift(iota((rows, 256), 1), 6).astype(f32)
    left = iota((rows, 2 * C), 1) < C
    for g in range(NW // per):
        cells = jnp.concatenate([cell_ref[g * per + j] for j in range(per)], axis=1)
        spread = dot(cells, sel, ((0,), (0,)))
        hots = []
        for s in range(CAP):
            low = spread[:, (2 * s + 1) * BLK : (2 * s + 2) * BLK]
            hots.append(
                jnp.where(jnp.concatenate([low, low], axis=1) == low_lane, 1.0, 0.0).astype(bf16)
            )
        got = dot(jnp.concatenate(hots, axis=0), table)
        found = []
        for s in range(CAP):
            high = spread[:, 2 * s * BLK : (2 * s + 1) * BLK]
            keep = jnp.concatenate([high, high], axis=1) == quarter
            one = jnp.where(keep, got[s * rows : (s + 1) * rows], 0.0)
            one = one[:, : 2 * C] + one[:, 2 * C :]
            found.append(one + pltpu.roll(one, C, 1))
        out = jnp.where(left, found[0], found[1]).astype(bf16)
        out_ref[g * per : (g + 1) * per] = out.reshape(per, BLK, 2 * C)
        copies[g].start()
    for copy in copies:
        copy.wait()


def prep_kernel(
    count_ref,
    me_ref,
    feat_ref,
    pos_ref,
    wgt_ref,
    idx_ref,
    cell_ref,
    first_ref,
    aw_ref,
    slope_ref,
    off_ref,
    aw_late_ref,
    slope_late_ref,
    off_late_ref,
    tab_ref,
):
    weighted = feat_ref[...].astype(f32) * wgt_ref[...]
    pos = pos_ref[...]
    p0 = pos.astype(bf16).astype(f32)
    p1 = (pos - p0).astype(bf16).astype(f32)
    p2 = pos - p0 - p1
    rest = jnp.concatenate([p0, p1, p2, jnp.zeros((40, PDEV), f32)], axis=0)
    tab_ref[0] = jnp.transpose(jnp.concatenate([weighted, rest], axis=0)).astype(bf16)
    tab_ref[1] = jnp.transpose(jnp.concatenate([rest, weighted], axis=0)).astype(bf16)

    point_lane = fiota((BLK, PDEV), 1)
    row8 = iota((8, BLK), 0)
    left = iota((BLK, 2 * C), 1) < C
    sel = jnp.where(row8 == 0, 64.0, jnp.where(row8 == 1, 1.0, 0.0)).astype(bf16)
    half = NW // 2

    def one_hot(idx_row):
        high = jnp.right_shift(idx_row, 6).astype(f32)
        low = jnp.bitwise_and(idx_row, 63).astype(f32)
        packed = jnp.where(row8 == 0, high, jnp.where(row8 == 1, low, 0.0)).astype(bf16)
        spread = dot(packed, sel, ((0,), (0,)))
        spread = jnp.concatenate([spread] * (PDEV // BLK), axis=1)
        return jnp.where(spread == point_lane, 1.0, 0.0).astype(bf16)

    def edge_rows(found_t, cell, target):
        spot = found_t[0:8] + found_t[8:16] + found_t[16:24]
        plane = jnp.right_shift(cell, 9)
        rowy = jnp.bitwise_and(jnp.right_shift(cell, 6), 7)
        depth = jnp.bitwise_and(cell, 63)
        first = ((target * XPL + plane).astype(f32) + 0.5) * (1.0 / 64)
        second = ((me_ref[0] * YR + rowy).astype(f32) + 0.5) * (1.0 / 64)
        third = (depth.astype(f32) + 0.5) * (1.0 / 64)
        centre = jnp.where(row8 == 0, first, jnp.where(row8 == 1, second, third))
        return jnp.where(row8 < 3, centre - spot, jnp.where(row8 == 5, 1.0, 0.0))

    def finish(slot, pair, one, two):
        weighted_pair = jnp.where(left, one, two)
        rows = [
            edge_rows(
                jnp.transpose(one)[C : C + 24], cell_ref[pair, pl.ds(slot, 1), :], pair
            ),
            edge_rows(
                jnp.transpose(two)[:24], cell_ref[pair + half, pl.ds(slot, 1), :], pair + half
            ),
        ]
        edge = jnp.concatenate(rows, axis=0).astype(bf16)
        aw_out = (aw_ref, aw_late_ref)[slot]
        slope_out = (slope_ref, slope_late_ref)[slot]
        off_out = (off_ref, off_late_ref)[slot]
        off_out[pair] = edge
        before = dot(jnp.concatenate([edge, edge, edge], axis=0), first_ref[...], ((0,), (0,)))
        phi = 0.5 * (1.0 + lax.erf(before * root_half))
        aw_out[pair] = jnp.concatenate([before * phi, weighted_pair], axis=1).astype(bf16)
        slope_out[pair] = phi + before * jnp.exp(-0.5 * before * before) * inv_root_tau

    group = 4

    def body(g, carry):
        base = g * group
        found = []
        for side in range(2):
            hot = jnp.concatenate(
                [
                    one_hot(idx_ref[base + j + side * half, pl.ds(0, 1), :])
                    for j in range(group)
                ],
                axis=0,
            )
            found.append(dot(hot, tab_ref[side]))
        for j in range(group):
            rows = slice(j * BLK, (j + 1) * BLK)
            finish(0, base + j, found[0][rows], found[1][rows])
        return carry

    lax.fori_loop(0, half // group, body, 0)

    def second(pair, carry):
        live_one = count_ref[pair] > 1
        live_two = count_ref[pair + half] > 1

        @pl.when(jnp.logical_or(live_one, live_two))
        def _():
            one = dot(one_hot(idx_ref[pair, pl.ds(1, 1), :]), tab_ref[0])
            two = dot(one_hot(idx_ref[pair + half, pl.ds(1, 1), :]), tab_ref[1])
            keep_one = jnp.where(live_one, 1.0, 0.0)
            keep_two = jnp.where(live_two, 1.0, 0.0)
            finish(1, pair, one * keep_one, two * keep_two)

        return carry

    lax.fori_loop(0, half, second, 0)


def edge_kernel(
    count_ref,
    grad_ref,
    aw_ref,
    slope_ref,
    off_ref,
    aw_hbm,
    slope_hbm,
    off_hbm,
    dmix_hbm,
    wa_ref,
    wb_ref,
    out_hbm,
    red_ref,
    pk_ref,
    pf_ref,
    aw_late,
    slope_late,
    off_late,
    dmix_ref,
    rows_ref,
    out_sems,
    late_sems,
):
    half = NW // 2
    per = 4
    groups = half // per

    dmix_copy = pltpu.make_async_copy(dmix_hbm, dmix_ref, out_sems.at[groups])

    def late_copies(pair):
        return [
            pltpu.make_async_copy(aw_hbm.at[pair], aw_late.at[pair], late_sems.at[0, pair]),
            pltpu.make_async_copy(
                slope_hbm.at[pair], slope_late.at[pair], late_sems.at[1, pair]
            ),
            pltpu.make_async_copy(off_hbm.at[pair], off_late.at[pair], late_sems.at[3, pair]),
        ]

    def late_out(pair):
        return pltpu.make_async_copy(
            rows_ref.at[1, pair], out_hbm.at[1, pair], late_sems.at[2, pair]
        )

    def each_live(step):
        def body(pair, carry):
            @pl.when(jnp.logical_or(count_ref[pair] > 1, count_ref[pair + half] > 1))
            def _():
                step(pair)

            return carry

        lax.fori_loop(0, half, body, 0)

    out_copies = [
        pltpu.make_async_copy(
            rows_ref.at[0, pl.ds(g * per, per)],
            out_hbm.at[0, pl.ds(g * per, per)],
            out_sems.at[g],
        )
        for g in range(groups)
    ]

    dmix_copy.start()

    def begin(pair):
        for copy in late_copies(pair):
            copy.start()

    each_live(begin)

    pk_ref[...] = jnp.zeros_like(pk_ref)
    pf_ref[...] = jnp.zeros_like(pf_ref)

    def work(first, count, slot):
        rows = count * BLK
        left = iota((rows, 2 * C), 1) < C
        one = grad_ref[0, pl.ds(first, count)].reshape(rows, 2 * C).astype(f32)
        two = grad_ref[1, pl.ds(first, count)].reshape(rows, 2 * C).astype(f32)
        if slot == 0:
            grads = jnp.where(left, one, pltpu.roll(two, C, 1))
        else:
            grads = jnp.where(left, pltpu.roll(one, C, 1), two)
        aw_in, slope_in, off_in = (
            (aw_ref, slope_ref, off_ref),
            (aw_late, slope_late, off_late),
        )[slot]
        actwgt = aw_in[pl.ds(first, count)].reshape(rows, 4 * C)
        kl = dot(actwgt, wa_ref[...])
        gated = (grads * kl[:, : 2 * C]).astype(bf16)
        dkval = (grads * kl[:, 2 * C :]).astype(bf16)
        gk = jnp.concatenate([gated, dkval], axis=1)
        back = dot(gk, wb_ref[...])
        rows_ref[slot, pl.ds(first, count)] = (
            back[:, : 2 * C].reshape(count, BLK, 2 * C).astype(bf16)
        )
        slope = slope_in[pl.ds(first, count)].reshape(rows, 2 * C)
        dbefore = back[:, 2 * C :] * slope
        pk_ref[...] += dot(actwgt, gk, ((0,), (0,)))
        high, low = split2(dbefore)
        edges = jnp.concatenate([off_in[first + j] for j in range(count)], axis=1)
        pf_ref[...] += dot(edges, high) + dot(edges, low)

    for g in range(groups):
        work(g * per, per, 0)
        out_copies[g].start()

    def second(pair):
        for copy in late_copies(pair):
            copy.wait()
        work(pair, 1, 1)
        late_out(pair).start()

    each_live(second)
    dmix_copy.wait()

    pk = pk_ref[...]
    pf = pf_ref[...]
    second_sum = pk[:C, 2 * C : 3 * C] + pk[C : 2 * C, 3 * C :]
    kernel_sum = pk[2 * C : 3 * C, :C] + pk[3 * C :, C : 2 * C]
    first_sum = pf[:8, :C] + pf[8:, C:]
    low_rows = jnp.concatenate([first_sum, jnp.zeros((C - 8, C), f32)], axis=0)
    red_ref[:C, :] = jnp.concatenate([kernel_sum, second_sum], axis=1)
    red_ref[C:, :] = jnp.concatenate([dmix_ref[...], low_rows], axis=1)
    for copy in out_copies:
        copy.wait()
    each_live(lambda pair: late_out(pair).wait())


def scatter_kernel(count_ref, rows_ref, idx_ref, wgt_ref, out_ref, acc_ref):
    step = pl.program_id(0)
    per = rows_ref.shape[1]
    half = NW // 2

    @pl.when(step == 0)
    def _():
        acc_ref[...] = jnp.zeros_like(acc_ref)

    low_row = iota((512, BLK), 0)
    row8 = iota((8, BLK), 0)
    ones = jnp.where(row8 == 0, 1.0, 0.0).astype(bf16)

    def add(targets, slot, values, count):
        hots = []
        tops = []
        for target in targets:
            idx = idx_ref[target, pl.ds(slot, 1), :]
            low = jnp.bitwise_and(idx, 511)
            hots.append(jnp.where(low_row == low, 1.0, 0.0).astype(bf16))
            top = jnp.right_shift(idx, 9).astype(f32)
            tops.append(jnp.where(row8 == 0, top, 0.0).astype(bf16))
        spread = dot(jnp.concatenate(tops, axis=1), ones, ((0,), (0,)))
        right = iota((count * BLK, 2 * C), 1) >= C
        quarter = jnp.where(right, 1.0, 0.0)
        first = jnp.where(spread == quarter, values, 0.0)
        second = jnp.where(spread == quarter + 2.0, values, 0.0)
        both = jnp.concatenate([first, second], axis=1).astype(bf16)
        acc_ref[...] += dot(jnp.concatenate(hots, axis=1), both)

    def doubled(values, side):
        left = iota(values.shape, 1) < C
        turned = pltpu.roll(values, C, 1)
        if side == 0:
            return jnp.where(left, values, turned)
        return jnp.where(left, turned, values)

    rows = rows_ref[0].reshape(per * BLK, 2 * C).astype(f32)
    for side in range(2):
        targets = [step * per + j + side * half for j in range(per)]
        add(targets, 0, doubled(rows, side), per)
    for j in range(per):
        for side in range(2):
            target = step * per + j + side * half

            @pl.when(count_ref[target] > 1)
            def _():
                add([target], 1, doubled(rows_ref[1, j].astype(f32), side), 1)

    @pl.when(step == pl.num_programs(0) - 1)
    def _():
        for pair in range(2):
            part = jnp.transpose(acc_ref[:, pair * 2 * C : (pair + 1) * 2 * C])
            for one in range(2):
                start = (2 * pair + one) * 512
                out_ref[:, start : start + 512] = (
                    part[one * C : (one + 1) * C] * wgt_ref[:, start : start + 512]
                )


def sum_kernel(in_ref, out_ref):
    total = in_ref[0]
    for j in range(1, in_ref.shape[0]):
        total = total + in_ref[j]
    out_ref[...] = jnp.broadcast_to(total[None], out_ref.shape)


def split_kernel(in_ref, kernel_ref, second_ref, mix_ref, first_ref, bias_ref):
    total = in_ref[...].reshape(2 * C, 2 * C)
    kernel_ref[...] = total[:C, :C]
    second_ref[...] = total[:C, C:]
    mix_ref[...] = total[C:, :C]
    first_ref[...] = total[C : C + 3, C:]
    bias_ref[...] = total[C + 5 : C + 6, C:]


def exchange(block, axis):
    return lax.all_to_all(block, axis, split_axis=0, concat_axis=0, tiled=True)


def vspec():
    return pl.BlockSpec(memory_space=pltpu.VMEM)


def hspec():
    return pl.BlockSpec(memory_space=pltpu.HBM)


def far(array):
    return pltpu.with_memory_space_constraint(array, pltpu.HBM)


def sspec():
    return pl.BlockSpec(memory_space=pltpu.SMEM)


def whole(shape):
    return pl.BlockSpec(shape, lambda g: (0,) * len(shape))


def lead(shape):
    return pl.BlockSpec(shape, lambda g: (g,) + (0,) * (len(shape) - 1))


def split3(values):
    a = lax.reduce_precision(values, 8, 7)
    b = lax.reduce_precision(values - a, 8, 7)
    c = values - a - b
    return [part.astype(bf16) for part in (a, b, c)]


def local(
    point_feats,
    point_pos,
    point_weight,
    nbr_point,
    nbr_cell,
    block_count,
    latent,
    preact,
    cotangent,
    spectral_weight,
    kernel_mat,
    first_weight,
    first_bias,
    second_weight,
    mix_weight,
):
    depth_t, row_t, plane_t, plane_inv_t, row_inv_t, depth_inv_t = [
        jnp.asarray(stack_hi_lo(pair)) for pair in make_tables()
    ]
    me = lax.axis_index("narrow").astype(jnp.int32).reshape(1)
    counts = block_count.reshape(NW)
    idx = nbr_point.reshape(NW, CAP, BLK)
    cell = nbr_cell.reshape(NW, CAP, BLK)
    wgt = point_weight.reshape(1, PDEV)
    pos8 = jnp.concatenate([point_pos, jnp.zeros((5, PDEV), f32)], axis=0)

    zero = jnp.zeros((C, C), bf16)
    sec = second_weight
    ker = kernel_mat
    wa = jnp.block(
        [
            [sec, zero, zero, zero],
            [zero, sec, zero, zero],
            [zero, zero, ker, zero],
            [zero, zero, zero, ker],
        ]
    )
    kt = ker.T
    st = sec.T
    wb = jnp.block(
        [
            [kt, zero, zero, zero],
            [zero, kt, zero, zero],
            [zero, zero, st, zero],
            [zero, zero, zero, st],
        ]
    )
    z2 = jnp.zeros((2, C), f32)
    half = jnp.concatenate([first_weight, z2, first_bias[None], z2], axis=0)
    zh = jnp.zeros((8, C), f32)
    first_full = jnp.concatenate(
        [jnp.concatenate([half, zh], axis=1), jnp.concatenate([zh, half], axis=1)], axis=0
    )
    first48 = jnp.concatenate(split3(first_full), axis=0)

    send1, grad_parts = call(
        depth_kernel,
        (sds((NN, XPL, 64, 2 * C), bf16), sds((XPL, 2 * C, 512), bf16)),
        in_specs=[vspec()] * 4,
        out_specs=(vspec(),) * 2,
        name="depth_forward",
    )(latent, preact, cotangent, depth_t)
    send1, weights = lax.optimization_barrier(
        (send1, spectral_weight.reshape(MODES * C, 2 * C))
    )
    recv1 = exchange(send1, "narrow")
    weights = weights.astype(bf16)
    dmix_part, mixg = call(
        mix_kernel,
        (sds((C, C), f32), sds((XPL, 512, C), f32)),
        in_specs=[vspec()] * 3,
        out_specs=(vspec(),) * 2,
        vmem=8,
        name="pointwise_mix",
    )(latent, grad_parts, mix_weight)
    recv1, mixg, weights = lax.optimization_barrier((recv1, mixg, weights))

    send2 = call(
        row_kernel,
        sds((NW, 16, 2 * C), bf16),
        in_specs=[vspec(), hspec()],
        out_specs=vspec(),
        scratch_shapes=[pltpu.VMEM(row_t.shape, bf16), pltpu.SemaphoreType.DMA],
        vmem=4,
        name="row_forward",
    )(recv1, far(row_t))
    recv2 = exchange(send2, "wide")
    spec, send3 = call(
        mode_kernel,
        (sds((2 * MODES, 2 * C), f32), sds((NW, 16, 2 * C), bf16)),
        in_specs=[vspec()] * 2 + [hspec()] * 3,
        out_specs=(vspec(),) * 2,
        scratch_shapes=[
            pltpu.VMEM((2 * MODES, 2 * C), bf16),
            pltpu.VMEM(plane_t.shape, bf16),
            pltpu.VMEM(plane_inv_t.shape, bf16),
            pltpu.VMEM(cell.shape, jnp.int32),
            pltpu.SemaphoreType.DMA((3,)),
        ],
        vmem=12,
        name="mode_mix",
    )(recv2, weights, far(plane_t), far(plane_inv_t), far(cell))
    recv3 = exchange(send3, "wide")

    send4 = call(
        row_inv_kernel,
        sds((NN, 64, 2 * C), bf16),
        in_specs=[vspec()] * 2,
        out_specs=vspec(),
        vmem=8,
        name="row_inverse",
    )(recv3, row_inv_t)
    recv4 = exchange(send4, "narrow")

    found = call(
        gather_kernel,
        pltpu.HBM((NW, BLK, 2 * C), bf16),
        in_specs=[vspec()] * 4,
        out_specs=hspec(),
        scratch_shapes=[
            pltpu.VMEM((NW, BLK, 2 * C), bf16),
            pltpu.SemaphoreType.DMA((4,)),
        ],
        vmem=20,
        name="cell_gather",
    )(recv4, mixg, depth_inv_t, recv3)

    found, idx, spec = lax.optimization_barrier((found, idx, spec))
    grads = exchange(found, "wide")

    half = NW // 2
    aw, slope, off, aw_late, slope_late, off_late = call(
        prep_kernel,
        (
            sds((half, BLK, 4 * C), bf16),
            sds((half, BLK, 2 * C), f32),
            sds((half, 16, 2 * C), bf16),
            pltpu.HBM((half, BLK, 4 * C), bf16),
            pltpu.HBM((half, BLK, 2 * C), f32),
            pltpu.HBM((half, 16, 2 * C), bf16),
        ),
        in_specs=[sspec(), sspec()] + [vspec()] * 6,
        out_specs=(vspec(),) * 6,
        scratch_shapes=[pltpu.VMEM((2, PDEV, 2 * C), bf16)],
        flops=2 * 10**9,
        bytes_accessed=2 * 10**7,
        vmem=32,
        name="edge_prepare",
    )(counts, me, point_feats, pos8, wgt, idx, cell, first48)

    d_spectral = call(
        outer_kernel,
        sds((MODES, C, 2 * C), f32),
        grid=(8,),
        in_specs=[whole((2 * MODES, 2 * C))],
        out_specs=lead((MODES // 8, C, 2 * C)),
        scratch_shapes=[pltpu.VMEM((C, 2 * MODES), f32), pltpu.VMEM((2, 2 * MODES, 2 * C), bf16)],
        flops=2 * 10**9,
        vmem=16,
        name="spectral_grad",
    )(spec).reshape(spectral_weight.shape)

    aw, d_spectral = lax.optimization_barrier((aw, d_spectral))
    rows, red = call(
        edge_kernel,
        (pltpu.HBM((CAP, half, BLK, 2 * C), bf16), sds((2 * C, 2 * C), f32)),
        in_specs=[sspec()] + [vspec()] * 4 + [hspec()] * 4 + [vspec()] * 2,
        out_specs=(hspec(), vspec()),
        scratch_shapes=[
            pltpu.VMEM((4 * C, 4 * C), f32),
            pltpu.VMEM((16, 2 * C), f32),
            pltpu.VMEM((half, BLK, 4 * C), bf16),
            pltpu.VMEM((half, BLK, 2 * C), f32),
            pltpu.VMEM((half, 16, 2 * C), bf16),
            pltpu.VMEM((C, C), f32),
            pltpu.VMEM((CAP, half, BLK, 2 * C), bf16),
            pltpu.SemaphoreType.DMA((5,)),
            pltpu.SemaphoreType.DMA((4, half)),
        ],
        vmem=24,
        name="edge_grads",
    )(
        counts,
        grads.reshape(2, half, BLK, 2 * C),
        aw,
        slope,
        off,
        far(aw_late),
        far(slope_late),
        far(off_late),
        far(dmix_part),
        wa,
        wb,
    )

    part = exchange(red.reshape(NN, 16, 2 * C), "narrow")
    part = call(
        sum_kernel,
        sds((NW, 16, 2 * C), f32),
        in_specs=[vspec()],
        out_specs=vspec(),
        vmem=4,
        name="sum_narrow",
    )(part)
    part = exchange(part, "wide")

    d_points = call(
        scatter_kernel,
        sds((C, PDEV), f32),
        grid=(4,),
        in_specs=[
            sspec(),
            pl.BlockSpec((CAP, half // 4, BLK, 2 * C), lambda g: (0, g, 0, 0)),
            whole((NW, CAP, BLK)),
            whole((1, PDEV)),
        ],
        out_specs=whole((C, PDEV)),
        scratch_shapes=[pltpu.VMEM((512, 4 * C), f32)],
        flops=2 * 10**9,
        vmem=32,
        name="point_grads",
    )(counts, far(rows), idx, wgt)

    part, d_points = lax.optimization_barrier((part, d_points))
    part = call(
        sum_kernel,
        sds((NN, 16, 2 * C), f32),
        in_specs=[vspec()],
        out_specs=vspec(),
        vmem=4,
        name="sum_wide",
    )(part)
    part = exchange(part, "narrow")

    d_kernel, d_second, d_mix, d_first, d_bias = call(
        split_kernel,
        (sds((C, C), f32),) * 3 + (sds((3, C), f32), sds((1, C), f32)),
        in_specs=[vspec()],
        out_specs=(vspec(),) * 5,
        vmem=4,
        name="split_sums",
    )(part)
    return (d_points, d_kernel, d_first, d_bias.reshape(C), d_second, d_mix, d_spectral)


def solution(mesh):
    return jax.shard_map(
        local,
        mesh=mesh,
        in_specs=(
            P(None, ("wide", "narrow")),
            P(None, ("wide", "narrow")),
            P(("wide", "narrow")),
            P("wide", "narrow", None, None, None),
            P("wide", "narrow", None, None, None),
            P("wide", "narrow", None),
            P("wide", None, "narrow"),
            P("wide", None, "narrow"),
            P("wide", None, "narrow"),
            P("wide", None, "narrow", None, None),
            P(),
            P(),
            P(),
            P(),
            P(),
        ),
        out_specs=(
            P(None, ("wide", "narrow")),
            P(),
            P(),
            P(),
            P(),
            P(),
            P("wide", None, "narrow", None, None),
        ),
        check_vma=False,
    )
```

```python
import math

import numpy as np
import ml_dtypes
import jax
import jax.numpy as jnp
from jax import lax
from jax.experimental import pallas as pl
from jax.experimental.pallas import tpu as pltpu
from jax.sharding import PartitionSpec as P

C = 64
GZ = 64
MZ = 32
CAP = 2
BLK = 128
XPL = 2
YR = 8
NW = 32
NN = 8
PDEV = 2048
CELLS = XPL * YR * GZ
KZL = MZ // NN
MODES = 32 * KZL

bf16 = jnp.bfloat16
f32 = jnp.float32
root_half = 0.7071067811865476
inv_root_tau = 0.3989422804014327


def hi_lo(table):
    table = np.asarray(table, np.float64)
    high = table.astype(ml_dtypes.bfloat16)
    low = (table - high.astype(np.float64)).astype(ml_dtypes.bfloat16)
    return high, low


def phases(freqs, positions):
    angle = (2.0 * math.pi / 64) * np.mod(np.outer(freqs, positions), 64)
    return np.cos(angle), np.sin(angle)


def make_tables():
    depth_f = np.arange(MZ)
    signed = np.where(np.arange(32) < 16, np.arange(32), np.arange(32) - 32)
    spots = np.arange(64)
    dc, ds = phases(depth_f, spots)
    rc, rs = phases(signed, spots)
    eye_2 = np.eye(2)
    eye_4 = np.eye(4)
    eye_k = np.eye(KZL)
    eye_x = np.eye(XPL)
    dri = np.stack([dc, -ds], 1).reshape(NN, KZL, 2, GZ)
    depth = np.einsum("nkrz,yw->nykrwz", dri, eye_2).reshape(128, 128)
    rot = np.zeros((2, 2, 32, 64))
    rot[0, 0] = rc
    rot[0, 1] = rs
    rot[1, 0] = -rs
    rot[1, 1] = rc
    row = np.einsum("abfy,kl->fkaylb", rot, eye_k).reshape(32 * KZL * 2, 64 * KZL * 2)
    plane = np.einsum("abfx,kl->afkxlb", rot, eye_k).reshape(2 * MODES, 64 * KZL * 2)
    volume = 64.0 * 64.0 * 64.0
    rinv = np.zeros((2, 2, 32, 64))
    rinv[0, 0] = rc
    rinv[0, 1] = -rs
    rinv[1, 0] = rs
    rinv[1, 1] = rc
    plane_inv = np.einsum("abfx,kl->axkbfl", rinv, eye_k).reshape(2 * 256, 2 * MODES) / volume
    both = np.stack([rc, rs], 0).reshape(2, 32, NN, YR)
    row_inv = np.einsum("pfny,xw,kl->nxykpfwl", both, eye_x, eye_k).reshape(512, 512)
    dinv = np.stack([dc, -ds], 0).reshape(2, NN, KZL, GZ)
    depth_inv = np.einsum("rnkz,yw->yzrnwk", dinv, eye_4).reshape(256, 256)
    return [hi_lo(t) for t in (depth, row, plane, plane_inv, row_inv, depth_inv)]


def stack_hi_lo(pair):
    return np.stack(pair, 0)


def dot(a, b, contract=((1,), (0,))):
    return lax.dot_general(a, b, (contract, ((), ())), preferred_element_type=f32)


def split2(values):
    high = values.astype(bf16)
    return high, (values - high.astype(f32)).astype(bf16)


def iota(shape, axis):
    return lax.broadcasted_iota(jnp.int32, shape, axis)


def fiota(shape, axis):
    return iota(shape, axis).astype(f32)


def call(kernel, out_shape, *, vmem=56, flops=10**8, bytes_accessed=4 * 10**6, name=None, **kw):
    return pl.pallas_call(
        kernel,
        out_shape=out_shape,
        name=name,
        compiler_params=pltpu.CompilerParams(vmem_limit_bytes=vmem * 1024 * 1024),
        cost_estimate=pl.CostEstimate(
            flops=flops, bytes_accessed=bytes_accessed, transcendentals=0
        ),
        **kw,
    )


def sds(shape, dtype):
    return jax.ShapeDtypeStruct(shape, dtype)


def depth_kernel(lat_ref, pre_ref, cot_ref, tab_ref, send_ref, grad_ref):
    nt = ((1,), (1,))
    mains = []
    rests = []
    for x in range(XPL):
        pre = pre_ref[x].astype(f32)
        slope = 0.5 * (1.0 + lax.erf(pre * root_half)) + pre * jnp.exp(
            -0.5 * pre * pre
        ) * inv_root_tau
        high, low = split2(cot_ref[x].astype(f32) * slope)
        grad_ref[x] = jnp.concatenate([high, low], axis=0)
        mains += [lat_ref[x], high]
        rests += [jnp.zeros_like(low), low]
    main = jnp.concatenate(mains, axis=0)
    rest = jnp.concatenate(rests, axis=0)
    tables = tab_ref[...].reshape(256, 128)
    for pair in range(YR // 2):
        cols = slice(pair * 128, (pair + 1) * 128)
        out = dot(tables, main[:, cols], nt)
        out = out[:128] + out[128:] + dot(tab_ref[0], rest[:, cols], nt)
        for x in range(XPL):
            block = out[:, x * 2 * C : (x + 1) * 2 * C]
            send_ref[:, x, pair * 16 : (pair + 1) * 16, :] = block.reshape(
                NN, 16, 2 * C
            ).astype(bf16)


def mix_kernel(lat_ref, grad_ref, mix_ref, dmix_ref, mixg_ref):
    dmix = jnp.zeros((C, C), f32)
    mix = mix_ref[...]
    nt = ((1,), (1,))
    for x in range(XPL):
        u = lat_ref[x]
        high = grad_ref[x, :C]
        low = grad_ref[x, C:]
        dmix = dmix + dot(u, high, nt) + dot(u, low, nt)
        mixg_ref[x] = dot(high, mix, ((0,), (1,))) + dot(low, mix, ((0,), (1,)))
    dmix_ref[...] = dmix


def row_kernel(recv_ref, tab_hbm, send_ref, tab_ref, sem):
    copy = pltpu.make_async_copy(tab_hbm, tab_ref, sem)
    copy.start()
    copy.wait()
    parts = []
    for x in range(XPL):
        block = recv_ref[:, x].reshape(512, 2 * C)
        out = dot(tab_ref[0], block) + dot(tab_ref[1], block)
        parts.append(out.reshape(32, 8, 2 * C))
    send_ref[...] = jnp.concatenate(parts, axis=1).astype(bf16)


def mode_kernel(
    recv_ref,
    w_ref,
    tab_hbm,
    inv_hbm,
    cell_hbm,
    spec_ref,
    send_ref,
    x_ref,
    tab_ref,
    inv_ref,
    cell_ref,
    sems,
):
    per = 16
    steps = MODES // per
    copies = [
        pltpu.make_async_copy(source, target, sems.at[k])
        for k, (source, target) in enumerate(
            ((tab_hbm, tab_ref), (inv_hbm, inv_ref), (cell_hbm, cell_ref))
        )
    ]
    for copy in copies:
        copy.start()
    copies[0].wait()
    block = recv_ref[...].reshape(512, 2 * C)
    spec = dot(tab_ref[0], block) + dot(tab_ref[1], block)
    spec_ref[...] = spec
    dr = spec[:MODES, C:]
    di = spec[MODES:, C:]
    x_ref[:MODES, :] = jnp.concatenate([dr, di], axis=1).astype(bf16)
    x_ref[MODES:, :] = jnp.concatenate([di, -dr], axis=1).astype(bf16)
    lane = jnp.bitwise_and(iota((C, 2 * MODES), 1), MODES - 1)
    nt = ((1,), (1,))
    acc = jnp.zeros((C, 2 * MODES), f32)
    for g in range(steps):
        weights = w_ref[g * per * C : (g + 1) * per * C, :]
        res = dot(weights, x_ref[...], nt)
        for j in range(per):
            acc = acc + jnp.where(lane == g * per + j, res[j * C : (j + 1) * C], 0.0)
    high, low = split2(acc)
    copies[1].wait()
    copies[2].wait()
    out = dot(inv_ref[0], high, nt) + dot(inv_ref[1], high, nt) + dot(inv_ref[0], low, nt)
    rows = jnp.concatenate([out[:256], out[256:]], axis=1).reshape(NW, 8, 2 * C)
    cells = cell_ref[...]
    part = iota((NW, 8, BLK), 1)
    cell = jnp.where(part < 2, cells[:, 0:1, :], cells[:, 1:2, :])
    high = jnp.right_shift(cell, 8)
    low = jnp.bitwise_and(cell, 255)
    tail = jnp.where(jnp.bitwise_and(part, 1) == 0, high, low).astype(f32)
    tail = jnp.where(part < 4, tail, 0.0)
    send_ref[...] = jnp.concatenate([rows, tail], axis=1).astype(bf16)


def outer_kernel(spec_ref, out_ref, l_ref, x_ref):
    step = pl.program_id(0)
    per = out_ref.shape[0]

    @pl.when(step == 0)
    def _():
        spec = spec_ref[...]
        l_ref[...] = jnp.transpose(spec)[:C] * (1.0 / 262144.0)
        dr = spec[:MODES, C:]
        di = spec[MODES:, C:]
        first = jnp.concatenate([dr, di], axis=1)
        second = jnp.concatenate([di, -dr], axis=1)
        high, low = split2(jnp.concatenate([first, second], axis=0))
        x_ref[0] = high
        x_ref[1] = low

    ut = l_ref[...]
    lane = jnp.bitwise_and(iota((C, 2 * MODES), 1), MODES - 1)
    rows = [jnp.where(lane == step * per + j, ut, 0.0) for j in range(per)]
    high, low = split2(jnp.concatenate(rows, axis=0))
    out = dot(high, x_ref[0]) + dot(high, x_ref[1]) + dot(low, x_ref[0])
    out_ref[...] = out.reshape(per, C, 2 * C)


def row_inv_kernel(recv_ref, tab_ref, send_ref):
    block = recv_ref[...].astype(f32)[:, :8, :].reshape(256, 2 * C)
    swapped = jnp.concatenate([-block[:, C:], block[:, :C]], axis=1)
    both = jnp.concatenate([block, swapped], axis=0).astype(bf16)
    out = dot(tab_ref[0], both) + dot(tab_ref[1], both)
    send_ref[...] = out.reshape(NN, 64, 2 * C).astype(bf16)


def gather_kernel(recv_ref, mixg_ref, dinv_ref, cell_ref, out_hbm, out_ref, sems):
    quarters = []
    for x in range(XPL):
        for half in range(2):
            start = x * 32 + half * 16
            block = recv_ref[:, start : start + 16, :].reshape(128, 2 * C)
            both = jnp.concatenate([block[:, :C], block[:, C:]], axis=0)
            grad = dot(dinv_ref[0], both) + dot(dinv_ref[1], both)
            quarters.append(grad + mixg_ref[x, half * 256 : (half + 1) * 256, :])
    table = jnp.concatenate(quarters, axis=1).astype(bf16)

    per = 8
    copies = [
        pltpu.make_async_copy(
            out_ref.at[pl.ds(g * per, per)], out_hbm.at[pl.ds(g * per, per)], sems.at[g]
        )
        for g in range(NW // per)
    ]
    rows = per * BLK
    row16 = iota((16, 4 * BLK), 0)
    part16 = jnp.right_shift(iota((16, 4 * BLK), 1), 7)
    sel = jnp.where(row16 == part16 + 8, 1.0, 0.0).astype(bf16)
    low_lane = fiota((rows, 256), 1)
    quarter = jnp.right_shift(iota((rows, 256), 1), 6).astype(f32)
    left = iota((rows, 2 * C), 1) < C
    for g in range(NW // per):
        cells = jnp.concatenate([cell_ref[g * per + j] for j in range(per)], axis=1)
        spread = dot(cells, sel, ((0,), (0,)))
        hots = []
        for s in range(CAP):
            low = spread[:, (2 * s + 1) * BLK : (2 * s + 2) * BLK]
            hots.append(
                jnp.where(jnp.concatenate([low, low], axis=1) == low_lane, 1.0, 0.0).astype(bf16)
            )
        got = dot(jnp.concatenate(hots, axis=0), table)
        found = []
        for s in range(CAP):
            high = spread[:, 2 * s * BLK : (2 * s + 1) * BLK]
            keep = jnp.concatenate([high, high], axis=1) == quarter
            one = jnp.where(keep, got[s * rows : (s + 1) * rows], 0.0)
            one = one[:, : 2 * C] + one[:, 2 * C :]
            found.append(one + pltpu.roll(one, C, 1))
        out = jnp.where(left, found[0], found[1]).astype(bf16)
        out_ref[g * per : (g + 1) * per] = out.reshape(per, BLK, 2 * C)
        copies[g].start()
    for copy in copies:
        copy.wait()


def prep_kernel(
    count_ref,
    me_ref,
    feat_ref,
    pos_ref,
    wgt_ref,
    idx_ref,
    cell_ref,
    first_ref,
    aw_ref,
    slope_ref,
    off_ref,
    aw_late_ref,
    slope_late_ref,
    off_late_ref,
    tab_ref,
):
    weighted = feat_ref[...].astype(f32) * wgt_ref[...]
    pos = pos_ref[...]
    p0 = pos.astype(bf16).astype(f32)
    p1 = (pos - p0).astype(bf16).astype(f32)
    p2 = pos - p0 - p1
    rest = jnp.concatenate([p0, p1, p2, jnp.zeros((40, PDEV), f32)], axis=0)
    tab_ref[0] = jnp.transpose(jnp.concatenate([weighted, rest], axis=0)).astype(bf16)
    tab_ref[1] = jnp.transpose(jnp.concatenate([rest, weighted], axis=0)).astype(bf16)

    point_lane = fiota((BLK, PDEV), 1)
    row8 = iota((8, BLK), 0)
    left = iota((BLK, 2 * C), 1) < C
    sel = jnp.where(row8 == 0, 64.0, jnp.where(row8 == 1, 1.0, 0.0)).astype(bf16)
    half = NW // 2

    def one_hot(idx_row):
        high = jnp.right_shift(idx_row, 6).astype(f32)
        low = jnp.bitwise_and(idx_row, 63).astype(f32)
        packed = jnp.where(row8 == 0, high, jnp.where(row8 == 1, low, 0.0)).astype(bf16)
        spread = dot(packed, sel, ((0,), (0,)))
        spread = jnp.concatenate([spread] * (PDEV // BLK), axis=1)
        return jnp.where(spread == point_lane, 1.0, 0.0).astype(bf16)

    def edge_rows(found_t, cell, target):
        spot = found_t[0:8] + found_t[8:16] + found_t[16:24]
        plane = jnp.right_shift(cell, 9)
        rowy = jnp.bitwise_and(jnp.right_shift(cell, 6), 7)
        depth = jnp.bitwise_and(cell, 63)
        first = ((target * XPL + plane).astype(f32) + 0.5) * (1.0 / 64)
        second = ((me_ref[0] * YR + rowy).astype(f32) + 0.5) * (1.0 / 64)
        third = (depth.astype(f32) + 0.5) * (1.0 / 64)
        centre = jnp.where(row8 == 0, first, jnp.where(row8 == 1, second, third))
        return jnp.where(row8 < 3, centre - spot, jnp.where(row8 == 5, 1.0, 0.0))

    def finish(slot, pair, one, two):
        weighted_pair = jnp.where(left, one, two)
        rows = [
            edge_rows(
                jnp.transpose(one)[C : C + 24], cell_ref[pair, pl.ds(slot, 1), :], pair
            ),
            edge_rows(
                jnp.transpose(two)[:24], cell_ref[pair + half, pl.ds(slot, 1), :], pair + half
            ),
        ]
        edge = jnp.concatenate(rows, axis=0).astype(bf16)
        aw_out = (aw_ref, aw_late_ref)[slot]
        slope_out = (slope_ref, slope_late_ref)[slot]
        off_out = (off_ref, off_late_ref)[slot]
        off_out[pair] = edge
        before = dot(jnp.concatenate([edge, edge, edge], axis=0), first_ref[...], ((0,), (0,)))
        phi = 0.5 * (1.0 + lax.erf(before * root_half))
        aw_out[pair] = jnp.concatenate([before * phi, weighted_pair], axis=1).astype(bf16)
        slope_out[pair] = phi + before * jnp.exp(-0.5 * before * before) * inv_root_tau

    group = 4

    def body(g, carry):
        base = g * group
        found = []
        for side in range(2):
            hot = jnp.concatenate(
                [
                    one_hot(idx_ref[base + j + side * half, pl.ds(0, 1), :])
                    for j in range(group)
                ],
                axis=0,
            )
            found.append(dot(hot, tab_ref[side]))
        for j in range(group):
            rows = slice(j * BLK, (j + 1) * BLK)
            finish(0, base + j, found[0][rows], found[1][rows])
        return carry

    lax.fori_loop(0, half // group, body, 0)

    def second(pair, carry):
        live_one = count_ref[pair] > 1
        live_two = count_ref[pair + half] > 1

        @pl.when(jnp.logical_or(live_one, live_two))
        def _():
            one = dot(one_hot(idx_ref[pair, pl.ds(1, 1), :]), tab_ref[0])
            two = dot(one_hot(idx_ref[pair + half, pl.ds(1, 1), :]), tab_ref[1])
            keep_one = jnp.where(live_one, 1.0, 0.0)
            keep_two = jnp.where(live_two, 1.0, 0.0)
            finish(1, pair, one * keep_one, two * keep_two)

        return carry

    lax.fori_loop(0, half, second, 0)


def edge_kernel(
    count_ref,
    grad_ref,
    aw_ref,
    slope_ref,
    off_ref,
    aw_hbm,
    slope_hbm,
    off_hbm,
    dmix_hbm,
    wa_ref,
    wb_ref,
    out_hbm,
    red_ref,
    pk_ref,
    pf_ref,
    aw_late,
    slope_late,
    off_late,
    dmix_ref,
    rows_ref,
    out_sems,
    late_sems,
):
    half = NW // 2
    per = 4
    groups = half // per

    dmix_copy = pltpu.make_async_copy(dmix_hbm, dmix_ref, out_sems.at[groups])

    def late_copies(pair):
        return [
            pltpu.make_async_copy(aw_hbm.at[pair], aw_late.at[pair], late_sems.at[0, pair]),
            pltpu.make_async_copy(
                slope_hbm.at[pair], slope_late.at[pair], late_sems.at[1, pair]
            ),
            pltpu.make_async_copy(off_hbm.at[pair], off_late.at[pair], late_sems.at[3, pair]),
        ]

    def late_out(pair):
        return pltpu.make_async_copy(
            rows_ref.at[1, pair], out_hbm.at[1, pair], late_sems.at[2, pair]
        )

    def each_live(step):
        def body(pair, carry):
            @pl.when(jnp.logical_or(count_ref[pair] > 1, count_ref[pair + half] > 1))
            def _():
                step(pair)

            return carry

        lax.fori_loop(0, half, body, 0)

    out_copies = [
        pltpu.make_async_copy(
            rows_ref.at[0, pl.ds(g * per, per)],
            out_hbm.at[0, pl.ds(g * per, per)],
            out_sems.at[g],
        )
        for g in range(groups)
    ]

    dmix_copy.start()

    def begin(pair):
        for copy in late_copies(pair):
            copy.start()

    each_live(begin)

    pk_ref[...] = jnp.zeros_like(pk_ref)
    pf_ref[...] = jnp.zeros_like(pf_ref)

    def work(first, count, slot):
        rows = count * BLK
        left = iota((rows, 2 * C), 1) < C
        one = grad_ref[0, pl.ds(first, count)].reshape(rows, 2 * C).astype(f32)
        two = grad_ref[1, pl.ds(first, count)].reshape(rows, 2 * C).astype(f32)
        if slot == 0:
            grads = jnp.where(left, one, pltpu.roll(two, C, 1))
        else:
            grads = jnp.where(left, pltpu.roll(one, C, 1), two)
        aw_in, slope_in, off_in = (
            (aw_ref, slope_ref, off_ref),
            (aw_late, slope_late, off_late),
        )[slot]
        actwgt = aw_in[pl.ds(first, count)].reshape(rows, 4 * C)
        kl = dot(actwgt, wa_ref[...])
        gated = (grads * kl[:, : 2 * C]).astype(bf16)
        dkval = (grads * kl[:, 2 * C :]).astype(bf16)
        gk = jnp.concatenate([gated, dkval], axis=1)
        back = dot(gk, wb_ref[...])
        rows_ref[slot, pl.ds(first, count)] = (
            back[:, : 2 * C].reshape(count, BLK, 2 * C).astype(bf16)
        )
        slope = slope_in[pl.ds(first, count)].reshape(rows, 2 * C)
        dbefore = back[:, 2 * C :] * slope
        pk_ref[...] += dot(actwgt, gk, ((0,), (0,)))
        high, low = split2(dbefore)
        edges = jnp.concatenate([off_in[first + j] for j in range(count)], axis=1)
        pf_ref[...] += dot(edges, high) + dot(edges, low)

    for g in range(groups):
        work(g * per, per, 0)
        out_copies[g].start()

    def second(pair):
        for copy in late_copies(pair):
            copy.wait()
        work(pair, 1, 1)
        late_out(pair).start()

    each_live(second)
    dmix_copy.wait()

    pk = pk_ref[...]
    pf = pf_ref[...]
    second_sum = pk[:C, 2 * C : 3 * C] + pk[C : 2 * C, 3 * C :]
    kernel_sum = pk[2 * C : 3 * C, :C] + pk[3 * C :, C : 2 * C]
    first_sum = pf[:8, :C] + pf[8:, C:]
    low_rows = jnp.concatenate([first_sum, jnp.zeros((C - 8, C), f32)], axis=0)
    red_ref[:C, :] = jnp.concatenate([kernel_sum, second_sum], axis=1)
    red_ref[C:, :] = jnp.concatenate([dmix_ref[...], low_rows], axis=1)
    for copy in out_copies:
        copy.wait()
    each_live(lambda pair: late_out(pair).wait())


def scatter_kernel(count_ref, rows_ref, idx_ref, wgt_ref, out_ref, acc_ref):
    step = pl.program_id(0)
    per = rows_ref.shape[1]
    half = NW // 2

    @pl.when(step == 0)
    def _():
        acc_ref[...] = jnp.zeros_like(acc_ref)

    low_row = iota((512, BLK), 0)
    row8 = iota((8, BLK), 0)
    ones = jnp.where(row8 == 0, 1.0, 0.0).astype(bf16)

    def add(targets, slot, values, count):
        hots = []
        tops = []
        for target in targets:
            idx = idx_ref[target, pl.ds(slot, 1), :]
            low = jnp.bitwise_and(idx, 511)
            hots.append(jnp.where(low_row == low, 1.0, 0.0).astype(bf16))
            top = jnp.right_shift(idx, 9).astype(f32)
            tops.append(jnp.where(row8 == 0, top, 0.0).astype(bf16))
        spread = dot(jnp.concatenate(tops, axis=1), ones, ((0,), (0,)))
        right = iota((count * BLK, 2 * C), 1) >= C
        quarter = jnp.where(right, 1.0, 0.0)
        first = jnp.where(spread == quarter, values, 0.0)
        second = jnp.where(spread == quarter + 2.0, values, 0.0)
        both = jnp.concatenate([first, second], axis=1).astype(bf16)
        acc_ref[...] += dot(jnp.concatenate(hots, axis=1), both)

    def doubled(values, side):
        left = iota(values.shape, 1) < C
        turned = pltpu.roll(values, C, 1)
        if side == 0:
            return jnp.where(left, values, turned)
        return jnp.where(left, turned, values)

    rows = rows_ref[0].reshape(per * BLK, 2 * C).astype(f32)
    for side in range(2):
        targets = [step * per + j + side * half for j in range(per)]
        add(targets, 0, doubled(rows, side), per)
    for j in range(per):
        for side in range(2):
            target = step * per + j + side * half

            @pl.when(count_ref[target] > 1)
            def _():
                add([target], 1, doubled(rows_ref[1, j].astype(f32), side), 1)

    @pl.when(step == pl.num_programs(0) - 1)
    def _():
        for pair in range(2):
            part = jnp.transpose(acc_ref[:, pair * 2 * C : (pair + 1) * 2 * C])
            for one in range(2):
                start = (2 * pair + one) * 512
                out_ref[:, start : start + 512] = (
                    part[one * C : (one + 1) * C] * wgt_ref[:, start : start + 512]
                )


def sum_kernel(in_ref, out_ref):
    total = in_ref[0]
    for j in range(1, in_ref.shape[0]):
        total = total + in_ref[j]
    out_ref[...] = jnp.broadcast_to(total[None], out_ref.shape)


def split_kernel(in_ref, kernel_ref, second_ref, mix_ref, first_ref, bias_ref):
    total = in_ref[...].reshape(2 * C, 2 * C)
    kernel_ref[...] = total[:C, :C]
    second_ref[...] = total[:C, C:]
    mix_ref[...] = total[C:, :C]
    first_ref[...] = total[C : C + 3, C:]
    bias_ref[...] = total[C + 5 : C + 6, C:]


def exchange(block, axis):
    return lax.all_to_all(block, axis, split_axis=0, concat_axis=0, tiled=True)


def exchange_near(block):
    groups = [[16 * k + j for j in range(16)] for k in range(16)]
    return grouped(block, groups)


def exchange_far(block):
    groups = [[16 * k + j for k in range(16)] for j in range(16)]
    return grouped(block, groups)


def grouped(block, groups):
    return lax.all_to_all(
        block,
        ("wide", "narrow"),
        split_axis=0,
        concat_axis=0,
        tiled=True,
        axis_index_groups=groups,
    )


def vspec():
    return pl.BlockSpec(memory_space=pltpu.VMEM)


def hspec():
    return pl.BlockSpec(memory_space=pltpu.HBM)


def far(array):
    return pltpu.with_memory_space_constraint(array, pltpu.HBM)


def sspec():
    return pl.BlockSpec(memory_space=pltpu.SMEM)


def whole(shape):
    return pl.BlockSpec(shape, lambda g: (0,) * len(shape))


def lead(shape):
    return pl.BlockSpec(shape, lambda g: (g,) + (0,) * (len(shape) - 1))


def split3(values):
    a = lax.reduce_precision(values, 8, 7)
    b = lax.reduce_precision(values - a, 8, 7)
    c = values - a - b
    return [part.astype(bf16) for part in (a, b, c)]


def local(
    point_feats,
    point_pos,
    point_weight,
    nbr_point,
    nbr_cell,
    block_count,
    latent,
    preact,
    cotangent,
    spectral_weight,
    kernel_mat,
    first_weight,
    first_bias,
    second_weight,
    mix_weight,
):
    depth_t, row_t, plane_t, plane_inv_t, row_inv_t, depth_inv_t = [
        jnp.asarray(stack_hi_lo(pair)) for pair in make_tables()
    ]
    me = lax.axis_index("narrow").astype(jnp.int32).reshape(1)
    counts = block_count.reshape(NW)
    idx = nbr_point.reshape(NW, CAP, BLK)
    cell = nbr_cell.reshape(NW, CAP, BLK)
    wgt = point_weight.reshape(1, PDEV)
    pos8 = jnp.concatenate([point_pos, jnp.zeros((5, PDEV), f32)], axis=0)

    zero = jnp.zeros((C, C), bf16)
    sec = second_weight
    ker = kernel_mat
    wa = jnp.block(
        [
            [sec, zero, zero, zero],
            [zero, sec, zero, zero],
            [zero, zero, ker, zero],
            [zero, zero, zero, ker],
        ]
    )
    kt = ker.T
    st = sec.T
    wb = jnp.block(
        [
            [kt, zero, zero, zero],
            [zero, kt, zero, zero],
            [zero, zero, st, zero],
            [zero, zero, zero, st],
        ]
    )
    z2 = jnp.zeros((2, C), f32)
    half = jnp.concatenate([first_weight, z2, first_bias[None], z2], axis=0)
    zh = jnp.zeros((8, C), f32)
    first_full = jnp.concatenate(
        [jnp.concatenate([half, zh], axis=1), jnp.concatenate([zh, half], axis=1)], axis=0
    )
    first48 = jnp.concatenate(split3(first_full), axis=0)

    send1, grad_parts = call(
        depth_kernel,
        (sds((NN, XPL, 64, 2 * C), bf16), sds((XPL, 2 * C, 512), bf16)),
        in_specs=[vspec()] * 4,
        out_specs=(vspec(),) * 2,
        name="depth_forward",
    )(latent, preact, cotangent, depth_t)
    send1, weights = lax.optimization_barrier(
        (send1, spectral_weight.reshape(MODES * C, 2 * C))
    )
    recv1 = exchange(send1, "narrow")
    weights = weights.astype(bf16)
    dmix_part, mixg = call(
        mix_kernel,
        (sds((C, C), f32), sds((XPL, 512, C), f32)),
        in_specs=[vspec()] * 3,
        out_specs=(vspec(),) * 2,
        vmem=8,
        name="pointwise_mix",
    )(latent, grad_parts, mix_weight)
    recv1, mixg, weights = lax.optimization_barrier((recv1, mixg, weights))

    send2 = call(
        row_kernel,
        sds((NW, 16, 2 * C), bf16),
        in_specs=[vspec(), hspec()],
        out_specs=vspec(),
        scratch_shapes=[pltpu.VMEM(row_t.shape, bf16), pltpu.SemaphoreType.DMA],
        vmem=4,
        name="row_forward",
    )(recv1, far(row_t))
    recv2 = exchange(send2, "wide")
    spec, send3 = call(
        mode_kernel,
        (sds((2 * MODES, 2 * C), f32), sds((NW, 16, 2 * C), bf16)),
        in_specs=[vspec()] * 2 + [hspec()] * 3,
        out_specs=(vspec(),) * 2,
        scratch_shapes=[
            pltpu.VMEM((2 * MODES, 2 * C), bf16),
            pltpu.VMEM(plane_t.shape, bf16),
            pltpu.VMEM(plane_inv_t.shape, bf16),
            pltpu.VMEM(cell.shape, jnp.int32),
            pltpu.SemaphoreType.DMA((3,)),
        ],
        vmem=12,
        name="mode_mix",
    )(recv2, weights, far(plane_t), far(plane_inv_t), far(cell))
    recv3 = exchange(send3, "wide")

    send4 = call(
        row_inv_kernel,
        sds((NN, 64, 2 * C), bf16),
        in_specs=[vspec()] * 2,
        out_specs=vspec(),
        vmem=8,
        name="row_inverse",
    )(recv3, row_inv_t)
    recv4 = exchange(send4, "narrow")

    found = call(
        gather_kernel,
        pltpu.HBM((NW, BLK, 2 * C), bf16),
        in_specs=[vspec()] * 4,
        out_specs=hspec(),
        scratch_shapes=[
            pltpu.VMEM((NW, BLK, 2 * C), bf16),
            pltpu.SemaphoreType.DMA((4,)),
        ],
        vmem=20,
        name="cell_gather",
    )(recv4, mixg, depth_inv_t, recv3)

    found, idx, spec = lax.optimization_barrier((found, idx, spec))
    grads = exchange(found, "wide")

    half = NW // 2
    aw, slope, off, aw_late, slope_late, off_late = call(
        prep_kernel,
        (
            sds((half, BLK, 4 * C), bf16),
            sds((half, BLK, 2 * C), f32),
            sds((half, 16, 2 * C), bf16),
            pltpu.HBM((half, BLK, 4 * C), bf16),
            pltpu.HBM((half, BLK, 2 * C), f32),
            pltpu.HBM((half, 16, 2 * C), bf16),
        ),
        in_specs=[sspec(), sspec()] + [vspec()] * 6,
        out_specs=(vspec(),) * 6,
        scratch_shapes=[pltpu.VMEM((2, PDEV, 2 * C), bf16)],
        flops=2 * 10**9,
        bytes_accessed=2 * 10**7,
        vmem=32,
        name="edge_prepare",
    )(counts, me, point_feats, pos8, wgt, idx, cell, first48)

    d_spectral = call(
        outer_kernel,
        sds((MODES, C, 2 * C), f32),
        grid=(8,),
        in_specs=[whole((2 * MODES, 2 * C))],
        out_specs=lead((MODES // 8, C, 2 * C)),
        scratch_shapes=[pltpu.VMEM((C, 2 * MODES), f32), pltpu.VMEM((2, 2 * MODES, 2 * C), bf16)],
        flops=2 * 10**9,
        vmem=16,
        name="spectral_grad",
    )(spec).reshape(spectral_weight.shape)

    aw, d_spectral = lax.optimization_barrier((aw, d_spectral))
    rows, red = call(
        edge_kernel,
        (pltpu.HBM((CAP, half, BLK, 2 * C), bf16), sds((2 * C, 2 * C), f32)),
        in_specs=[sspec()] + [vspec()] * 4 + [hspec()] * 4 + [vspec()] * 2,
        out_specs=(hspec(), vspec()),
        scratch_shapes=[
            pltpu.VMEM((4 * C, 4 * C), f32),
            pltpu.VMEM((16, 2 * C), f32),
            pltpu.VMEM((half, BLK, 4 * C), bf16),
            pltpu.VMEM((half, BLK, 2 * C), f32),
            pltpu.VMEM((half, 16, 2 * C), bf16),
            pltpu.VMEM((C, C), f32),
            pltpu.VMEM((CAP, half, BLK, 2 * C), bf16),
            pltpu.SemaphoreType.DMA((5,)),
            pltpu.SemaphoreType.DMA((4, half)),
        ],
        vmem=24,
        name="edge_grads",
    )(
        counts,
        grads.reshape(2, half, BLK, 2 * C),
        aw,
        slope,
        off,
        far(aw_late),
        far(slope_late),
        far(off_late),
        far(dmix_part),
        wa,
        wb,
    )

    part = exchange_near(red.reshape(16, 8, 2 * C))
    part = call(
        sum_kernel,
        sds((16, 8, 2 * C), f32),
        in_specs=[vspec()],
        out_specs=vspec(),
        vmem=4,
        name="sum_near",
    )(part)
    part = exchange_far(part)

    d_points = call(
        scatter_kernel,
        sds((C, PDEV), f32),
        grid=(4,),
        in_specs=[
            sspec(),
            pl.BlockSpec((CAP, half // 4, BLK, 2 * C), lambda g: (0, g, 0, 0)),
            whole((NW, CAP, BLK)),
            whole((1, PDEV)),
        ],
        out_specs=whole((C, PDEV)),
        scratch_shapes=[pltpu.VMEM((512, 4 * C), f32)],
        flops=2 * 10**9,
        vmem=32,
        name="point_grads",
    )(counts, far(rows), idx, wgt)

    part, d_points = lax.optimization_barrier((part, d_points))
    part = call(
        sum_kernel,
        sds((16, 8, 2 * C), f32),
        in_specs=[vspec()],
        out_specs=vspec(),
        vmem=4,
        name="sum_far",
    )(part)
    part = exchange_near(part)

    d_kernel, d_second, d_mix, d_first, d_bias = call(
        split_kernel,
        (sds((C, C), f32),) * 3 + (sds((3, C), f32), sds((1, C), f32)),
        in_specs=[vspec()],
        out_specs=(vspec(),) * 5,
        vmem=4,
        name="split_sums",
    )(part)
    return (d_points, d_kernel, d_first, d_bias.reshape(C), d_second, d_mix, d_spectral)


def solution(mesh):
    return jax.shard_map(
        local,
        mesh=mesh,
        in_specs=(
            P(None, ("wide", "narrow")),
            P(None, ("wide", "narrow")),
            P(("wide", "narrow")),
            P("wide", "narrow", None, None, None),
            P("wide", "narrow", None, None, None),
            P("wide", "narrow", None),
            P("wide", None, "narrow"),
            P("wide", None, "narrow"),
            P("wide", None, "narrow"),
            P("wide", None, "narrow", None, None),
            P(),
            P(),
            P(),
            P(),
            P(),
        ),
        out_specs=(
            P(None, ("wide", "narrow")),
            P(),
            P(),
            P(),
            P(),
            P(),
            P("wide", None, "narrow", None, None),
        ),
        check_vma=False,
    )
```

```python
import math

import numpy as np
import ml_dtypes
import jax
import jax.numpy as jnp
from jax import lax
from jax.experimental import pallas as pl
from jax.experimental.pallas import tpu as pltpu
from jax.sharding import PartitionSpec as P

C = 64
GZ = 64
MZ = 32
CAP = 2
BLK = 128
XPL = 2
YR = 8
NW = 32
NN = 8
PDEV = 2048
CELLS = XPL * YR * GZ
KZL = MZ // NN
MODES = 32 * KZL

bf16 = jnp.bfloat16
f32 = jnp.float32
root_half = 0.7071067811865476
inv_root_tau = 0.3989422804014327


def hi_lo(table):
    table = np.asarray(table, np.float64)
    high = table.astype(ml_dtypes.bfloat16)
    low = (table - high.astype(np.float64)).astype(ml_dtypes.bfloat16)
    return high, low


def phases(freqs, positions):
    angle = (2.0 * math.pi / 64) * np.mod(np.outer(freqs, positions), 64)
    return np.cos(angle), np.sin(angle)


def make_tables():
    depth_f = np.arange(MZ)
    signed = np.where(np.arange(32) < 16, np.arange(32), np.arange(32) - 32)
    spots = np.arange(64)
    dc, ds = phases(depth_f, spots)
    rc, rs = phases(signed, spots)
    eye_2 = np.eye(2)
    eye_4 = np.eye(4)
    eye_k = np.eye(KZL)
    eye_x = np.eye(XPL)
    dri = np.stack([dc, -ds], 1).reshape(NN, KZL, 2, GZ)
    depth = np.einsum("nkrz,yw->nykrwz", dri, eye_2).reshape(128, 128)
    rot = np.zeros((2, 2, 32, 64))
    rot[0, 0] = rc
    rot[0, 1] = rs
    rot[1, 0] = -rs
    rot[1, 1] = rc
    row = np.einsum("abfy,kl->fkaylb", rot, eye_k).reshape(32 * KZL * 2, 64 * KZL * 2)
    plane = np.einsum("abfx,kl->afkxlb", rot, eye_k).reshape(2 * MODES, 64 * KZL * 2)
    volume = 64.0 * 64.0 * 64.0
    rinv = np.zeros((2, 2, 32, 64))
    rinv[0, 0] = rc
    rinv[0, 1] = -rs
    rinv[1, 0] = rs
    rinv[1, 1] = rc
    plane_inv = np.einsum("abfx,kl->axkbfl", rinv, eye_k).reshape(2 * 256, 2 * MODES) / volume
    both = np.stack([rc, rs], 0).reshape(2, 32, NN, YR)
    row_inv = np.einsum("pfny,xw,kl->nxykpfwl", both, eye_x, eye_k).reshape(512, 512)
    dinv = np.stack([dc, -ds], 0).reshape(2, NN, KZL, GZ)
    depth_inv = np.einsum("rnkz,yw->yzrnwk", dinv, eye_4).reshape(256, 256)
    return [hi_lo(t) for t in (depth, row, plane, plane_inv, row_inv, depth_inv)]


def stack_hi_lo(pair):
    return np.stack(pair, 0)


def dot(a, b, contract=((1,), (0,))):
    return lax.dot_general(a, b, (contract, ((), ())), preferred_element_type=f32)


def split2(values):
    high = values.astype(bf16)
    return high, (values - high.astype(f32)).astype(bf16)


def iota(shape, axis):
    return lax.broadcasted_iota(jnp.int32, shape, axis)


def fiota(shape, axis):
    return iota(shape, axis).astype(f32)


def call(kernel, out_shape, *, vmem=56, flops=10**8, bytes_accessed=4 * 10**6, name=None, **kw):
    return pl.pallas_call(
        kernel,
        out_shape=out_shape,
        name=name,
        compiler_params=pltpu.CompilerParams(vmem_limit_bytes=vmem * 1024 * 1024),
        cost_estimate=pl.CostEstimate(
            flops=flops, bytes_accessed=bytes_accessed, transcendentals=0
        ),
        **kw,
    )


def sds(shape, dtype):
    return jax.ShapeDtypeStruct(shape, dtype)


def depth_kernel(lat_ref, pre_ref, cot_ref, tab_ref, send_ref, grad_ref):
    nt = ((1,), (1,))
    mains = []
    rests = []
    for x in range(XPL):
        pre = pre_ref[x].astype(f32)
        slope = 0.5 * (1.0 + lax.erf(pre * root_half)) + pre * jnp.exp(
            -0.5 * pre * pre
        ) * inv_root_tau
        high, low = split2(cot_ref[x].astype(f32) * slope)
        grad_ref[x] = jnp.concatenate([high, low], axis=0)
        mains += [lat_ref[x], high]
        rests += [jnp.zeros_like(low), low]
    main = jnp.concatenate(mains, axis=0)
    rest = jnp.concatenate(rests, axis=0)
    tables = tab_ref[...].reshape(256, 128)
    for pair in range(YR // 2):
        cols = slice(pair * 128, (pair + 1) * 128)
        out = dot(tables, main[:, cols], nt)
        out = out[:128] + out[128:] + dot(tab_ref[0], rest[:, cols], nt)
        for x in range(XPL):
            block = out[:, x * 2 * C : (x + 1) * 2 * C]
            send_ref[:, x, pair * 16 : (pair + 1) * 16, :] = block.reshape(
                NN, 16, 2 * C
            ).astype(bf16)


def mix_kernel(lat_ref, grad_ref, mix_ref, dmix_ref, mixg_ref):
    dmix = jnp.zeros((C, C), f32)
    mix = mix_ref[...]
    nt = ((1,), (1,))
    for x in range(XPL):
        u = lat_ref[x]
        high = grad_ref[x, :C]
        low = grad_ref[x, C:]
        dmix = dmix + dot(u, high, nt) + dot(u, low, nt)
        mixg_ref[x] = dot(high, mix, ((0,), (1,))) + dot(low, mix, ((0,), (1,)))
    dmix_ref[...] = dmix


def row_kernel(recv_ref, tab_hbm, send_ref, tab_ref, sems):
    copies = [
        pltpu.make_async_copy(tab_hbm.at[k], tab_ref.at[k], sems.at[k]) for k in range(2)
    ]
    for copy in copies:
        copy.start()
    blocks = [recv_ref[:, x].reshape(512, 2 * C) for x in range(XPL)]
    block = jnp.concatenate(blocks, axis=1)
    copies[0].wait()
    out = dot(tab_ref[0], block)
    copies[1].wait()
    out = out + dot(tab_ref[1], block)
    parts = [out[:, x * 2 * C : (x + 1) * 2 * C].reshape(32, 8, 2 * C) for x in range(XPL)]
    send_ref[...] = jnp.concatenate(parts, axis=1).astype(bf16)


def mode_kernel(
    recv_ref,
    w_ref,
    tab_hbm,
    inv_hbm,
    cell_hbm,
    spec_ref,
    send_ref,
    x_ref,
    tab_ref,
    inv_ref,
    cell_ref,
    sems,
):
    per = 16
    steps = MODES // per
    copies = [
        pltpu.make_async_copy(source, target, sems.at[k])
        for k, (source, target) in enumerate(
            (
                (tab_hbm.at[0], tab_ref.at[0]),
                (tab_hbm.at[1], tab_ref.at[1]),
                (inv_hbm, inv_ref),
                (cell_hbm, cell_ref),
            )
        )
    ]
    for copy in copies:
        copy.start()
    block = recv_ref[...].reshape(512, 2 * C)
    copies[0].wait()
    spec = dot(tab_ref[0], block)
    copies[1].wait()
    spec = spec + dot(tab_ref[1], block)
    spec_ref[...] = spec
    dr = spec[:MODES, C:]
    di = spec[MODES:, C:]
    x_ref[:MODES, :] = jnp.concatenate([dr, di], axis=1).astype(bf16)
    x_ref[MODES:, :] = jnp.concatenate([di, -dr], axis=1).astype(bf16)
    lane = jnp.bitwise_and(iota((C, 2 * MODES), 1), MODES - 1)
    nt = ((1,), (1,))
    acc = jnp.zeros((C, 2 * MODES), f32)
    for g in range(steps):
        weights = w_ref[g * per * C : (g + 1) * per * C, :]
        res = dot(weights, x_ref[...], nt)
        for j in range(per):
            acc = acc + jnp.where(lane == g * per + j, res[j * C : (j + 1) * C], 0.0)
    high, low = split2(acc)
    copies[2].wait()
    copies[3].wait()
    out = dot(inv_ref[0], high, nt) + dot(inv_ref[1], high, nt) + dot(inv_ref[0], low, nt)
    rows = jnp.concatenate([out[:256], out[256:]], axis=1).reshape(NW, 8, 2 * C)
    cells = cell_ref[...]
    part = iota((NW, 8, BLK), 1)
    cell = jnp.where(part < 2, cells[:, 0:1, :], cells[:, 1:2, :])
    high = jnp.right_shift(cell, 8)
    low = jnp.bitwise_and(cell, 255)
    tail = jnp.where(jnp.bitwise_and(part, 1) == 0, high, low).astype(f32)
    tail = jnp.where(part < 4, tail, 0.0)
    send_ref[...] = jnp.concatenate([rows, tail], axis=1).astype(bf16)


def outer_kernel(spec_ref, out_ref, l_ref, x_ref):
    step = pl.program_id(0)
    per = out_ref.shape[0]

    @pl.when(step == 0)
    def _():
        spec = spec_ref[...]
        l_ref[...] = jnp.transpose(spec)[:C] * (1.0 / 262144.0)
        dr = spec[:MODES, C:]
        di = spec[MODES:, C:]
        first = jnp.concatenate([dr, di], axis=1)
        second = jnp.concatenate([di, -dr], axis=1)
        high, low = split2(jnp.concatenate([first, second], axis=0))
        x_ref[0] = high
        x_ref[1] = low

    ut = l_ref[...]
    lane = jnp.bitwise_and(iota((C, 2 * MODES), 1), MODES - 1)
    rows = [jnp.where(lane == step * per + j, ut, 0.0) for j in range(per)]
    high, low = split2(jnp.concatenate(rows, axis=0))
    out = dot(high, x_ref[0]) + dot(high, x_ref[1]) + dot(low, x_ref[0])
    out_ref[...] = out.reshape(per, C, 2 * C)


def row_inv_kernel(recv_ref, tab_ref, send_ref):
    block = recv_ref[...].astype(f32)[:, :8, :].reshape(256, 2 * C)
    swapped = jnp.concatenate([-block[:, C:], block[:, :C]], axis=1)
    both = jnp.concatenate([block, swapped], axis=0).astype(bf16)
    out = dot(tab_ref[0], both) + dot(tab_ref[1], both)
    send_ref[...] = out.reshape(NN, 64, 2 * C).astype(bf16)


def gather_kernel(recv_ref, mixg_ref, dinv_ref, cell_ref, out_hbm, out_ref, sems):
    quarters = []
    for x in range(XPL):
        for half in range(2):
            start = x * 32 + half * 16
            block = recv_ref[:, start : start + 16, :].reshape(128, 2 * C)
            both = jnp.concatenate([block[:, :C], block[:, C:]], axis=0)
            grad = dot(dinv_ref[0], both) + dot(dinv_ref[1], both)
            quarters.append(grad + mixg_ref[x, half * 256 : (half + 1) * 256, :])
    table = jnp.concatenate(quarters, axis=1).astype(bf16)

    per = 8
    copies = [
        pltpu.make_async_copy(
            out_ref.at[pl.ds(g * per, per)], out_hbm.at[pl.ds(g * per, per)], sems.at[g]
        )
        for g in range(NW // per)
    ]
    rows = per * BLK
    row16 = iota((16, 4 * BLK), 0)
    part16 = jnp.right_shift(iota((16, 4 * BLK), 1), 7)
    sel = jnp.where(row16 == part16 + 8, 1.0, 0.0).astype(bf16)
    low_lane = fiota((rows, 256), 1)
    quarter = jnp.right_shift(iota((rows, 256), 1), 6).astype(f32)
    left = iota((rows, 2 * C), 1) < C
    for g in range(NW // per):
        cells = jnp.concatenate([cell_ref[g * per + j] for j in range(per)], axis=1)
        spread = dot(cells, sel, ((0,), (0,)))
        hots = []
        for s in range(CAP):
            low = spread[:, (2 * s + 1) * BLK : (2 * s + 2) * BLK]
            hots.append(
                jnp.where(jnp.concatenate([low, low], axis=1) == low_lane, 1.0, 0.0).astype(bf16)
            )
        got = dot(jnp.concatenate(hots, axis=0), table)
        found = []
        for s in range(CAP):
            high = spread[:, 2 * s * BLK : (2 * s + 1) * BLK]
            keep = jnp.concatenate([high, high], axis=1) == quarter
            one = jnp.where(keep, got[s * rows : (s + 1) * rows], 0.0)
            one = one[:, : 2 * C] + one[:, 2 * C :]
            found.append(one + pltpu.roll(one, C, 1))
        out = jnp.where(left, found[0], found[1]).astype(bf16)
        out_ref[g * per : (g + 1) * per] = out.reshape(per, BLK, 2 * C)
        copies[g].start()
    for copy in copies:
        copy.wait()


def prep_kernel(
    count_ref,
    me_ref,
    feat_ref,
    pos_ref,
    wgt_ref,
    idx_ref,
    cell_ref,
    first_ref,
    aw_ref,
    slope_ref,
    off_ref,
    aw_late_ref,
    slope_late_ref,
    off_late_ref,
    tab_ref,
):
    weighted = feat_ref[...].astype(f32) * wgt_ref[...]
    pos = pos_ref[...]
    p0 = pos.astype(bf16).astype(f32)
    p1 = (pos - p0).astype(bf16).astype(f32)
    p2 = pos - p0 - p1
    rest = jnp.concatenate([p0, p1, p2, jnp.zeros((40, PDEV), f32)], axis=0)
    tab_ref[0] = jnp.transpose(jnp.concatenate([weighted, rest], axis=0)).astype(bf16)
    tab_ref[1] = jnp.transpose(jnp.concatenate([rest, weighted], axis=0)).astype(bf16)

    point_lane = fiota((BLK, PDEV), 1)
    row8 = iota((8, BLK), 0)
    left = iota((BLK, 2 * C), 1) < C
    sel = jnp.where(row8 == 0, 64.0, jnp.where(row8 == 1, 1.0, 0.0)).astype(bf16)
    half = NW // 2

    def one_hot(idx_row):
        high = jnp.right_shift(idx_row, 6).astype(f32)
        low = jnp.bitwise_and(idx_row, 63).astype(f32)
        packed = jnp.where(row8 == 0, high, jnp.where(row8 == 1, low, 0.0)).astype(bf16)
        spread = dot(packed, sel, ((0,), (0,)))
        spread = jnp.concatenate([spread] * (PDEV // BLK), axis=1)
        return jnp.where(spread == point_lane, 1.0, 0.0).astype(bf16)

    def edge_rows(found_t, cell, target):
        spot = found_t[0:8] + found_t[8:16] + found_t[16:24]
        plane = jnp.right_shift(cell, 9)
        rowy = jnp.bitwise_and(jnp.right_shift(cell, 6), 7)
        depth = jnp.bitwise_and(cell, 63)
        first = ((target * XPL + plane).astype(f32) + 0.5) * (1.0 / 64)
        second = ((me_ref[0] * YR + rowy).astype(f32) + 0.5) * (1.0 / 64)
        third = (depth.astype(f32) + 0.5) * (1.0 / 64)
        centre = jnp.where(row8 == 0, first, jnp.where(row8 == 1, second, third))
        return jnp.where(row8 < 3, centre - spot, jnp.where(row8 == 5, 1.0, 0.0))

    def finish(slot, pair, one, two):
        weighted_pair = jnp.where(left, one, two)
        rows = [
            edge_rows(
                jnp.transpose(one)[C : C + 24], cell_ref[pair, pl.ds(slot, 1), :], pair
            ),
            edge_rows(
                jnp.transpose(two)[:24], cell_ref[pair + half, pl.ds(slot, 1), :], pair + half
            ),
        ]
        edge = jnp.concatenate(rows, axis=0).astype(bf16)
        aw_out = (aw_ref, aw_late_ref)[slot]
        slope_out = (slope_ref, slope_late_ref)[slot]
        off_out = (off_ref, off_late_ref)[slot]
        off_out[pair] = edge
        before = dot(jnp.concatenate([edge, edge, edge], axis=0), first_ref[...], ((0,), (0,)))
        phi = 0.5 * (1.0 + lax.erf(before * root_half))
        aw_out[pair] = jnp.concatenate([before * phi, weighted_pair], axis=1).astype(bf16)
        slope_out[pair] = phi + before * jnp.exp(-0.5 * before * before) * inv_root_tau

    group = 4

    def body(g, carry):
        base = g * group
        found = []
        for side in range(2):
            hot = jnp.concatenate(
                [
                    one_hot(idx_ref[base + j + side * half, pl.ds(0, 1), :])
                    for j in range(group)
                ],
                axis=0,
            )
            found.append(dot(hot, tab_ref[side]))
        for j in range(group):
            rows = slice(j * BLK, (j + 1) * BLK)
            finish(0, base + j, found[0][rows], found[1][rows])
        return carry

    lax.fori_loop(0, half // group, body, 0)

    def second(pair, carry):
        live_one = count_ref[pair] > 1
        live_two = count_ref[pair + half] > 1

        @pl.when(jnp.logical_or(live_one, live_two))
        def _():
            one = dot(one_hot(idx_ref[pair, pl.ds(1, 1), :]), tab_ref[0])
            two = dot(one_hot(idx_ref[pair + half, pl.ds(1, 1), :]), tab_ref[1])
            keep_one = jnp.where(live_one, 1.0, 0.0)
            keep_two = jnp.where(live_two, 1.0, 0.0)
            finish(1, pair, one * keep_one, two * keep_two)

        return carry

    lax.fori_loop(0, half, second, 0)


def edge_kernel(
    count_ref,
    grad_ref,
    aw_ref,
    slope_ref,
    off_ref,
    aw_hbm,
    slope_hbm,
    off_hbm,
    dmix_hbm,
    wa_ref,
    wb_ref,
    out_hbm,
    red_ref,
    pk_ref,
    pf_ref,
    aw_late,
    slope_late,
    off_late,
    dmix_ref,
    rows_ref,
    out_sems,
    late_sems,
):
    half = NW // 2
    per = 4
    groups = half // per

    dmix_copy = pltpu.make_async_copy(dmix_hbm, dmix_ref, out_sems.at[groups])

    def late_copies(pair):
        return [
            pltpu.make_async_copy(aw_hbm.at[pair], aw_late.at[pair], late_sems.at[0, pair]),
            pltpu.make_async_copy(
                slope_hbm.at[pair], slope_late.at[pair], late_sems.at[1, pair]
            ),
            pltpu.make_async_copy(off_hbm.at[pair], off_late.at[pair], late_sems.at[3, pair]),
        ]

    def late_out(pair):
        return pltpu.make_async_copy(
            rows_ref.at[1, pair], out_hbm.at[1, pair], late_sems.at[2, pair]
        )

    def each_live(step):
        def body(pair, carry):
            @pl.when(jnp.logical_or(count_ref[pair] > 1, count_ref[pair + half] > 1))
            def _():
                step(pair)

            return carry

        lax.fori_loop(0, half, body, 0)

    out_copies = [
        pltpu.make_async_copy(
            rows_ref.at[0, pl.ds(g * per, per)],
            out_hbm.at[0, pl.ds(g * per, per)],
            out_sems.at[g],
        )
        for g in range(groups)
    ]

    dmix_copy.start()

    def begin(pair):
        for copy in late_copies(pair):
            copy.start()

    each_live(begin)

    pk_ref[...] = jnp.zeros_like(pk_ref)
    pf_ref[...] = jnp.zeros_like(pf_ref)

    def work(first, count, slot):
        rows = count * BLK
        left = iota((rows, 2 * C), 1) < C
        one = grad_ref[0, pl.ds(first, count)].reshape(rows, 2 * C).astype(f32)
        two = grad_ref[1, pl.ds(first, count)].reshape(rows, 2 * C).astype(f32)
        if slot == 0:
            grads = jnp.where(left, one, pltpu.roll(two, C, 1))
        else:
            grads = jnp.where(left, pltpu.roll(one, C, 1), two)
        aw_in, slope_in, off_in = (
            (aw_ref, slope_ref, off_ref),
            (aw_late, slope_late, off_late),
        )[slot]
        actwgt = aw_in[pl.ds(first, count)].reshape(rows, 4 * C)
        kl = dot(actwgt, wa_ref[...])
        gated = (grads * kl[:, : 2 * C]).astype(bf16)
        dkval = (grads * kl[:, 2 * C :]).astype(bf16)
        gk = jnp.concatenate([gated, dkval], axis=1)
        back = dot(gk, wb_ref[...])
        rows_ref[slot, pl.ds(first, count)] = (
            back[:, : 2 * C].reshape(count, BLK, 2 * C).astype(bf16)
        )
        slope = slope_in[pl.ds(first, count)].reshape(rows, 2 * C)
        dbefore = back[:, 2 * C :] * slope
        pk_ref[...] += dot(actwgt, gk, ((0,), (0,)))
        high, low = split2(dbefore)
        edges = jnp.concatenate([off_in[first + j] for j in range(count)], axis=1)
        pf_ref[...] += dot(edges, high) + dot(edges, low)

    for g in range(groups):
        work(g * per, per, 0)
        out_copies[g].start()

    def second(pair):
        for copy in late_copies(pair):
            copy.wait()
        work(pair, 1, 1)
        late_out(pair).start()

    each_live(second)
    dmix_copy.wait()

    pk = pk_ref[...]
    pf = pf_ref[...]
    second_sum = pk[:C, 2 * C : 3 * C] + pk[C : 2 * C, 3 * C :]
    kernel_sum = pk[2 * C : 3 * C, :C] + pk[3 * C :, C : 2 * C]
    first_sum = pf[:8, :C] + pf[8:, C:]
    low_rows = jnp.concatenate([first_sum, jnp.zeros((C - 8, C), f32)], axis=0)
    red_ref[:C, :] = jnp.concatenate([kernel_sum, second_sum], axis=1)
    red_ref[C:, :] = jnp.concatenate([dmix_ref[...], low_rows], axis=1)
    for copy in out_copies:
        copy.wait()
    each_live(lambda pair: late_out(pair).wait())


def scatter_kernel(count_ref, rows_ref, idx_ref, wgt_ref, out_ref, acc_ref):
    step = pl.program_id(0)
    per = rows_ref.shape[1]
    half = NW // 2

    @pl.when(step == 0)
    def _():
        acc_ref[...] = jnp.zeros_like(acc_ref)

    low_row = iota((512, BLK), 0)
    row8 = iota((8, BLK), 0)
    ones = jnp.where(row8 == 0, 1.0, 0.0).astype(bf16)

    def add(targets, slot, values, count):
        hots = []
        tops = []
        for target in targets:
            idx = idx_ref[target, pl.ds(slot, 1), :]
            low = jnp.bitwise_and(idx, 511)
            hots.append(jnp.where(low_row == low, 1.0, 0.0).astype(bf16))
            top = jnp.right_shift(idx, 9).astype(f32)
            tops.append(jnp.where(row8 == 0, top, 0.0).astype(bf16))
        spread = dot(jnp.concatenate(tops, axis=1), ones, ((0,), (0,)))
        right = iota((count * BLK, 2 * C), 1) >= C
        quarter = jnp.where(right, 1.0, 0.0)
        first = jnp.where(spread == quarter, values, 0.0)
        second = jnp.where(spread == quarter + 2.0, values, 0.0)
        both = jnp.concatenate([first, second], axis=1).astype(bf16)
        acc_ref[...] += dot(jnp.concatenate(hots, axis=1), both)

    def doubled(values, side):
        left = iota(values.shape, 1) < C
        turned = pltpu.roll(values, C, 1)
        if side == 0:
            return jnp.where(left, values, turned)
        return jnp.where(left, turned, values)

    rows = rows_ref[0].reshape(per * BLK, 2 * C).astype(f32)
    for side in range(2):
        targets = [step * per + j + side * half for j in range(per)]
        add(targets, 0, doubled(rows, side), per)
    for j in range(per):
        for side in range(2):
            target = step * per + j + side * half

            @pl.when(count_ref[target] > 1)
            def _():
                add([target], 1, doubled(rows_ref[1, j].astype(f32), side), 1)

    @pl.when(step == pl.num_programs(0) - 1)
    def _():
        for pair in range(2):
            part = jnp.transpose(acc_ref[:, pair * 2 * C : (pair + 1) * 2 * C])
            for one in range(2):
                start = (2 * pair + one) * 512
                out_ref[:, start : start + 512] = (
                    part[one * C : (one + 1) * C] * wgt_ref[:, start : start + 512]
                )


def sum_kernel(in_ref, out_ref):
    total = in_ref[0]
    for j in range(1, in_ref.shape[0]):
        total = total + in_ref[j]
    out_ref[...] = jnp.broadcast_to(total[None], out_ref.shape)


def split_kernel(in_ref, kernel_ref, second_ref, mix_ref, first_ref, bias_ref):
    total = in_ref[...].reshape(2 * C, 2 * C)
    kernel_ref[...] = total[:C, :C]
    second_ref[...] = total[:C, C:]
    mix_ref[...] = total[C:, :C]
    first_ref[...] = total[C : C + 3, C:]
    bias_ref[...] = total[C + 5 : C + 6, C:]


def exchange(block, axis):
    return lax.all_to_all(block, axis, split_axis=0, concat_axis=0, tiled=True)


def exchange_near(block):
    groups = [[16 * k + j for j in range(16)] for k in range(16)]
    return grouped(block, groups)


def exchange_far(block):
    groups = [[16 * k + j for k in range(16)] for j in range(16)]
    return grouped(block, groups)


def grouped(block, groups):
    return lax.all_to_all(
        block,
        ("wide", "narrow"),
        split_axis=0,
        concat_axis=0,
        tiled=True,
        axis_index_groups=groups,
    )


def vspec():
    return pl.BlockSpec(memory_space=pltpu.VMEM)


def hspec():
    return pl.BlockSpec(memory_space=pltpu.HBM)


def far(array):
    return pltpu.with_memory_space_constraint(array, pltpu.HBM)


def sspec():
    return pl.BlockSpec(memory_space=pltpu.SMEM)


def whole(shape):
    return pl.BlockSpec(shape, lambda g: (0,) * len(shape))


def lead(shape):
    return pl.BlockSpec(shape, lambda g: (g,) + (0,) * (len(shape) - 1))


def split3(values):
    a = lax.reduce_precision(values, 8, 7)
    b = lax.reduce_precision(values - a, 8, 7)
    c = values - a - b
    return [part.astype(bf16) for part in (a, b, c)]


def local(
    point_feats,
    point_pos,
    point_weight,
    nbr_point,
    nbr_cell,
    block_count,
    latent,
    preact,
    cotangent,
    spectral_weight,
    kernel_mat,
    first_weight,
    first_bias,
    second_weight,
    mix_weight,
):
    depth_t, row_t, plane_t, plane_inv_t, row_inv_t, depth_inv_t = [
        jnp.asarray(stack_hi_lo(pair)) for pair in make_tables()
    ]
    me = lax.axis_index("narrow").astype(jnp.int32).reshape(1)
    counts = block_count.reshape(NW)
    idx = nbr_point.reshape(NW, CAP, BLK)
    cell = nbr_cell.reshape(NW, CAP, BLK)
    wgt = point_weight.reshape(1, PDEV)
    pos8 = jnp.concatenate([point_pos, jnp.zeros((5, PDEV), f32)], axis=0)

    zero = jnp.zeros((C, C), bf16)
    sec = second_weight
    ker = kernel_mat
    wa = jnp.block(
        [
            [sec, zero, zero, zero],
            [zero, sec, zero, zero],
            [zero, zero, ker, zero],
            [zero, zero, zero, ker],
        ]
    )
    kt = ker.T
    st = sec.T
    wb = jnp.block(
        [
            [kt, zero, zero, zero],
            [zero, kt, zero, zero],
            [zero, zero, st, zero],
            [zero, zero, zero, st],
        ]
    )
    z2 = jnp.zeros((2, C), f32)
    half = jnp.concatenate([first_weight, z2, first_bias[None], z2], axis=0)
    zh = jnp.zeros((8, C), f32)
    first_full = jnp.concatenate(
        [jnp.concatenate([half, zh], axis=1), jnp.concatenate([zh, half], axis=1)], axis=0
    )
    first48 = jnp.concatenate(split3(first_full), axis=0)

    send1, grad_parts = call(
        depth_kernel,
        (sds((NN, XPL, 64, 2 * C), bf16), sds((XPL, 2 * C, 512), bf16)),
        in_specs=[vspec()] * 4,
        out_specs=(vspec(),) * 2,
        name="depth_forward",
    )(latent, preact, cotangent, depth_t)
    send1, weights = lax.optimization_barrier(
        (send1, spectral_weight.reshape(MODES * C, 2 * C))
    )
    recv1 = exchange(send1, "narrow")
    weights = weights.astype(bf16)
    dmix_part, mixg = call(
        mix_kernel,
        (sds((C, C), f32), sds((XPL, 512, C), f32)),
        in_specs=[vspec()] * 3,
        out_specs=(vspec(),) * 2,
        vmem=8,
        name="pointwise_mix",
    )(latent, grad_parts, mix_weight)
    recv1, mixg, weights = lax.optimization_barrier((recv1, mixg, weights))

    send2 = call(
        row_kernel,
        sds((NW, 16, 2 * C), bf16),
        in_specs=[vspec(), hspec()],
        out_specs=vspec(),
        scratch_shapes=[pltpu.VMEM(row_t.shape, bf16), pltpu.SemaphoreType.DMA((2,))],
        vmem=4,
        name="row_forward",
    )(recv1, far(row_t))
    recv2 = exchange(send2, "wide")
    spec, send3 = call(
        mode_kernel,
        (sds((2 * MODES, 2 * C), f32), sds((NW, 16, 2 * C), bf16)),
        in_specs=[vspec()] * 2 + [hspec()] * 3,
        out_specs=(vspec(),) * 2,
        scratch_shapes=[
            pltpu.VMEM((2 * MODES, 2 * C), bf16),
            pltpu.VMEM(plane_t.shape, bf16),
            pltpu.VMEM(plane_inv_t.shape, bf16),
            pltpu.VMEM(cell.shape, jnp.int32),
            pltpu.SemaphoreType.DMA((4,)),
        ],
        vmem=12,
        name="mode_mix",
    )(recv2, weights, far(plane_t), far(plane_inv_t), far(cell))
    recv3 = exchange(send3, "wide")

    send4 = call(
        row_inv_kernel,
        sds((NN, 64, 2 * C), bf16),
        in_specs=[vspec()] * 2,
        out_specs=vspec(),
        vmem=8,
        name="row_inverse",
    )(recv3, row_inv_t)
    recv4 = exchange(send4, "narrow")

    found = call(
        gather_kernel,
        pltpu.HBM((NW, BLK, 2 * C), bf16),
        in_specs=[vspec()] * 4,
        out_specs=hspec(),
        scratch_shapes=[
            pltpu.VMEM((NW, BLK, 2 * C), bf16),
            pltpu.SemaphoreType.DMA((4,)),
        ],
        vmem=20,
        name="cell_gather",
    )(recv4, mixg, depth_inv_t, recv3)

    found, idx, spec = lax.optimization_barrier((found, idx, spec))
    grads = exchange(found, "wide")

    half = NW // 2
    aw, slope, off, aw_late, slope_late, off_late = call(
        prep_kernel,
        (
            sds((half, BLK, 4 * C), bf16),
            sds((half, BLK, 2 * C), f32),
            sds((half, 16, 2 * C), bf16),
            pltpu.HBM((half, BLK, 4 * C), bf16),
            pltpu.HBM((half, BLK, 2 * C), f32),
            pltpu.HBM((half, 16, 2 * C), bf16),
        ),
        in_specs=[sspec(), sspec()] + [vspec()] * 6,
        out_specs=(vspec(),) * 6,
        scratch_shapes=[pltpu.VMEM((2, PDEV, 2 * C), bf16)],
        flops=2 * 10**9,
        bytes_accessed=2 * 10**7,
        vmem=32,
        name="edge_prepare",
    )(counts, me, point_feats, pos8, wgt, idx, cell, first48)

    d_spectral = call(
        outer_kernel,
        sds((MODES, C, 2 * C), f32),
        grid=(8,),
        in_specs=[whole((2 * MODES, 2 * C))],
        out_specs=lead((MODES // 8, C, 2 * C)),
        scratch_shapes=[pltpu.VMEM((C, 2 * MODES), f32), pltpu.VMEM((2, 2 * MODES, 2 * C), bf16)],
        flops=2 * 10**9,
        vmem=16,
        name="spectral_grad",
    )(spec).reshape(spectral_weight.shape)

    aw, d_spectral = lax.optimization_barrier((aw, d_spectral))
    rows, red = call(
        edge_kernel,
        (pltpu.HBM((CAP, half, BLK, 2 * C), bf16), sds((2 * C, 2 * C), f32)),
        in_specs=[sspec()] + [vspec()] * 4 + [hspec()] * 4 + [vspec()] * 2,
        out_specs=(hspec(), vspec()),
        scratch_shapes=[
            pltpu.VMEM((4 * C, 4 * C), f32),
            pltpu.VMEM((16, 2 * C), f32),
            pltpu.VMEM((half, BLK, 4 * C), bf16),
            pltpu.VMEM((half, BLK, 2 * C), f32),
            pltpu.VMEM((half, 16, 2 * C), bf16),
            pltpu.VMEM((C, C), f32),
            pltpu.VMEM((CAP, half, BLK, 2 * C), bf16),
            pltpu.SemaphoreType.DMA((5,)),
            pltpu.SemaphoreType.DMA((4, half)),
        ],
        vmem=24,
        name="edge_grads",
    )(
        counts,
        grads.reshape(2, half, BLK, 2 * C),
        aw,
        slope,
        off,
        far(aw_late),
        far(slope_late),
        far(off_late),
        far(dmix_part),
        wa,
        wb,
    )

    part = exchange_near(red.reshape(16, 8, 2 * C))
    part = call(
        sum_kernel,
        sds((16, 8, 2 * C), f32),
        in_specs=[vspec()],
        out_specs=vspec(),
        vmem=4,
        name="sum_near",
    )(part)
    part = exchange_far(part)

    d_points = call(
        scatter_kernel,
        sds((C, PDEV), f32),
        grid=(4,),
        in_specs=[
            sspec(),
            pl.BlockSpec((CAP, half // 4, BLK, 2 * C), lambda g: (0, g, 0, 0)),
            whole((NW, CAP, BLK)),
            whole((1, PDEV)),
        ],
        out_specs=whole((C, PDEV)),
        scratch_shapes=[pltpu.VMEM((512, 4 * C), f32)],
        flops=2 * 10**9,
        vmem=32,
        name="point_grads",
    )(counts, far(rows), idx, wgt)

    part, d_points = lax.optimization_barrier((part, d_points))
    part = call(
        sum_kernel,
        sds((16, 8, 2 * C), f32),
        in_specs=[vspec()],
        out_specs=vspec(),
        vmem=4,
        name="sum_far",
    )(part)
    part = exchange_near(part)

    d_kernel, d_second, d_mix, d_first, d_bias = call(
        split_kernel,
        (sds((C, C), f32),) * 3 + (sds((3, C), f32), sds((1, C), f32)),
        in_specs=[vspec()],
        out_specs=(vspec(),) * 5,
        vmem=4,
        name="split_sums",
    )(part)
    return (d_points, d_kernel, d_first, d_bias.reshape(C), d_second, d_mix, d_spectral)


def solution(mesh):
    return jax.shard_map(
        local,
        mesh=mesh,
        in_specs=(
            P(None, ("wide", "narrow")),
            P(None, ("wide", "narrow")),
            P(("wide", "narrow")),
            P("wide", "narrow", None, None, None),
            P("wide", "narrow", None, None, None),
            P("wide", "narrow", None),
            P("wide", None, "narrow"),
            P("wide", None, "narrow"),
            P("wide", None, "narrow"),
            P("wide", None, "narrow", None, None),
            P(),
            P(),
            P(),
            P(),
            P(),
        ),
        out_specs=(
            P(None, ("wide", "narrow")),
            P(),
            P(),
            P(),
            P(),
            P(),
            P("wide", None, "narrow", None, None),
        ),
        check_vma=False,
    )
```

```python
import math

import numpy as np
import ml_dtypes
import jax
import jax.numpy as jnp
from jax import lax
from jax.experimental import pallas as pl
from jax.experimental.pallas import tpu as pltpu
from jax.sharding import PartitionSpec as P

C = 64
GZ = 64
MZ = 32
CAP = 2
BLK = 128
XPL = 2
YR = 8
NW = 32
NN = 8
PDEV = 2048
CELLS = XPL * YR * GZ
KZL = MZ // NN
MODES = 32 * KZL

bf16 = jnp.bfloat16
f32 = jnp.float32
root_half = 0.7071067811865476
inv_root_tau = 0.3989422804014327


def hi_lo(table):
    table = np.asarray(table, np.float64)
    high = table.astype(ml_dtypes.bfloat16)
    low = (table - high.astype(np.float64)).astype(ml_dtypes.bfloat16)
    return high, low


def phases(freqs, positions):
    angle = (2.0 * math.pi / 64) * np.mod(np.outer(freqs, positions), 64)
    return np.cos(angle), np.sin(angle)


def make_tables():
    depth_f = np.arange(MZ)
    signed = np.where(np.arange(32) < 16, np.arange(32), np.arange(32) - 32)
    spots = np.arange(64)
    dc, ds = phases(depth_f, spots)
    rc, rs = phases(signed, spots)
    eye_2 = np.eye(2)
    eye_4 = np.eye(4)
    eye_k = np.eye(KZL)
    eye_x = np.eye(XPL)
    dri = np.stack([dc, -ds], 1).reshape(NN, KZL, 2, GZ)
    depth = np.einsum("nkrz,yw->nykrwz", dri, eye_2).reshape(128, 128)
    rot = np.zeros((2, 2, 32, 64))
    rot[0, 0] = rc
    rot[0, 1] = rs
    rot[1, 0] = -rs
    rot[1, 1] = rc
    row = np.einsum("abfy,kl->fkaylb", rot, eye_k).reshape(32 * KZL * 2, 64 * KZL * 2)
    plane = np.einsum("abfx,kl->afkxlb", rot, eye_k).reshape(2 * MODES, 64 * KZL * 2)
    volume = 64.0 * 64.0 * 64.0
    rinv = np.zeros((2, 2, 32, 64))
    rinv[0, 0] = rc
    rinv[0, 1] = -rs
    rinv[1, 0] = rs
    rinv[1, 1] = rc
    plane_inv = np.einsum("abfx,kl->axkbfl", rinv, eye_k).reshape(2 * 256, 2 * MODES) / volume
    both = np.stack([rc, rs], 0).reshape(2, 32, NN, YR)
    row_inv = np.einsum("pfny,xw,kl->nxykpfwl", both, eye_x, eye_k).reshape(512, 512)
    dinv = np.stack([dc, -ds], 0).reshape(2, NN, KZL, GZ)
    depth_inv = np.einsum("rnkz,yw->yzrnwk", dinv, eye_4).reshape(256, 256)
    return [hi_lo(t) for t in (depth, row, plane, plane_inv, row_inv, depth_inv)]


def stack_hi_lo(pair):
    return np.stack(pair, 0)


def dot(a, b, contract=((1,), (0,))):
    return lax.dot_general(a, b, (contract, ((), ())), preferred_element_type=f32)


def split2(values):
    high = values.astype(bf16)
    return high, (values - high.astype(f32)).astype(bf16)


def iota(shape, axis):
    return lax.broadcasted_iota(jnp.int32, shape, axis)


def fiota(shape, axis):
    return iota(shape, axis).astype(f32)


def call(kernel, out_shape, *, vmem=56, flops=10**8, bytes_accessed=4 * 10**6, name=None, **kw):
    return pl.pallas_call(
        kernel,
        out_shape=out_shape,
        name=name,
        compiler_params=pltpu.CompilerParams(vmem_limit_bytes=vmem * 1024 * 1024),
        cost_estimate=pl.CostEstimate(
            flops=flops, bytes_accessed=bytes_accessed, transcendentals=0
        ),
        **kw,
    )


def sds(shape, dtype):
    return jax.ShapeDtypeStruct(shape, dtype)


def depth_kernel(lat_ref, pre_ref, cot_ref, tab_ref, send_ref, grad_ref):
    nt = ((1,), (1,))
    mains = []
    rests = []
    for x in range(XPL):
        pre = pre_ref[x].astype(f32)
        slope = 0.5 * (1.0 + lax.erf(pre * root_half)) + pre * jnp.exp(
            -0.5 * pre * pre
        ) * inv_root_tau
        high, low = split2(cot_ref[x].astype(f32) * slope)
        grad_ref[x] = jnp.concatenate([high, low], axis=0)
        mains += [lat_ref[x], high]
        rests += [jnp.zeros_like(low), low]
    main = jnp.concatenate(mains, axis=0)
    rest = jnp.concatenate(rests, axis=0)
    tables = tab_ref[...].reshape(256, 128)
    for pair in range(YR // 2):
        cols = slice(pair * 128, (pair + 1) * 128)
        out = dot(tables, main[:, cols], nt)
        out = out[:128] + out[128:] + dot(tab_ref[0], rest[:, cols], nt)
        for x in range(XPL):
            block = out[:, x * 2 * C : (x + 1) * 2 * C]
            send_ref[:, x, pair * 16 : (pair + 1) * 16, :] = block.reshape(
                NN, 16, 2 * C
            ).astype(bf16)


def mix_kernel(lat_ref, grad_ref, mix_ref, dmix_ref, mixg_ref):
    dmix = jnp.zeros((C, C), f32)
    mix = mix_ref[...]
    nt = ((1,), (1,))
    for x in range(XPL):
        u = lat_ref[x]
        high = grad_ref[x, :C]
        low = grad_ref[x, C:]
        dmix = dmix + dot(u, high, nt) + dot(u, low, nt)
        mixg_ref[x] = dot(high, mix, ((0,), (1,))) + dot(low, mix, ((0,), (1,)))
    dmix_ref[...] = dmix


def row_kernel(recv_ref, tab_hbm, send_ref, tab_ref, sems):
    copies = [
        pltpu.make_async_copy(tab_hbm.at[k], tab_ref.at[k], sems.at[k]) for k in range(2)
    ]
    for copy in copies:
        copy.start()
    blocks = [recv_ref[:, x].reshape(512, 2 * C) for x in range(XPL)]
    block = jnp.concatenate(blocks, axis=1)
    copies[0].wait()
    out = dot(tab_ref[0], block)
    copies[1].wait()
    out = out + dot(tab_ref[1], block)
    parts = [out[:, x * 2 * C : (x + 1) * 2 * C].reshape(32, 8, 2 * C) for x in range(XPL)]
    send_ref[...] = jnp.concatenate(parts, axis=1).astype(bf16)


def mode_kernel(
    recv_ref,
    w_ref,
    tab_hbm,
    inv_hbm,
    cell_hbm,
    spec_ref,
    send_ref,
    x_ref,
    tab_ref,
    inv_ref,
    cell_ref,
    sems,
):
    per = 16
    steps = MODES // per
    copies = [
        pltpu.make_async_copy(source, target, sems.at[k])
        for k, (source, target) in enumerate(
            (
                (tab_hbm.at[0], tab_ref.at[0]),
                (tab_hbm.at[1], tab_ref.at[1]),
                (inv_hbm, inv_ref),
                (cell_hbm, cell_ref),
            )
        )
    ]
    for copy in copies:
        copy.start()
    block = recv_ref[...].reshape(512, 2 * C)
    copies[0].wait()
    spec = dot(tab_ref[0], block)
    copies[1].wait()
    spec = spec + dot(tab_ref[1], block)
    spec_ref[...] = spec
    dr = spec[:MODES, C:]
    di = spec[MODES:, C:]
    x_ref[:MODES, :] = jnp.concatenate([dr, di], axis=1).astype(bf16)
    x_ref[MODES:, :] = jnp.concatenate([di, -dr], axis=1).astype(bf16)
    lane = jnp.bitwise_and(iota((C, 2 * MODES), 1), MODES - 1)
    nt = ((1,), (1,))
    acc = jnp.zeros((C, 2 * MODES), f32)
    for g in range(steps):
        weights = w_ref[g * per * C : (g + 1) * per * C, :]
        res = dot(weights, x_ref[...], nt)
        for j in range(per):
            acc = acc + jnp.where(lane == g * per + j, res[j * C : (j + 1) * C], 0.0)
    high, low = split2(acc)
    copies[2].wait()
    copies[3].wait()
    out = dot(inv_ref[0], high, nt) + dot(inv_ref[1], high, nt) + dot(inv_ref[0], low, nt)
    rows = jnp.concatenate([out[:256], out[256:]], axis=1).reshape(NW, 8, 2 * C)
    cells = cell_ref[...]
    part = iota((NW, 8, BLK), 1)
    cell = jnp.where(part < 2, cells[:, 0:1, :], cells[:, 1:2, :])
    high = jnp.right_shift(cell, 8)
    low = jnp.bitwise_and(cell, 255)
    tail = jnp.where(jnp.bitwise_and(part, 1) == 0, high, low).astype(f32)
    tail = jnp.where(part < 4, tail, 0.0)
    send_ref[...] = jnp.concatenate([rows, tail], axis=1).astype(bf16)


def outer_kernel(spec_ref, out_ref, l_ref, x_ref):
    step = pl.program_id(0)
    per = out_ref.shape[0]

    @pl.when(step == 0)
    def _():
        spec = spec_ref[...]
        l_ref[...] = jnp.transpose(spec)[:C] * (1.0 / 262144.0)
        dr = spec[:MODES, C:]
        di = spec[MODES:, C:]
        first = jnp.concatenate([dr, di], axis=1)
        second = jnp.concatenate([di, -dr], axis=1)
        high, low = split2(jnp.concatenate([first, second], axis=0))
        x_ref[0] = high
        x_ref[1] = low

    ut = l_ref[...]
    lane = jnp.bitwise_and(iota((C, 2 * MODES), 1), MODES - 1)
    rows = [jnp.where(lane == step * per + j, ut, 0.0) for j in range(per)]
    high, low = split2(jnp.concatenate(rows, axis=0))
    out = dot(high, x_ref[0]) + dot(high, x_ref[1]) + dot(low, x_ref[0])
    out_ref[...] = out.reshape(per, C, 2 * C)


def row_inv_kernel(recv_ref, tab_ref, send_ref):
    block = recv_ref[...].astype(f32)[:, :8, :].reshape(256, 2 * C)
    swapped = jnp.concatenate([-block[:, C:], block[:, :C]], axis=1)
    both = jnp.concatenate([block, swapped], axis=0).astype(bf16)
    out = dot(tab_ref[0], both) + dot(tab_ref[1], both)
    send_ref[...] = out.reshape(NN, 64, 2 * C).astype(bf16)


def gather_kernel(recv_ref, mixg_ref, dinv_ref, cell_ref, out_hbm, out_ref, sems):
    quarters = []
    for x in range(XPL):
        for half in range(2):
            start = x * 32 + half * 16
            block = recv_ref[:, start : start + 16, :].reshape(128, 2 * C)
            both = jnp.concatenate([block[:, :C], block[:, C:]], axis=0)
            grad = dot(dinv_ref[0], both) + dot(dinv_ref[1], both)
            quarters.append(grad + mixg_ref[x, half * 256 : (half + 1) * 256, :])
    table = jnp.concatenate(quarters, axis=1).astype(bf16)

    per = 4
    copies = [
        pltpu.make_async_copy(
            out_ref.at[pl.ds(g * per, per)], out_hbm.at[pl.ds(g * per, per)], sems.at[g]
        )
        for g in range(NW // per)
    ]
    rows = per * BLK
    row16 = iota((16, 4 * BLK), 0)
    part16 = jnp.right_shift(iota((16, 4 * BLK), 1), 7)
    sel = jnp.where(row16 == part16 + 8, 1.0, 0.0).astype(bf16)
    low_lane = fiota((rows, 256), 1)
    quarter = jnp.right_shift(iota((rows, 256), 1), 6).astype(f32)
    left = iota((rows, 2 * C), 1) < C
    for g in range(NW // per):
        cells = jnp.concatenate([cell_ref[g * per + j] for j in range(per)], axis=1)
        spread = dot(cells, sel, ((0,), (0,)))
        hots = []
        for s in range(CAP):
            low = spread[:, (2 * s + 1) * BLK : (2 * s + 2) * BLK]
            hots.append(
                jnp.where(jnp.concatenate([low, low], axis=1) == low_lane, 1.0, 0.0).astype(bf16)
            )
        got = dot(jnp.concatenate(hots, axis=0), table)
        found = []
        for s in range(CAP):
            high = spread[:, 2 * s * BLK : (2 * s + 1) * BLK]
            keep = jnp.concatenate([high, high], axis=1) == quarter
            one = jnp.where(keep, got[s * rows : (s + 1) * rows], 0.0)
            one = one[:, : 2 * C] + one[:, 2 * C :]
            found.append(one + pltpu.roll(one, C, 1))
        out = jnp.where(left, found[0], found[1]).astype(bf16)
        out_ref[g * per : (g + 1) * per] = out.reshape(per, BLK, 2 * C)
        copies[g].start()
    for copy in copies:
        copy.wait()


def prep_kernel(
    count_ref,
    me_ref,
    feat_ref,
    pos_ref,
    wgt_ref,
    idx_ref,
    cell_ref,
    first_ref,
    aw_ref,
    slope_ref,
    off_ref,
    aw_late_ref,
    slope_late_ref,
    off_late_ref,
    tab_ref,
):
    weighted = feat_ref[...].astype(f32) * wgt_ref[...]
    pos = pos_ref[...]
    p0 = pos.astype(bf16).astype(f32)
    p1 = (pos - p0).astype(bf16).astype(f32)
    p2 = pos - p0 - p1
    rest = jnp.concatenate([p0, p1, p2, jnp.zeros((40, PDEV), f32)], axis=0)
    tab_ref[0] = jnp.transpose(jnp.concatenate([weighted, rest], axis=0)).astype(bf16)
    tab_ref[1] = jnp.transpose(jnp.concatenate([rest, weighted], axis=0)).astype(bf16)

    point_lane = fiota((BLK, PDEV), 1)
    row8 = iota((8, BLK), 0)
    left = iota((BLK, 2 * C), 1) < C
    sel = jnp.where(row8 == 0, 64.0, jnp.where(row8 == 1, 1.0, 0.0)).astype(bf16)
    half = NW // 2

    def one_hot(idx_row):
        high = jnp.right_shift(idx_row, 6).astype(f32)
        low = jnp.bitwise_and(idx_row, 63).astype(f32)
        packed = jnp.where(row8 == 0, high, jnp.where(row8 == 1, low, 0.0)).astype(bf16)
        spread = dot(packed, sel, ((0,), (0,)))
        spread = jnp.concatenate([spread] * (PDEV // BLK), axis=1)
        return jnp.where(spread == point_lane, 1.0, 0.0).astype(bf16)

    def edge_rows(found_t, cell, target):
        spot = found_t[0:8] + found_t[8:16] + found_t[16:24]
        plane = jnp.right_shift(cell, 9)
        rowy = jnp.bitwise_and(jnp.right_shift(cell, 6), 7)
        depth = jnp.bitwise_and(cell, 63)
        first = ((target * XPL + plane).astype(f32) + 0.5) * (1.0 / 64)
        second = ((me_ref[0] * YR + rowy).astype(f32) + 0.5) * (1.0 / 64)
        third = (depth.astype(f32) + 0.5) * (1.0 / 64)
        centre = jnp.where(row8 == 0, first, jnp.where(row8 == 1, second, third))
        return jnp.where(row8 < 3, centre - spot, jnp.where(row8 == 5, 1.0, 0.0))

    def finish(slot, pair, one, two):
        weighted_pair = jnp.where(left, one, two)
        rows = [
            edge_rows(
                jnp.transpose(one)[C : C + 24], cell_ref[pair, pl.ds(slot, 1), :], pair
            ),
            edge_rows(
                jnp.transpose(two)[:24], cell_ref[pair + half, pl.ds(slot, 1), :], pair + half
            ),
        ]
        edge = jnp.concatenate(rows, axis=0).astype(bf16)
        aw_out = (aw_ref, aw_late_ref)[slot]
        slope_out = (slope_ref, slope_late_ref)[slot]
        off_out = (off_ref, off_late_ref)[slot]
        off_out[pair] = edge
        before = dot(jnp.concatenate([edge, edge, edge], axis=0), first_ref[...], ((0,), (0,)))
        phi = 0.5 * (1.0 + lax.erf(before * root_half))
        aw_out[pair] = jnp.concatenate([before * phi, weighted_pair], axis=1).astype(bf16)
        slope_out[pair] = phi + before * jnp.exp(-0.5 * before * before) * inv_root_tau

    group = 4

    def body(g, carry):
        base = g * group
        found = []
        for side in range(2):
            hot = jnp.concatenate(
                [
                    one_hot(idx_ref[base + j + side * half, pl.ds(0, 1), :])
                    for j in range(group)
                ],
                axis=0,
            )
            found.append(dot(hot, tab_ref[side]))
        for j in range(group):
            rows = slice(j * BLK, (j + 1) * BLK)
            finish(0, base + j, found[0][rows], found[1][rows])
        return carry

    lax.fori_loop(0, half // group, body, 0)

    def second(pair, carry):
        live_one = count_ref[pair] > 1
        live_two = count_ref[pair + half] > 1

        @pl.when(jnp.logical_or(live_one, live_two))
        def _():
            one = dot(one_hot(idx_ref[pair, pl.ds(1, 1), :]), tab_ref[0])
            two = dot(one_hot(idx_ref[pair + half, pl.ds(1, 1), :]), tab_ref[1])
            keep_one = jnp.where(live_one, 1.0, 0.0)
            keep_two = jnp.where(live_two, 1.0, 0.0)
            finish(1, pair, one * keep_one, two * keep_two)

        return carry

    lax.fori_loop(0, half, second, 0)


def edge_kernel(
    count_ref,
    grad_ref,
    aw_ref,
    slope_ref,
    off_ref,
    aw_hbm,
    slope_hbm,
    off_hbm,
    dmix_hbm,
    wa_ref,
    wb_ref,
    out_hbm,
    red_ref,
    pk_ref,
    pf_ref,
    aw_late,
    slope_late,
    off_late,
    dmix_ref,
    rows_ref,
    out_sems,
    late_sems,
):
    half = NW // 2
    per = 4
    groups = half // per

    dmix_copy = pltpu.make_async_copy(dmix_hbm, dmix_ref, out_sems.at[groups])

    def late_copies(pair):
        return [
            pltpu.make_async_copy(aw_hbm.at[pair], aw_late.at[pair], late_sems.at[0, pair]),
            pltpu.make_async_copy(
                slope_hbm.at[pair], slope_late.at[pair], late_sems.at[1, pair]
            ),
            pltpu.make_async_copy(off_hbm.at[pair], off_late.at[pair], late_sems.at[3, pair]),
        ]

    def late_out(pair):
        return pltpu.make_async_copy(
            rows_ref.at[1, pair], out_hbm.at[1, pair], late_sems.at[2, pair]
        )

    def each_live(step):
        def body(pair, carry):
            @pl.when(jnp.logical_or(count_ref[pair] > 1, count_ref[pair + half] > 1))
            def _():
                step(pair)

            return carry

        lax.fori_loop(0, half, body, 0)

    out_copies = [
        pltpu.make_async_copy(
            rows_ref.at[0, pl.ds(g * per, per)],
            out_hbm.at[0, pl.ds(g * per, per)],
            out_sems.at[g],
        )
        for g in range(groups)
    ]

    dmix_copy.start()

    def begin(pair):
        for copy in late_copies(pair):
            copy.start()

    each_live(begin)

    pk_ref[...] = jnp.zeros_like(pk_ref)
    pf_ref[...] = jnp.zeros_like(pf_ref)

    def work(first, count, slot):
        rows = count * BLK
        left = iota((rows, 2 * C), 1) < C
        one = grad_ref[0, pl.ds(first, count)].reshape(rows, 2 * C).astype(f32)
        two = grad_ref[1, pl.ds(first, count)].reshape(rows, 2 * C).astype(f32)
        if slot == 0:
            grads = jnp.where(left, one, pltpu.roll(two, C, 1))
        else:
            grads = jnp.where(left, pltpu.roll(one, C, 1), two)
        aw_in, slope_in, off_in = (
            (aw_ref, slope_ref, off_ref),
            (aw_late, slope_late, off_late),
        )[slot]
        actwgt = aw_in[pl.ds(first, count)].reshape(rows, 4 * C)
        kl = dot(actwgt, wa_ref[...])
        gated = (grads * kl[:, : 2 * C]).astype(bf16)
        dkval = (grads * kl[:, 2 * C :]).astype(bf16)
        gk = jnp.concatenate([gated, dkval], axis=1)
        back = dot(gk, wb_ref[...])
        rows_ref[slot, pl.ds(first, count)] = (
            back[:, : 2 * C].reshape(count, BLK, 2 * C).astype(bf16)
        )
        slope = slope_in[pl.ds(first, count)].reshape(rows, 2 * C)
        dbefore = back[:, 2 * C :] * slope
        pk_ref[...] += dot(actwgt, gk, ((0,), (0,)))
        high, low = split2(dbefore)
        edges = jnp.concatenate([off_in[first + j] for j in range(count)], axis=1)
        pf_ref[...] += dot(edges, high) + dot(edges, low)

    for g in range(groups):
        work(g * per, per, 0)
        out_copies[g].start()

    def second(pair):
        for copy in late_copies(pair):
            copy.wait()
        work(pair, 1, 1)
        late_out(pair).start()

    each_live(second)
    dmix_copy.wait()

    pk = pk_ref[...]
    pf = pf_ref[...]
    second_sum = pk[:C, 2 * C : 3 * C] + pk[C : 2 * C, 3 * C :]
    kernel_sum = pk[2 * C : 3 * C, :C] + pk[3 * C :, C : 2 * C]
    first_sum = pf[:8, :C] + pf[8:, C:]
    low_rows = jnp.concatenate([first_sum, jnp.zeros((C - 8, C), f32)], axis=0)
    red_ref[:C, :] = jnp.concatenate([kernel_sum, second_sum], axis=1)
    red_ref[C:, :] = jnp.concatenate([dmix_ref[...], low_rows], axis=1)
    for copy in out_copies:
        copy.wait()
    each_live(lambda pair: late_out(pair).wait())


def scatter_kernel(count_ref, rows_ref, idx_ref, wgt_ref, out_ref, acc_ref):
    step = pl.program_id(0)
    per = rows_ref.shape[1]
    half = NW // 2

    @pl.when(step == 0)
    def _():
        acc_ref[...] = jnp.zeros_like(acc_ref)

    low_row = iota((512, BLK), 0)
    row8 = iota((8, BLK), 0)
    ones = jnp.where(row8 == 0, 1.0, 0.0).astype(bf16)

    def add(targets, slot, values, count):
        hots = []
        tops = []
        for target in targets:
            idx = idx_ref[target, pl.ds(slot, 1), :]
            low = jnp.bitwise_and(idx, 511)
            hots.append(jnp.where(low_row == low, 1.0, 0.0).astype(bf16))
            top = jnp.right_shift(idx, 9).astype(f32)
            tops.append(jnp.where(row8 == 0, top, 0.0).astype(bf16))
        spread = dot(jnp.concatenate(tops, axis=1), ones, ((0,), (0,)))
        right = iota((count * BLK, 2 * C), 1) >= C
        quarter = jnp.where(right, 1.0, 0.0)
        first = jnp.where(spread == quarter, values, 0.0)
        second = jnp.where(spread == quarter + 2.0, values, 0.0)
        both = jnp.concatenate([first, second], axis=1).astype(bf16)
        acc_ref[...] += dot(jnp.concatenate(hots, axis=1), both)

    def doubled(values, side):
        left = iota(values.shape, 1) < C
        turned = pltpu.roll(values, C, 1)
        if side == 0:
            return jnp.where(left, values, turned)
        return jnp.where(left, turned, values)

    rows = rows_ref[0].reshape(per * BLK, 2 * C).astype(f32)
    for side in range(2):
        targets = [step * per + j + side * half for j in range(per)]
        add(targets, 0, doubled(rows, side), per)
    for j in range(per):
        for side in range(2):
            target = step * per + j + side * half

            @pl.when(count_ref[target] > 1)
            def _():
                add([target], 1, doubled(rows_ref[1, j].astype(f32), side), 1)

    @pl.when(step == pl.num_programs(0) - 1)
    def _():
        for pair in range(2):
            part = jnp.transpose(acc_ref[:, pair * 2 * C : (pair + 1) * 2 * C])
            for one in range(2):
                start = (2 * pair + one) * 512
                out_ref[:, start : start + 512] = (
                    part[one * C : (one + 1) * C] * wgt_ref[:, start : start + 512]
                )


def sum_kernel(in_ref, out_ref):
    total = in_ref[0]
    for j in range(1, in_ref.shape[0]):
        total = total + in_ref[j]
    out_ref[...] = jnp.broadcast_to(total[None], out_ref.shape)


def split_kernel(in_ref, kernel_ref, second_ref, mix_ref, first_ref, bias_ref):
    total = in_ref[...].reshape(2 * C, 2 * C)
    kernel_ref[...] = total[:C, :C]
    second_ref[...] = total[:C, C:]
    mix_ref[...] = total[C:, :C]
    first_ref[...] = total[C : C + 3, C:]
    bias_ref[...] = total[C + 5 : C + 6, C:]


def exchange(block, axis):
    return lax.all_to_all(block, axis, split_axis=0, concat_axis=0, tiled=True)


def exchange_near(block):
    groups = [[16 * k + j for j in range(16)] for k in range(16)]
    return grouped(block, groups)


def exchange_far(block):
    groups = [[16 * k + j for k in range(16)] for j in range(16)]
    return grouped(block, groups)


def grouped(block, groups):
    return lax.all_to_all(
        block,
        ("wide", "narrow"),
        split_axis=0,
        concat_axis=0,
        tiled=True,
        axis_index_groups=groups,
    )


def vspec():
    return pl.BlockSpec(memory_space=pltpu.VMEM)


def hspec():
    return pl.BlockSpec(memory_space=pltpu.HBM)


def far(array):
    return pltpu.with_memory_space_constraint(array, pltpu.HBM)


def sspec():
    return pl.BlockSpec(memory_space=pltpu.SMEM)


def whole(shape):
    return pl.BlockSpec(shape, lambda g: (0,) * len(shape))


def lead(shape):
    return pl.BlockSpec(shape, lambda g: (g,) + (0,) * (len(shape) - 1))


def split3(values):
    a = lax.reduce_precision(values, 8, 7)
    b = lax.reduce_precision(values - a, 8, 7)
    c = values - a - b
    return [part.astype(bf16) for part in (a, b, c)]


def local(
    point_feats,
    point_pos,
    point_weight,
    nbr_point,
    nbr_cell,
    block_count,
    latent,
    preact,
    cotangent,
    spectral_weight,
    kernel_mat,
    first_weight,
    first_bias,
    second_weight,
    mix_weight,
):
    depth_t, row_t, plane_t, plane_inv_t, row_inv_t, depth_inv_t = [
        jnp.asarray(stack_hi_lo(pair)) for pair in make_tables()
    ]
    me = lax.axis_index("narrow").astype(jnp.int32).reshape(1)
    counts = block_count.reshape(NW)
    idx = nbr_point.reshape(NW, CAP, BLK)
    cell = nbr_cell.reshape(NW, CAP, BLK)
    wgt = point_weight.reshape(1, PDEV)
    pos8 = jnp.concatenate([point_pos, jnp.zeros((5, PDEV), f32)], axis=0)

    zero = jnp.zeros((C, C), bf16)
    sec = second_weight
    ker = kernel_mat
    wa = jnp.block(
        [
            [sec, zero, zero, zero],
            [zero, sec, zero, zero],
            [zero, zero, ker, zero],
            [zero, zero, zero, ker],
        ]
    )
    kt = ker.T
    st = sec.T
    wb = jnp.block(
        [
            [kt, zero, zero, zero],
            [zero, kt, zero, zero],
            [zero, zero, st, zero],
            [zero, zero, zero, st],
        ]
    )
    z2 = jnp.zeros((2, C), f32)
    half = jnp.concatenate([first_weight, z2, first_bias[None], z2], axis=0)
    zh = jnp.zeros((8, C), f32)
    first_full = jnp.concatenate(
        [jnp.concatenate([half, zh], axis=1), jnp.concatenate([zh, half], axis=1)], axis=0
    )
    first48 = jnp.concatenate(split3(first_full), axis=0)

    send1, grad_parts = call(
        depth_kernel,
        (sds((NN, XPL, 64, 2 * C), bf16), sds((XPL, 2 * C, 512), bf16)),
        in_specs=[vspec()] * 4,
        out_specs=(vspec(),) * 2,
        name="depth_forward",
    )(latent, preact, cotangent, depth_t)
    send1, weights = lax.optimization_barrier(
        (send1, spectral_weight.reshape(MODES * C, 2 * C))
    )
    recv1 = exchange(send1, "narrow")
    weights = weights.astype(bf16)
    dmix_part, mixg = call(
        mix_kernel,
        (sds((C, C), f32), sds((XPL, 512, C), f32)),
        in_specs=[vspec()] * 3,
        out_specs=(vspec(),) * 2,
        vmem=8,
        name="pointwise_mix",
    )(latent, grad_parts, mix_weight)
    recv1, mixg, weights = lax.optimization_barrier((recv1, mixg, weights))

    send2 = call(
        row_kernel,
        sds((NW, 16, 2 * C), bf16),
        in_specs=[vspec(), hspec()],
        out_specs=vspec(),
        scratch_shapes=[pltpu.VMEM(row_t.shape, bf16), pltpu.SemaphoreType.DMA((2,))],
        vmem=4,
        name="row_forward",
    )(recv1, far(row_t))
    recv2 = exchange(send2, "wide")
    spec, send3 = call(
        mode_kernel,
        (sds((2 * MODES, 2 * C), f32), sds((NW, 16, 2 * C), bf16)),
        in_specs=[vspec()] * 2 + [hspec()] * 3,
        out_specs=(vspec(),) * 2,
        scratch_shapes=[
            pltpu.VMEM((2 * MODES, 2 * C), bf16),
            pltpu.VMEM(plane_t.shape, bf16),
            pltpu.VMEM(plane_inv_t.shape, bf16),
            pltpu.VMEM(cell.shape, jnp.int32),
            pltpu.SemaphoreType.DMA((4,)),
        ],
        vmem=12,
        name="mode_mix",
    )(recv2, weights, far(plane_t), far(plane_inv_t), far(cell))
    recv3 = exchange(send3, "wide")

    send4 = call(
        row_inv_kernel,
        sds((NN, 64, 2 * C), bf16),
        in_specs=[vspec()] * 2,
        out_specs=vspec(),
        vmem=8,
        name="row_inverse",
    )(recv3, row_inv_t)
    recv4 = exchange(send4, "narrow")

    found = call(
        gather_kernel,
        pltpu.HBM((NW, BLK, 2 * C), bf16),
        in_specs=[vspec()] * 4,
        out_specs=hspec(),
        scratch_shapes=[
            pltpu.VMEM((NW, BLK, 2 * C), bf16),
            pltpu.SemaphoreType.DMA((8,)),
        ],
        vmem=20,
        name="cell_gather",
    )(recv4, mixg, depth_inv_t, recv3)

    found, idx, spec = lax.optimization_barrier((found, idx, spec))
    grads = exchange(found, "wide")

    half = NW // 2
    aw, slope, off, aw_late, slope_late, off_late = call(
        prep_kernel,
        (
            sds((half, BLK, 4 * C), bf16),
            sds((half, BLK, 2 * C), f32),
            sds((half, 16, 2 * C), bf16),
            pltpu.HBM((half, BLK, 4 * C), bf16),
            pltpu.HBM((half, BLK, 2 * C), f32),
            pltpu.HBM((half, 16, 2 * C), bf16),
        ),
        in_specs=[sspec(), sspec()] + [vspec()] * 6,
        out_specs=(vspec(),) * 6,
        scratch_shapes=[pltpu.VMEM((2, PDEV, 2 * C), bf16)],
        flops=2 * 10**9,
        bytes_accessed=2 * 10**7,
        vmem=32,
        name="edge_prepare",
    )(counts, me, point_feats, pos8, wgt, idx, cell, first48)

    d_spectral = call(
        outer_kernel,
        sds((MODES, C, 2 * C), f32),
        grid=(8,),
        in_specs=[whole((2 * MODES, 2 * C))],
        out_specs=lead((MODES // 8, C, 2 * C)),
        scratch_shapes=[pltpu.VMEM((C, 2 * MODES), f32), pltpu.VMEM((2, 2 * MODES, 2 * C), bf16)],
        flops=2 * 10**9,
        vmem=16,
        name="spectral_grad",
    )(spec).reshape(spectral_weight.shape)

    aw, d_spectral = lax.optimization_barrier((aw, d_spectral))
    rows, red = call(
        edge_kernel,
        (pltpu.HBM((CAP, half, BLK, 2 * C), bf16), sds((2 * C, 2 * C), f32)),
        in_specs=[sspec()] + [vspec()] * 4 + [hspec()] * 4 + [vspec()] * 2,
        out_specs=(hspec(), vspec()),
        scratch_shapes=[
            pltpu.VMEM((4 * C, 4 * C), f32),
            pltpu.VMEM((16, 2 * C), f32),
            pltpu.VMEM((half, BLK, 4 * C), bf16),
            pltpu.VMEM((half, BLK, 2 * C), f32),
            pltpu.VMEM((half, 16, 2 * C), bf16),
            pltpu.VMEM((C, C), f32),
            pltpu.VMEM((CAP, half, BLK, 2 * C), bf16),
            pltpu.SemaphoreType.DMA((5,)),
            pltpu.SemaphoreType.DMA((4, half)),
        ],
        vmem=24,
        name="edge_grads",
    )(
        counts,
        grads.reshape(2, half, BLK, 2 * C),
        aw,
        slope,
        off,
        far(aw_late),
        far(slope_late),
        far(off_late),
        far(dmix_part),
        wa,
        wb,
    )

    part = exchange_near(red.reshape(16, 8, 2 * C))
    part = call(
        sum_kernel,
        sds((16, 8, 2 * C), f32),
        in_specs=[vspec()],
        out_specs=vspec(),
        vmem=4,
        name="sum_near",
    )(part)
    part = exchange_far(part)

    d_points = call(
        scatter_kernel,
        sds((C, PDEV), f32),
        grid=(4,),
        in_specs=[
            sspec(),
            pl.BlockSpec((CAP, half // 4, BLK, 2 * C), lambda g: (0, g, 0, 0)),
            whole((NW, CAP, BLK)),
            whole((1, PDEV)),
        ],
        out_specs=whole((C, PDEV)),
        scratch_shapes=[pltpu.VMEM((512, 4 * C), f32)],
        flops=2 * 10**9,
        vmem=32,
        name="point_grads",
    )(counts, far(rows), idx, wgt)

    part, d_points = lax.optimization_barrier((part, d_points))
    part = call(
        sum_kernel,
        sds((16, 8, 2 * C), f32),
        in_specs=[vspec()],
        out_specs=vspec(),
        vmem=4,
        name="sum_far",
    )(part)
    part = exchange_near(part)

    d_kernel, d_second, d_mix, d_first, d_bias = call(
        split_kernel,
        (sds((C, C), f32),) * 3 + (sds((3, C), f32), sds((1, C), f32)),
        in_specs=[vspec()],
        out_specs=(vspec(),) * 5,
        vmem=4,
        name="split_sums",
    )(part)
    return (d_points, d_kernel, d_first, d_bias.reshape(C), d_second, d_mix, d_spectral)


def solution(mesh):
    return jax.shard_map(
        local,
        mesh=mesh,
        in_specs=(
            P(None, ("wide", "narrow")),
            P(None, ("wide", "narrow")),
            P(("wide", "narrow")),
            P("wide", "narrow", None, None, None),
            P("wide", "narrow", None, None, None),
            P("wide", "narrow", None),
            P("wide", None, "narrow"),
            P("wide", None, "narrow"),
            P("wide", None, "narrow"),
            P("wide", None, "narrow", None, None),
            P(),
            P(),
            P(),
            P(),
            P(),
        ),
        out_specs=(
            P(None, ("wide", "narrow")),
            P(),
            P(),
            P(),
            P(),
            P(),
            P("wide", None, "narrow", None, None),
        ),
        check_vma=False,
    )
```
